32 devices in a mesh: group: 4 (over y, core), shard: 8 (over z, x).
Axes of the slice: x: 2, y: 2, z: 4, core: 2. Of those that a mesh axis runs over, the one named last changes fastest.
Arguments:
- edge_state: bfloat16 [32768, 128], P(('group', 'shard')), may hold values from -6 to 6
- atom_state: bfloat16 [2048, 256], P(('group', 'shard')), may hold values from -6 to 6
- radial_basis: bfloat16 [32768, 16], P(('group', 'shard')), may hold values from -6 to 6
- triplet_basis: bfloat16 [131072, 16], P(('group', 'shard')), may hold values from -6 to 6
- quad_basis: bfloat16 [131072, 16], P(('group', 'shard')), may hold values from -6 to 6
- dst_owner: int32 [32768, 1], P(('group', 'shard')), may hold values from 0 to 7; in each aligned block of 1024 rows (0 to 1023, 1024 to 2047, ...) at most 256 rows name the same one
- dst_local: int32 [32768], P(('group', 'shard')), may hold values from 0 to 63
- src_owner: int32 [32768, 1], P(('group', 'shard')), may hold values from 0 to 7; in each aligned block of 1024 rows (0 to 1023, 1024 to 2047, ...) at most 256 rows name the same one
- src_local: int32 [32768], P(('group', 'shard')), may hold values from 0 to 63
- triplet_in: int32 [131072], P(('group', 'shard')), may hold values from 0 to 1023
- triplet_out: int32 [131072], P(('group', 'shard')), may hold values from 0 to 1023
- quad_in: int32 [131072], P(('group', 'shard')), may hold values from 0 to 1023
- quad_out: int32 [131072], P(('group', 'shard')), may hold values from 0 to 1023
- fixed_atoms: int32 [2048], P(('group', 'shard')), may hold values 0 or 1
- edge_cotangent: bfloat16 [32768, 128], P(('group', 'shard')), may hold values from -6 to 6
- atom_cotangent: bfloat16 [2048, 256], P(('group', 'shard')), may hold values from -6 to 6
- weights: float32 [3000, 128], P(None, 'shard')
- first_moment: float32 [3000, 128], P(None, 'shard'), as said below
- second_moment: float32 [3000, 128], P(None, 'shard'), as said below
Outputs:
- edge_out: bfloat16 [32768, 128], P(('group', 'shard'))
- atom_out: bfloat16 [2048, 256], P(('group', 'shard'))
- edge_grad: float32 [32768, 128], P(('group', 'shard'))
- atom_grad: float32 [2048, 256], P(('group', 'shard'))
- weight_grad: float32 [3000, 128], P(None, 'shard')
- new_weights: float32 [3000, 128], P(None, 'shard')
- new_first: float32 [3000, 128], P(None, 'shard')
- new_second: float32 [3000, 128], P(None, 'shard')
- weights_low: bfloat16 [3000, 128], P(None, 'shard')
The draws below stay inside these ranges and needn't reach their ends.
Inputs may be any that keep to these rules, and one draw needn't show every extreme that they name: `dst_owner`: in the rows of one device no owner is named by more than 256 edges; in the rows of some devices one owner is named by exactly 256. `src_owner`: in the rows of one device no owner is named by more than 256 edges; in the rows of some devices one owner is named by exactly 256. `first_moment`: state of earlier steps, of both signs. `second_moment`: state of earlier steps, positive.
All inputs are finite; a program needn't handle non-finite values. No bound on the sum of `fixed_atoms` on one device may be relied on, other than what follows from the above.
Results may differ from the reference program's by a relative error of at most 0.035.
Values may be sent and summed in bfloat16 or wider, within the bound.
No kernel may reach another device: no remote copies, remote signals or barrier semaphores. Data moves between devices by JAX's collectives and lax.ppermute only.
A program may use at most 128 MiB of HBM per device.

```python
import math
import jax
import jax.numpy as jnp
import numpy as np
from jax import lax

D_EDGE = 128
D_ATOM = 256
D_TRI = 64
D_QUAD = 32
D_BASIS = 16
BLOCKS = 2
E_DEV = 1024
A_DEV = 64
T_DEV = 4096
Q_DEV = 4096
CAP = 256
EDGES = 32768
ATOMS = 2048
TRIPLETS = 131072
QUADS = 131072
PROWS = 3000
N_SHARD = 8


def region_rows():
    shapes = [(D_EDGE, D_TRI, 0), (D_BASIS, D_TRI, 1), (D_TRI, D_EDGE, 0), (D_EDGE, D_QUAD, 0), (D_BASIS, D_QUAD, 2), (D_QUAD, D_EDGE, 0), (D_BASIS, D_EDGE, 0), (D_EDGE, D_ATOM, 3), (D_ATOM, D_ATOM, 3), (D_ATOM, D_EDGE, 0), (D_ATOM, D_EDGE, 0)]
    typical = [0.7 * EDGES ** 0.5, 0.3 * TRIPLETS ** 0.5, 0.3 * QUADS ** 0.5, ATOMS ** 0.5]
    fan_list = []
    grad_list = []
    for layer_index in range(BLOCKS):
        for fan_in, width_out, family in shapes:
            rows_here = fan_in * width_out // 128
            fan_list = fan_list + [float(fan_in)] * rows_here
            grad_list = grad_list + [typical[family]] * rows_here
    return (np.array(fan_list, np.float32), np.array(grad_list, np.float32))


def draw_weights(key, part):
    fan_rows, grad_rows = region_rows()
    spread = jnp.asarray(fan_rows ** (-0.5))[:, None]
    values = jnp.clip(jax.random.normal(key, (PROWS, 128), jnp.float32), -6.0, 6.0)
    return (values * spread).astype(jnp.float32)


def draw_first_moment(key, part):
    fan_rows, grad_rows = region_rows()
    typical = jnp.asarray(grad_rows)[:, None]
    key_size, key_sign = jax.random.split(jax.random.fold_in(key, 11))
    magnitude = jax.random.uniform(key_size, (PROWS, 128), jnp.float32, 0.5, 1.5)
    choose = jax.random.uniform(key_sign, (PROWS, 128), jnp.float32)
    signs = jnp.where(choose < 0.5, -1.0, 1.0)
    return (typical * magnitude * signs).astype(jnp.float32)


def draw_second_moment(key, part):
    fan_rows, grad_rows = region_rows()
    typical = jnp.asarray(grad_rows)[:, None]
    factor = jax.random.uniform(jax.random.fold_in(key, 23), (PROWS, 128), jnp.float32, 1.0, 4.0)
    return (typical * typical * factor).astype(jnp.float32)


def touch_ends(result, key, smallest, largest):
    longest = result.shape.index(max(result.shape))
    spots = []
    for shift in (0, 1):
        where = [jax.random.randint(jax.random.fold_in(key, axis), (), 0, length) for axis, length in enumerate(result.shape)]
        where[longest] = (where[longest] + shift) % result.shape[longest]
        spots.append(tuple(where))
    return result.at[spots[0]].set(smallest).at[spots[1]].set(largest)


def block_levels(own_key, extent, pieces, smallest, top_value):
    def one(position, blocks):
        draws = jax.random.uniform(jax.random.fold_in(jax.random.fold_in(own_key, 6), position), (blocks,), jnp.float32, smallest / len(pieces), top_value / len(pieces))
        return jnp.repeat(jnp.exp(draws), extent[position] // blocks).reshape((-1,) + (1,) * (len(extent) - position - 1))

    loudness = one(*pieces[0])
    for cut in pieces[1:]:
        loudness = loudness * one(*cut)
    return loudness


def deal_out(key, own, number, rows, amount, top, most, lean):
    sequence = jax.random.permutation(key, amount)
    crowded, usual = portions_of(amount, rows * top, most, lean, True), portions_of(amount, rows * top, most, lean, False)
    places = jnp.arange(amount)

    def named(sizes, offset_by):
        used = int((sizes > 0).sum())
        fixed = max(1, used // 4)
        passed = fixed + (places - fixed + offset_by * (used - fixed)) % max(1, amount - fixed)
        return jnp.zeros((amount,), jnp.int32).at[sequence[jnp.where(places < fixed, places, passed)]].set(jnp.asarray(sizes, jnp.int32))

    sizes = jnp.where(number % 4 == 0, named(crowded, number // 4), named(usual, number - number // 4 - 1))
    mixed = jax.random.permutation(jax.random.fold_in(own, 3), amount)
    donor, sink = mixed[0:amount // 2 * 2:2], mixed[1:amount // 2 * 2:2]
    margin = jnp.minimum(sizes[donor] - 1, most - sizes[sink]) // 2
    margin = jnp.where((donor == sequence[0]) | (sink == sequence[0]) | (sizes[sink] == 0), 0, jnp.maximum(margin, 0))
    passed = jax.random.randint(jax.random.fold_in(own, 4), (amount // 2,), 0, 1 << 20) % (margin + 1)
    sizes = sizes.at[donor].add(-passed).at[sink].add(passed)
    members = jnp.searchsorted(jnp.cumsum(sizes), jnp.arange(rows * top), side="right").astype(jnp.int32)
    listing = members.reshape(top, rows).T
    listing = listing[jax.random.permutation(jax.random.fold_in(own, 1), rows)]
    offset_by = jax.random.randint(jax.random.fold_in(own, 2), (rows, 1), 0, top)
    return jnp.take_along_axis(listing, (jnp.arange(top)[None, :] + offset_by) % top, axis=1)


def portions_of(amount, total, most, slope, full):
    loads = [(1 << 20) // math.isqrt(standing ** slope) + 1 for standing in range(1, amount + 1)]
    largest = most if full else min(most, max(-(-total // amount), total * loads[0] // sum(loads)))
    least = 1 if total - largest >= amount - 1 else 0
    counts, spare = [largest] + [least] * (amount - 1), total - largest - least * (amount - 1)
    while spare > 0:
        free = [i for i in range(1, amount) if counts[i] < largest] or [i for i in range(1, amount) if counts[i] < most]
        whole, budget = sum([loads[i] for i in free]), spare
        for i in free:
            extra = min(most - counts[i], max(1, budget * loads[i] // whole), spare)
            counts[i] = counts[i] + extra
            spare = spare - extra
    return np.array(counts)


def centred(stream_key, dims, scale, bound, pieces=(), held_as=jnp.bfloat16):
    gain = block_levels(stream_key, dims, pieces, -0.22, 0.18) if pieces else 1.0
    entries = jax.random.normal(stream_key, dims, jnp.float32) * scale * gain
    return jnp.minimum(jnp.maximum(entries, -bound), bound).astype(held_as)


def setup_inputs(seed: int = 0) -> dict:
    seeds = jax.random.split(jax.random.key(seed), 20)
    edge_state = centred(seeds[0], (EDGES, D_EDGE), 1.0, 6.0, ((0, 32),))
    atom_state = centred(seeds[1], (ATOMS, D_ATOM), 1.0, 6.0, ((0, 32),))
    radial_basis = centred(seeds[2], (EDGES, D_BASIS), 1.0, 6.0, ((0, 32),))
    triplet_basis = centred(seeds[3], (TRIPLETS, D_BASIS), 1.0, 6.0, ((0, 32),))
    quad_basis = centred(seeds[4], (QUADS, D_BASIS), 1.0, 6.0, ((0, 32),))
    dst_owner_keys = jax.random.split(jax.random.fold_in(seeds[5], 1), EDGES // E_DEV)
    dst_owner_turns = jax.random.permutation(jax.random.fold_in(seeds[5], 3), EDGES // E_DEV)
    dst_owner = jax.vmap(lambda own, number: deal_out(jax.random.fold_in(seeds[5], 2), own, number, E_DEV, N_SHARD, 1, CAP, 2))(dst_owner_keys, dst_owner_turns).reshape((EDGES, 1))
    dst_local = touch_ends(jax.random.randint(seeds[6], (EDGES,), 0, A_DEV), jax.random.fold_in(seeds[6], 1), 0, A_DEV - 1).astype(jnp.int32)
    src_owner_keys = jax.random.split(jax.random.fold_in(seeds[7], 1), EDGES // E_DEV)
    src_owner_turns = jax.random.permutation(jax.random.fold_in(seeds[7], 3), EDGES // E_DEV)
    src_owner = jax.vmap(lambda own, number: deal_out(jax.random.fold_in(seeds[7], 2), own, number, E_DEV, N_SHARD, 1, CAP, 1))(src_owner_keys, src_owner_turns).reshape((EDGES, 1))
    src_local = touch_ends(jax.random.randint(seeds[8], (EDGES,), 0, A_DEV), jax.random.fold_in(seeds[8], 1), 0, A_DEV - 1).astype(jnp.int32)
    triplet_in = touch_ends(jax.random.randint(seeds[9], (TRIPLETS,), 0, E_DEV), jax.random.fold_in(seeds[9], 1), 0, E_DEV - 1).astype(jnp.int32)
    triplet_out = touch_ends(jax.random.randint(seeds[10], (TRIPLETS,), 0, E_DEV), jax.random.fold_in(seeds[10], 1), 0, E_DEV - 1).astype(jnp.int32)
    quad_in = touch_ends(jax.random.randint(seeds[11], (QUADS,), 0, E_DEV), jax.random.fold_in(seeds[11], 1), 0, E_DEV - 1).astype(jnp.int32)
    quad_out = touch_ends(jax.random.randint(seeds[12], (QUADS,), 0, E_DEV), jax.random.fold_in(seeds[12], 1), 0, E_DEV - 1).astype(jnp.int32)
    fixed_atoms = touch_ends((jax.random.randint(seeds[13], (ATOMS,), 0, 5) < 1).astype(jnp.int32), jax.random.fold_in(seeds[13], 1), 0, 1)
    edge_cotangent = centred(seeds[14], (EDGES, D_EDGE), 1.0, 6.0, ((0, 32),))
    atom_cotangent = centred(seeds[15], (ATOMS, D_ATOM), 1.0, 6.0, ((0, 32),))
    weights = draw_weights(jax.random.fold_in(seeds[19], 71), 0)
    first_moment = draw_first_moment(jax.random.fold_in(seeds[19], 71), 0)
    second_moment = draw_second_moment(jax.random.fold_in(seeds[19], 71), 0)
    return dict(edge_state=edge_state, atom_state=atom_state, radial_basis=radial_basis, triplet_basis=triplet_basis, quad_basis=quad_basis, dst_owner=dst_owner, dst_local=dst_local, src_owner=src_owner, src_local=src_local, triplet_in=triplet_in, triplet_out=triplet_out, quad_in=quad_in, quad_out=quad_out, fixed_atoms=fixed_atoms, edge_cotangent=edge_cotangent, atom_cotangent=atom_cotangent, weights=weights, first_moment=first_moment, second_moment=second_moment)


edge_scale = 0.25
pair_scale = 0.5
beta_one = 0.5
beta_two = 0.5
learn_rate = 0.1
decay_rate = 0.01
epsilon = 1e-08
adam_step = 4

@jax.custom_vjp
def low(v):
    return lax.optimization_barrier(v.astype(jnp.bfloat16)).astype(jnp.float32)

@jax.custom_vjp
def low_back(v):
    return v

def low_keep(v):
    return (low(v), None)

def low_pass(kept, grad):
    return (grad,)

def back_keep(v):
    return (v, None)

def back_low(kept, grad):
    return (low(grad),)
low.defvjp(low_keep, low_pass)
low_back.defvjp(back_keep, back_low)

def dense(left_side, right_side):
    return jnp.dot(left_side, right_side, precision=lax.Precision.HIGHEST, preferred_element_type=jnp.float32)

def matrix_shapes():
    return [(D_EDGE, D_TRI), (D_BASIS, D_TRI), (D_TRI, D_EDGE), (D_EDGE, D_QUAD), (D_BASIS, D_QUAD), (D_QUAD, D_EDGE), (D_BASIS, D_EDGE), (D_EDGE, D_ATOM), (D_ATOM, D_ATOM), (D_ATOM, D_EDGE), (D_ATOM, D_EDGE)]

def unpack(flat):
    result_list = []
    offset = 0
    for layer_index in range(BLOCKS):
        matrices = []
        for fan_in, width_out in matrix_shapes():
            row_total = fan_in * width_out // 128
            matrices.append(flat[offset:offset + row_total].reshape(fan_in, width_out))
            offset = offset + row_total
        result_list.append(matrices)
    return result_list

def pair_block(edge_low, basis_rows, source_edges, target_edges, down_weight, basis_weight, up_weight, edge_total):
    activated = jax.nn.silu(low_back(dense(edge_low, low(down_weight))))
    basis_out = low_back(dense(basis_rows, low(basis_weight)))
    products = jnp.take(activated, source_edges, axis=0) * basis_out
    aggregate = jax.ops.segment_sum(products, target_edges, num_segments=edge_total) * pair_scale
    return jax.nn.silu(low_back(dense(low(aggregate), low(up_weight))))

def adam_update(grad_flat, weights, first_moment, second_moment):
    new_first = beta_one * first_moment + (1.0 - beta_one) * grad_flat
    new_second = beta_two * second_moment + (1.0 - beta_two) * grad_flat * grad_flat
    first_hat = new_first / (1.0 - beta_one ** adam_step)
    second_hat = new_second / (1.0 - beta_two ** adam_step)
    new_weights = weights - learn_rate * (first_hat / (jnp.sqrt(second_hat) + epsilon) + decay_rate * weights)
    return (new_first, new_second, new_weights)

def reference(edge_state, atom_state, radial_basis, triplet_basis, quad_basis, dst_owner, dst_local, src_owner, src_local, triplet_in, triplet_out, quad_in, quad_out, fixed_atoms, edge_cotangent, atom_cotangent, weights, first_moment, second_moment):
    edges_all = edge_state.shape[0]
    atoms_all = atom_state.shape[0]
    device_total = edges_all // E_DEV
    group_atoms = A_DEV * N_SHARD
    group_total = atoms_all // group_atoms
    edge_rows = jnp.arange(edges_all, dtype=jnp.int32)
    group_base = edge_rows // (E_DEV * N_SHARD) * group_atoms
    dst_inside = (dst_owner[:, 0] * A_DEV + dst_local).astype(jnp.int32)
    src_inside = (src_owner[:, 0] * A_DEV + src_local).astype(jnp.int32)
    dst_global = (group_base + dst_inside).astype(jnp.int32)
    device_group = (jnp.arange(device_total, dtype=jnp.int32) // N_SHARD).astype(jnp.int32)
    dst_by_device = dst_inside.reshape(device_total, E_DEV)
    src_by_device = src_inside.reshape(device_total, E_DEV)
    trip_rows = jnp.arange(triplet_in.shape[0], dtype=jnp.int32)
    trip_base = trip_rows // T_DEV * E_DEV
    trip_source = (triplet_in + trip_base).astype(jnp.int32)
    trip_target = (triplet_out + trip_base).astype(jnp.int32)
    quad_rows = jnp.arange(quad_in.shape[0], dtype=jnp.int32)
    quad_base = quad_rows // Q_DEV * E_DEV
    quad_source = (quad_in + quad_base).astype(jnp.int32)
    quad_target = (quad_out + quad_base).astype(jnp.int32)
    free_rows = (1 - fixed_atoms).astype(jnp.float32)[:, None]
    radial_float = radial_basis.astype(jnp.float32)
    trip_float = triplet_basis.astype(jnp.float32)
    quad_float = quad_basis.astype(jnp.float32)

    def edge_rows_of(atom_sent):
        tables = atom_sent.reshape(group_total, group_atoms, atom_sent.shape[1])

        def one_device(carry, items):
            group_id, src_index, dst_index = items
            table = low_back(lax.dynamic_index_in_dim(tables, group_id, 0, keepdims=False))
            return (carry, (jnp.take(table, src_index, axis=0), jnp.take(table, dst_index, axis=0)))
        unused, picked = lax.scan(one_device, jnp.zeros((), jnp.int32), (device_group, src_by_device, dst_by_device))
        return (picked[0].reshape(edges_all, -1), picked[1].reshape(edges_all, -1))

    def forward(edge_start, atom_start, flat):
        block_weights = unpack(flat)
        state_edge = edge_start
        state_atom = atom_start
        for layer_index in range(BLOCKS):
            down_trip, basis_trip, up_trip, down_quad, basis_quad, up_quad, radial_proj, atom_first, atom_second, src_proj, dst_proj = block_weights[layer_index]
            edge_low = low(state_edge)
            trip_value = pair_block(edge_low, trip_float, trip_source, trip_target, down_trip, basis_trip, up_trip, edges_all)
            quad_value = pair_block(edge_low, quad_float, quad_source, quad_target, down_quad, basis_quad, up_quad, edges_all)
            middle = state_edge + trip_value + quad_value
            radial = low_back(dense(radial_float, low(radial_proj)))
            message = low(middle * radial)
            atom_input = jax.ops.segment_sum(message, dst_global, num_segments=atoms_all) * edge_scale
            atom_low = low(low_back(atom_input))
            pre_atom = low_back(dense(atom_low, low(atom_first)))
            hidden = low(jax.nn.silu(pre_atom))
            update = low_back(dense(hidden, low(atom_second)))
            new_atom = state_atom + free_rows * update
            atom_sent = low(new_atom)
            src_rows, dst_rows = edge_rows_of(atom_sent)
            pre_edge = low_back(dense(src_rows, low(src_proj)) + dense(dst_rows, low(dst_proj)))
            state_edge = middle + jax.nn.silu(pre_edge)
            state_atom = new_atom
        return (state_edge, state_atom)
    outputs, pullback = jax.vjp(forward, edge_state.astype(jnp.float32), atom_state.astype(jnp.float32), weights)
    edge_grad, atom_grad, weight_grad = pullback((edge_cotangent.astype(jnp.float32), atom_cotangent.astype(jnp.float32)))
    new_first, new_second, new_weights = adam_update(weight_grad, weights, first_moment, second_moment)
    return (outputs[0].astype(jnp.bfloat16), outputs[1].astype(jnp.bfloat16), edge_grad, atom_grad, weight_grad, new_weights, new_first, new_second, new_weights.astype(jnp.bfloat16))
```

```python
import functools

import jax
import jax.numpy as jnp
from jax import lax
from jax.experimental import pallas as pl
from jax.experimental.pallas import tpu as pltpu
from jax.sharding import PartitionSpec as P

D_EDGE = 128
D_ATOM = 256
D_TRI = 64
D_QUAD = 32
D_BASIS = 16
BLOCKS = 2
FOLD = 256
CHUNK = 1024
SMALL = 220
BIG = 1280
PAD = 256

edge_scale = 0.25
pair_scale = 0.5
beta_one = 0.5
beta_two = 0.5
learn_rate = 0.1
decay_rate = 0.01
epsilon = 1e-08
adam_step = 4

OFF_DOWN = {D_TRI: 0, D_QUAD: 136}
OFF_BASIS = {D_TRI: 64, D_QUAD: 168}
OFF_UP = {D_TRI: 72, D_QUAD: 172}
OFF_RADIAL = 204

F32 = jnp.float32
BF16 = jnp.bfloat16


def sds(shape, dtype):
    return jax.ShapeDtypeStruct(shape, dtype)


def call(body, outs, args, flops=10**9, smem=0):
    space = [pltpu.SMEM] * smem + [pltpu.VMEM] * (len(args) - smem)
    return pl.pallas_call(
        body,
        out_shape=outs,
        in_specs=[pl.BlockSpec(memory_space=s) for s in space],
        out_specs=[pl.BlockSpec(memory_space=pltpu.VMEM)] * len(outs),
        compiler_params=pltpu.CompilerParams(vmem_limit_bytes=40 * 2**20),
        cost_estimate=pl.CostEstimate(flops=flops, bytes_accessed=4 * 2**20, transcendentals=0),
        name=body.func.__name__ if isinstance(body, functools.partial) else body.__name__,
    )(*args)


def dot(a, b):
    return jnp.dot(a, b, preferred_element_type=F32)


def dot_nt(a, b):
    return lax.dot_general(a, b, (((1,), (1,)), ((), ())), preferred_element_type=F32)


def low(v):
    return v.astype(BF16)


def iota(shape, axis):
    return lax.broadcasted_iota(jnp.int32, shape, axis)


def ones_where(mask):
    return jnp.where(mask, 1.0, 0.0).astype(BF16)


def onehot(count, row, first=0):
    return ones_where(iota((count, row.shape[1]), 0) + first == row)


def sigmoid(v):
    return 1.0 / (1.0 + jnp.exp(-v))


def silu_pair(v):
    s = sigmoid(v)
    return v * s, s * (1.0 + v * (1.0 - s))


def cut(value, width):
    count = FOLD // width
    length = value.shape[1] // count
    return jnp.concatenate([value[:, g * length : (g + 1) * length] for g in range(count)], axis=0)


def uncut(value, width):
    count = FOLD // width
    return jnp.concatenate([value[g * width : (g + 1) * width] for g in range(count)], axis=1)


def pick(folded, high, width):
    result = folded[:width]
    for g in range(1, FOLD // width):
        result = jnp.where(high == g, folded[g * width : (g + 1) * width], result)
    return result


def spread(value, high, width):
    return jnp.concatenate(
        [low(jnp.where(high == g, value, 0.0)) for g in range(FOLD // width)], axis=0
    )


def high_low(index, length):
    return index // length, index % length


def small_t(raw, offset, width, columns):
    count = 128 // width
    total = None
    for p in range(count):
        lane, d = iota((PAD, columns), 0), iota((PAD, columns), 1)
        sel = ones_where((d % count == p) & (lane == offset + d // count))
        part = dot(raw[p * width : (p + 1) * width], sel)
        total = part if total is None else total + part
    return low(total)


def small_plain(raw, offset, width, rows):
    count = 128 // width
    total = None
    for p in range(count):
        d, lane = iota((rows, PAD), 0), iota((rows, PAD), 1)
        sel = ones_where((d % count == p) & (lane == offset + d // count))
        part = dot_nt(sel, raw[p * width : (p + 1) * width])
        total = part if total is None else total + part
    return low(total)


def wide_t(raw, offset, rows):
    lane, d = iota((PAD, rows), 0), iota((PAD, rows), 1)
    return low(dot(raw, ones_where(lane == offset + d)))


def wide_plain(raw, offset, rows):
    d, lane = iota((rows, PAD), 0), iota((rows, PAD), 1)
    return low(dot_nt(ones_where(lane == offset + d), raw))


def double_plain(raw, rows):
    d, lane = iota((rows, 2 * rows), 0), iota((rows, 2 * rows), 1)
    return jnp.concatenate(
        [low(dot_nt(ones_where(lane == 2 * d + p), raw)) for p in range(2)], axis=1
    )


def put_small(grad_t, offset, width):
    count = 128 // width
    columns = grad_t.shape[1]
    value = low(grad_t)
    parts = []
    for p in range(count):
        d, lane = iota((columns, PAD), 0), iota((columns, PAD), 1)
        sel = ones_where((d % count == p) & (lane == offset + d // count))
        parts.append(dot(value, sel))
    return jnp.concatenate(parts, axis=0)


def put_wide(grad_t, offset):
    columns = grad_t.shape[1]
    d, lane = iota((columns, PAD), 0), iota((columns, PAD), 1)
    return dot(low(grad_t), ones_where(lane == offset + d))


def put_double(grad_t):
    rows = grad_t.shape[1]
    d, lane = iota((rows, 2 * rows), 0), iota((rows, 2 * rows), 1)
    value = low(grad_t)
    return low(
        dot(value[:128], ones_where(lane == 2 * d)) + dot(value[128:], ones_where(lane == 2 * d + 1))
    )


def pair_forward(edge_t, basis_ref, in_ref, out_ref, raw, width, xg_ref, bt_ref, kept_row):
    edges = edge_t.shape[1]
    length = edges * width // FOLD
    down_t = small_t(raw, OFF_DOWN[width], width, D_EDGE)
    basis_t = small_t(raw, OFF_BASIS[width], width, D_BASIS)
    up_t = wide_t(raw, OFF_UP[width], width)
    act, slope_in = silu_pair(dot(down_t, edge_t))
    table = cut(low(act), width)
    total = jnp.zeros((FOLD, length), F32)
    rows = pl.ds(kept_row, width)
    items = in_ref.shape[1]
    chunk = min(CHUNK, items)
    for start in range(0, items, chunk):
        cols = pl.ds(start, chunk)
        in_high, in_low = high_low(in_ref[:, cols], length)
        out_high, out_low = high_low(out_ref[:, cols], length)
        xg = pick(dot(table, onehot(length, in_low)), in_high, width)
        bt = dot(basis_t, basis_ref[:, cols])
        xg_ref[rows, cols] = low(xg)
        bt_ref[rows, cols] = low(bt)
        total = total + dot_nt(spread(xg * bt, out_high, width), onehot(length, out_low))
    agg_t = low(uncut(total, width) * pair_scale)
    value, slope_out = silu_pair(dot(up_t, agg_t))
    return value, slope_in, agg_t, slope_out


def pair_backward(
    grad_mid, edge_t, basis_ref, in_ref, out_ref, raw, width, xg_ref, bt_ref, kept_row,
    slope_in, agg_t, slope_out,
):
    edges = edge_t.shape[1]
    length = edges * width // FOLD
    up = wide_plain(raw, OFF_UP[width], width)
    down = small_plain(raw, OFF_DOWN[width], width, D_EDGE)
    grad_out = low(grad_mid * slope_out)
    grad_up_t = dot_nt(grad_out, agg_t)
    table = cut(low(dot(up, grad_out) * pair_scale), width)
    total = jnp.zeros((FOLD, length), F32)
    grad_basis_t = jnp.zeros((width, D_BASIS), F32)
    rows = pl.ds(kept_row, width)
    items = in_ref.shape[1]
    chunk = min(CHUNK, items)
    for start in range(0, items, chunk):
        cols = pl.ds(start, chunk)
        in_high, in_low = high_low(in_ref[:, cols], length)
        out_high, out_low = high_low(out_ref[:, cols], length)
        gy = pick(dot(table, onehot(length, out_low)), out_high, width)
        grad_bt = low(gy * xg_ref[rows, cols].astype(F32))
        grad_basis_t = grad_basis_t + dot_nt(grad_bt, basis_ref[:, cols])
        moved = gy * bt_ref[rows, cols].astype(F32)
        total = total + dot_nt(spread(moved, in_high, width), onehot(length, in_low))
    grad_in = low(uncut(total, width) * slope_in)
    grad_down_t = dot_nt(grad_in, edge_t)
    small = (
        put_small(grad_down_t, OFF_DOWN[width], width)
        + put_small(grad_basis_t, OFF_BASIS[width], width)
        + put_wide(grad_up_t, OFF_UP[width])
    )
    return dot(down, grad_in), small


def block_forward(
    state_t, raw, radial_basis, tri_basis, quad_basis, tri_in, tri_out, quad_in, quad_out, dst_row,
    atoms, out_refs,
):
    edge_ref, mid_ref, slope_in_ref, agg_ref, slope_out_ref, xg_ref, bt_ref, table_ref = out_refs
    edge_t = low(state_t)
    edge_ref[...] = edge_t
    tri, s_in, agg, s_out = pair_forward(
        edge_t, tri_basis, tri_in, tri_out, raw, D_TRI, xg_ref, bt_ref, 0
    )
    slope_in_ref[:D_TRI] = low(s_in)
    agg_ref[:D_TRI] = agg
    slope_out_ref[:D_EDGE] = low(s_out)
    quad, s_in, agg, s_out = pair_forward(
        edge_t, quad_basis, quad_in, quad_out, raw, D_QUAD, xg_ref, bt_ref, D_TRI
    )
    slope_in_ref[D_TRI:] = low(s_in)
    agg_ref[D_TRI:] = agg
    slope_out_ref[D_EDGE:] = low(s_out)
    mid = state_t + tri + quad
    mid_ref[...] = mid
    radial = dot(wide_t(raw, OFF_RADIAL, D_BASIS), radial_basis[...])
    message = low(mid * radial)
    step = min(512, atoms)
    for start in range(0, atoms, step):
        table_ref[pl.ds(start, step)] = low(
            dot_nt(onehot(step, dst_row[...], start), message)
        )


def kept_shapes(edges, items, atoms):
    return [
        sds((D_EDGE, edges), BF16),
        sds((D_EDGE, edges), F32),
        sds((D_TRI + D_QUAD, edges), BF16),
        sds((D_TRI + D_QUAD, edges), BF16),
        sds((2 * D_EDGE, edges), BF16),
        sds((D_TRI + D_QUAD, items), BF16),
        sds((D_TRI + D_QUAD, items), BF16),
        sds((atoms, D_EDGE), BF16),
    ]


def first_half(
    edge_state, raw, radial_basis, tri_basis, quad_basis, tri_in, tri_out, quad_in, quad_out, dst_row,
    *out_refs,
):
    eye = ones_where(iota((D_EDGE, D_EDGE), 0) == iota((D_EDGE, D_EDGE), 1))
    state_t = dot_nt(eye, edge_state[...])
    atoms = out_refs[-1].shape[0]
    block_forward(
        state_t, raw[...], radial_basis, tri_basis, quad_basis, tri_in, tri_out, quad_in, quad_out,
        dst_row, atoms, out_refs,
    )


def atom_forward(near, far, state, free, big):
    atom_in = low((near[...].astype(F32) + far[...].astype(F32)) * edge_scale)
    first = double_plain(big[:, :256], D_EDGE)
    second = double_plain(big[:, 256:768], D_ATOM)
    act, slope = silu_pair(dot(atom_in, first))
    hidden = low(act)
    new_state = state + free * dot(hidden, second)
    return atom_in, hidden, slope, new_state


def edge_pre(sent, big, src_row, dst_row):
    src_t = low(dot_nt(big[:, 768:1024], sent))
    dst_t = low(dot_nt(big[:, 1024:1280], sent))
    atoms = sent.shape[0]
    step = min(512, atoms)
    total = None
    for start in range(0, atoms, step):
        part = dot(src_t[:, start : start + step], onehot(step, src_row[...], start))
        part = part + dot(dst_t[:, start : start + step], onehot(step, dst_row[...], start))
        total = part if total is None else total + part
    return total


def middle_half(
    near, far, atom_pack, big, mid_in, raw, radial_basis, tri_basis, quad_basis, tri_in, tri_out,
    quad_in, quad_out, src_row, dst_row,
    atom_in_ref, hidden_ref, slope_atom_ref, state_ref, free_ref, slope_edge_ref, *out_refs,
):
    owners = atom_pack.shape[0]
    count = state_ref.shape[0] // owners
    eye = iota((count, count), 0) == iota((count, count), 1)
    for s in range(owners):
        rows = pl.ds(s * count, count)
        state_ref[rows] = atom_pack[s, :count].astype(F32)
        flag = atom_pack[s, count : count + 1, :count].astype(F32)
        column = jnp.sum(jnp.where(eye, flag, 0.0), axis=1, keepdims=True)
        free_ref[rows] = low(jnp.broadcast_to(column, (count, D_ATOM)))
    atom_in, hidden, slope, state = atom_forward(
        near, far, state_ref[...], free_ref[...].astype(F32), big[...]
    )
    atom_in_ref[...] = atom_in
    hidden_ref[...] = hidden
    slope_atom_ref[...] = low(slope)
    state_ref[...] = state
    act, slope_edge = silu_pair(edge_pre(low(state), big[...], src_row, dst_row))
    slope_edge_ref[...] = low(slope_edge)
    block_forward(
        mid_in[...] + act, raw[...], radial_basis, tri_basis, quad_basis, tri_in, tri_out, quad_in,
        quad_out, dst_row, state.shape[0], out_refs,
    )


def edge_tables(
    grad_pre, sent, big, src_row, dst_row, free, slope_atom, own, own_row,
    part_ref, gain_ref, grad_proj_ref, scratch,
):
    atoms = sent.shape[0]
    count = own.shape[0]
    step = min(512, atoms)
    src_t, dst_t = big[:, 768:1024], big[:, 1024:1280]
    grad_src = jnp.zeros((D_EDGE, D_ATOM), F32)
    grad_dst = jnp.zeros((D_EDGE, D_ATOM), F32)
    for start in range(0, atoms, step):
        rows = pl.ds(start, step)
        pick_src = onehot(step, src_row[...], start)
        pick_dst = onehot(step, dst_row[...], start)
        sent_here = sent[start : start + step]
        grad_src = grad_src + dot(low(dot_nt(grad_pre, pick_src)), sent_here)
        grad_dst = grad_dst + dot(low(dot_nt(grad_pre, pick_dst)), sent_here)
        part = dot(low(dot_nt(pick_src, grad_pre)), src_t) + dot(low(dot_nt(pick_dst, grad_pre)), dst_t)
        part_ref[rows] = low(part)
        scratch[rows] = part
    grad_proj_ref[:, :D_ATOM] = low(grad_src)
    grad_proj_ref[:, D_ATOM:] = low(grad_dst)
    mine = pl.ds(pl.multiple_of(own_row, count), count)
    scratch[mine] = scratch[mine] + own
    first = double_plain(big[:, :256], D_EDGE)
    second = double_plain(big[:, 256:768], D_ATOM)
    pushed = dot_nt(low(scratch[...] * free), second) * slope_atom
    gain_ref[...] = low(dot_nt(first, low(pushed)))


def turn(
    me, near, far, state_in, free_ref, big, mid_in, src_row, dst_row, edge_cotangent, own,
    atom_in_ref, hidden_ref, slope_atom_ref, edge_out_ref, atom_out_ref, grad_ref, part_ref,
    gain_ref, grad_proj_ref, scratch, hold,
):
    free = free_ref[...].astype(F32)
    atom_in, hidden, slope, state = atom_forward(near, far, state_in[...], free, big[...])
    atom_in_ref[...] = atom_in
    hidden_ref[...] = hidden
    slope_atom_ref[...] = low(slope)
    sent = low(state)
    hold[...] = state
    count = atom_out_ref.shape[0]
    own_row = me[0] * count
    atom_out_ref[...] = low(hold[pl.ds(pl.multiple_of(own_row, count), count)])
    act, slope_edge = silu_pair(edge_pre(sent, big[...], src_row, dst_row))
    edge_out_ref[...] = low(jnp.transpose(mid_in[...] + act))
    eye = ones_where(iota((D_EDGE, D_EDGE), 0) == iota((D_EDGE, D_EDGE), 1))
    grad = dot_nt(eye, edge_cotangent[...])
    grad_ref[...] = grad
    edge_tables(
        low(grad * slope_edge), sent, big[...], src_row, dst_row, free, slope,
        own[...].astype(F32), own_row, part_ref, gain_ref, grad_proj_ref, scratch,
    )


def block_backward(
    near, far, grad_in, mid, raw, radial_basis, tri_basis, quad_basis, tri_in, tri_out, quad_in,
    quad_out, dst_row, edge_t, slope_in, agg, slope_out, xg_ref, bt_ref, small_ref,
):
    gain_t = low(near[...].astype(F32) + far[...].astype(F32))
    atoms = gain_t.shape[1]
    step = min(512, atoms)
    grad_message = None
    for start in range(0, atoms, step):
        part = dot(gain_t[:, start : start + step], onehot(step, dst_row[...], start))
        grad_message = part if grad_message is None else grad_message + part
    grad_message = grad_message * edge_scale
    weights = raw[...]
    radial = dot(wide_t(weights, OFF_RADIAL, D_BASIS), radial_basis[...])
    grad_mid = grad_in[...] + grad_message * radial
    grad_radial = low(grad_message * mid[...])
    small = put_wide(dot_nt(grad_radial, radial_basis[...]), OFF_RADIAL)
    tri, more = pair_backward(
        grad_mid, edge_t[...], tri_basis, tri_in, tri_out, weights, D_TRI, xg_ref, bt_ref, 0,
        slope_in[:D_TRI].astype(F32), agg[:D_TRI], slope_out[:D_EDGE].astype(F32),
    )
    small = small + more
    quad, more = pair_backward(
        grad_mid, edge_t[...], quad_basis, quad_in, quad_out, weights, D_QUAD, xg_ref, bt_ref, D_TRI,
        slope_in[D_TRI:].astype(F32), agg[D_TRI:], slope_out[D_EDGE:].astype(F32),
    )
    small_ref[...] = low(small + more)
    return grad_mid + tri + quad


def back_pairs(*refs):
    *rest, small_ref, grad_ref = refs
    grad_ref[...] = block_backward(*rest, small_ref)


def back_last(*refs):
    *rest, small_ref, grad_ref = refs
    grad_ref[...] = jnp.transpose(block_backward(*rest, small_ref))


def atom_sums(me, arrived, own, free, hidden, slope_atom, atom_in, grad_proj, big, grad_ref, out_ref):
    owners, count, width = arrived.shape
    total = own[...].astype(F32)
    for s in range(owners):
        total = total + arrived[s].astype(F32)
    grad_ref[...] = total
    mine = pl.ds(pl.multiple_of(me[0] * count, count), count)
    update = total * free[mine].astype(F32)
    second = double_plain(big[:, 256:768], D_ATOM)
    pushed = dot_nt(low(update), second) * slope_atom[mine].astype(F32)
    grad_second_t = dot(low(jnp.transpose(update)), hidden[mine])
    grad_first_t = dot(low(jnp.transpose(pushed)), atom_in[mine])
    out_ref[:, :256] = put_double(grad_first_t)
    out_ref[:, 256:768] = put_double(grad_second_t)
    out_ref[:, 768:] = grad_proj[...]


def back_tables(
    me, grad, slope_edge, state, big, src_row, dst_row, free_ref, slope_atom, own,
    part_ref, gain_ref, grad_proj_ref, scratch,
):
    grad_pre = low(grad[...] * slope_edge[...].astype(F32))
    edge_tables(
        grad_pre, low(state[...]), big[...], src_row, dst_row, free_ref[...].astype(F32),
        slope_atom[...].astype(F32), own[...], me[0] * own.shape[0], part_ref, gain_ref, grad_proj_ref,
        scratch,
    )


def shard_sum(arrived, out_ref):
    total = arrived[0].astype(F32)
    for s in range(1, arrived.shape[0]):
        total = total + arrived[s].astype(F32)
    out_ref[...] = low(total)


def adam(arrived, weights, first, second, grad_ref, weights_ref, first_ref, second_ref, low_ref):
    total = arrived[0].astype(F32)
    for s in range(1, arrived.shape[0]):
        total = total + arrived[s].astype(F32)
    grad = jnp.concatenate(
        [
            total[:, :SMALL],
            total[:, PAD : PAD + BIG],
            total[:, PAD + BIG : PAD + BIG + SMALL],
            total[:, 2 * PAD + BIG :],
        ],
        axis=1,
    )
    grad_ref[...] = grad
    old = weights[...]
    new_first = beta_one * first[...] + (1.0 - beta_one) * grad
    new_second = beta_two * second[...] + (1.0 - beta_two) * grad * grad
    first_ref[...] = new_first
    second_ref[...] = new_second
    first_hat = new_first / (1.0 - beta_one**adam_step)
    second_hat = new_second / (1.0 - beta_two**adam_step)
    new = old - learn_rate * (first_hat / (jnp.sqrt(second_hat) + epsilon) + decay_rate * old)
    weights_ref[...] = new
    low_ref[...] = low(new)


def call_scratch(body, outs, args, scratch, flops=10**9):
    return pl.pallas_call(
        body,
        out_shape=outs,
        in_specs=[pl.BlockSpec(memory_space=pltpu.SMEM)]
        + [pl.BlockSpec(memory_space=pltpu.VMEM)] * (len(args) - 1),
        out_specs=[pl.BlockSpec(memory_space=pltpu.VMEM)] * len(outs),
        scratch_shapes=[pltpu.VMEM(s, F32) for s in scratch],
        compiler_params=pltpu.CompilerParams(vmem_limit_bytes=40 * 2**20),
        cost_estimate=pl.CostEstimate(flops=flops, bytes_accessed=4 * 2**20, transcendentals=0),
        name=body.__name__,
    )(*args)


def to_all(value, owners):
    return lax.all_to_all(
        jnp.broadcast_to(value[None], (owners,) + value.shape), "shard", split_axis=0, concat_axis=0
    )


def sum_pair(table, owners):
    far = None
    step = 1
    while step < owners:
        if far is not None:
            table = table + far
        far = lax.ppermute(table, "shard", [(i, i ^ step) for i in range(owners)])
        step = 2 * step
    return table, far


def per_device(
    edge_state, atom_state, radial_basis, triplet_basis, quad_basis, dst_owner, dst_local, src_owner,
    src_local, triplet_in, triplet_out, quad_in, quad_out, fixed_atoms, edge_cotangent,
    atom_cotangent, weights, first_moment, second_moment,
):
    owners = lax.axis_size("shard")
    edges = edge_state.shape[0]
    count = atom_state.shape[0]
    atoms = count * owners
    items = triplet_in.shape[0]
    me = lax.axis_index("shard").astype(jnp.int32).reshape(1)
    weights_t = jnp.transpose(weights)
    low_t = weights_t.astype(BF16)
    cols = low_t.shape[0]
    half = SMALL + BIG
    gap = ((0, 0), (0, PAD - SMALL))
    small_one = jnp.pad(low_t[:, :SMALL], gap)
    rest = jnp.concatenate(
        [low_t[:, SMALL:half], jnp.pad(low_t[:, half : half + SMALL], gap), low_t[:, half + SMALL :]],
        axis=1,
    )
    raw_one = to_all(small_one, owners).reshape(owners * cols, PAD)
    rest = to_all(rest, owners).reshape(owners * cols, 2 * BIG + PAD)
    big_one, raw_two, big_two = rest[:, :BIG], rest[:, BIG : BIG + PAD], rest[:, BIG + PAD :]
    flag = jnp.zeros((16, D_ATOM), BF16).at[0, :count].set((1 - fixed_atoms).astype(BF16))
    atom_pack = to_all(jnp.concatenate([atom_state, flag], axis=0), owners)

    dst_row = (dst_owner[:, 0] * count + dst_local).reshape(1, edges)
    src_row = (src_owner[:, 0] * count + src_local).reshape(1, edges)
    graph = [
        jnp.transpose(radial_basis),
        jnp.transpose(triplet_basis),
        jnp.transpose(quad_basis),
        triplet_in.reshape(1, items),
        triplet_out.reshape(1, items),
        quad_in.reshape(1, items),
        quad_out.reshape(1, items),
    ]
    kept = kept_shapes(edges, items, atoms)
    edge_shape = sds((D_EDGE, edges), BF16)
    atom_shapes = [
        sds((atoms, D_EDGE), BF16),
        sds((atoms, D_ATOM), BF16),
        sds((atoms, D_ATOM), BF16),
    ]
    *kept_one, table = call(
        first_half, kept, [edge_state, raw_one] + graph + [dst_row], flops=8 * 10**9
    )
    near, far = sum_pair(table, owners)
    atom_in_one, hidden_one, slope_one, state_one, free, slope_edge_one, *kept_two, table = call(
        middle_half,
        atom_shapes + [sds((atoms, D_ATOM), F32), sds((atoms, D_ATOM), BF16), edge_shape] + kept,
        [near, far, atom_pack, big_one, kept_one[1], raw_two] + graph + [src_row, dst_row],
        flops=10 * 10**9,
    )
    near, far = sum_pair(table, owners)
    tables_shape = [
        sds((atoms, D_ATOM), BF16),
        sds((D_EDGE, atoms), BF16),
        sds((D_EDGE, 2 * D_ATOM), BF16),
    ]
    (
        atom_in_two, hidden_two, slope_two, edge_out, atom_out, grad_t, part, gain, grad_proj_two,
    ) = call_scratch(
        turn,
        atom_shapes
        + [sds((edges, D_EDGE), BF16), sds((count, D_ATOM), BF16), sds((D_EDGE, edges), F32)]
        + tables_shape,
        [me, near, far, state_one, free, big_two, kept_two[1], src_row, dst_row, edge_cotangent,
         atom_cotangent],
        [(atoms, D_ATOM), (atoms, D_ATOM)],
        flops=2 * 10**9,
    )

    def summed(part):
        return lax.all_to_all(
            part.reshape(owners, count, D_ATOM), "shard", split_axis=0, concat_axis=0
        )

    def backward(body, near, far, grad_t, kept, raw, out):
        edge_t, mid, slope_in, agg, slope_out, xg, bt = kept
        return call(
            body,
            [sds((D_EDGE, PAD), BF16), out],
            [near, far, grad_t, mid, raw]
            + graph
            + [dst_row, edge_t, slope_in, agg, slope_out, xg, bt],
            flops=10 * 10**9,
        )

    def sums(part, own, hidden, slope, atom_in, grad_proj, big):
        return call(
            atom_sums,
            [sds((count, D_ATOM), F32), sds((D_EDGE, BIG), BF16)],
            [me, summed(part), own, free, hidden, slope, atom_in, grad_proj, big],
            flops=10**9,
            smem=1,
        )

    near, far = sum_pair(gain, owners)
    grad_atom, grad_big_two = sums(
        part, atom_cotangent, hidden_two, slope_two, atom_in_two, grad_proj_two, big_two
    )
    grad_small_two, grad_t = backward(
        back_pairs, near, far, grad_t, kept_two, raw_two, sds((D_EDGE, edges), F32)
    )
    part, gain, grad_proj_one = call_scratch(
        back_tables,
        tables_shape,
        [me, grad_t, slope_edge_one, state_one, big_one, src_row, dst_row, free, slope_one, grad_atom],
        [(atoms, D_ATOM)],
        flops=2 * 10**9,
    )
    near, far = sum_pair(gain, owners)
    grad_atom, grad_big_one = sums(
        part, grad_atom, hidden_one, slope_one, atom_in_one, grad_proj_one, big_one
    )
    grad_small_one, grad_edge = backward(
        back_last, near, far, grad_t, kept_one, raw_one, sds((edges, D_EDGE), F32)
    )
    grads = jnp.concatenate([grad_small_one, grad_big_one, grad_small_two, grad_big_two], axis=1)
    grads = lax.all_to_all(
        grads.reshape(owners, cols, 2 * (PAD + BIG)), "shard", split_axis=0, concat_axis=0
    )
    [grads] = call(shard_sum, [sds((cols, 2 * (PAD + BIG)), BF16)], [grads], flops=10**8)
    grads = lax.all_gather(grads, "group", axis=0)
    rows = weights.shape[0]
    results = call(
        adam,
        [sds((cols, rows), F32)] * 4 + [sds((cols, rows), BF16)],
        [grads, weights_t, jnp.transpose(first_moment), jnp.transpose(second_moment)],
        flops=10**8,
    )
    return (edge_out, atom_out, grad_edge, grad_atom) + tuple(jnp.transpose(r) for r in results)


def solution(mesh):
    both = P(("group", "shard"), None)
    line = P(("group", "shard"))
    flat = P(None, "shard")
    in_specs = (both,) * 6 + (line, both) + (line,) * 6 + (both, both) + (flat,) * 3
    out_specs = (both,) * 4 + (flat,) * 5
    return jax.shard_map(
        per_device, mesh=mesh, in_specs=in_specs, out_specs=out_specs, check_vma=False
    )
```

```python
import jax
import jax.numpy as jnp
from jax import lax
from jax.experimental import pallas as pl
from jax.experimental.pallas import tpu as pltpu
from jax.sharding import PartitionSpec as P

D_EDGE = 128
D_ATOM = 256
D_TRI = 64
D_QUAD = 32
D_BASIS = 16
BLOCKS = 2
FOLD = 256
CHUNK = 1024
SMALL = 220
BIG = 1280
PAD = 256
ROWS = 16

edge_scale = 0.25
pair_scale = 0.5
beta_one = 0.5
beta_two = 0.5
learn_rate = 0.1
decay_rate = 0.01
epsilon = 1e-08
adam_step = 4

OFF_DOWN = {D_TRI: 0, D_QUAD: 136}
OFF_BASIS = {D_TRI: 64, D_QUAD: 168}
OFF_UP = {D_TRI: 72, D_QUAD: 172}
OFF_RADIAL = 204

F32 = jnp.float32
BF16 = jnp.bfloat16


def sds(shape, dtype):
    return jax.ShapeDtypeStruct(shape, dtype)


class Late:
    def __init__(self, source, ref, sem):
        self.ref, self.copy, self.here = ref, pltpu.make_async_copy(source, ref, sem), False
        self.shape = ref.shape
        self.copy.start()

    def wait(self):
        if not self.here:
            self.copy.wait()
            self.here = True

    def __getitem__(self, index):
        self.wait()
        return self.ref[index]


class Kept:
    def __init__(self, target, ref, sem):
        self.ref, self.copy, self.sent = ref, pltpu.make_async_copy(ref, target, sem), False
        self.shape, self.dtype = ref.shape, ref.dtype

    def __getitem__(self, index):
        return self.ref[index]

    def __setitem__(self, index, value):
        self.ref[index] = value

    def send(self):
        if not self.sent:
            self.copy.start()
            self.sent = True


def send(*refs):
    for ref in refs:
        if isinstance(ref, Kept):
            ref.send()


def call(body, outs, args, flops=10**9, late=(), kept=(), smem=0, scratch=()):
    moved = [args[i] for i in late] + [outs[i] for i in kept]

    def kernel(*refs):
        refs = list(refs)
        ins, rest = refs[: len(args)], refs[len(args) :]
        results, rest = rest[: len(outs)], rest[len(outs) :]
        extra, rest = rest[: len(scratch)], rest[len(scratch) :]
        buffers, sems = rest[: len(moved)], rest[len(moved) :]
        for k, i in enumerate(late):
            ins[i] = Late(ins[i], buffers[k], sems[k])
        for k, i in enumerate(kept, len(late)):
            results[i] = Kept(results[i], buffers[k], sems[k])
        body(*ins, *results, *extra)
        for i in late:
            ins[i].wait()
        for i in kept:
            results[i].send()
        for i in kept:
            results[i].copy.wait()

    args = [pltpu.with_memory_space_constraint(x, pltpu.HBM) if i in late else x for i, x in enumerate(args)]
    outs = [pltpu.HBM(x.shape, x.dtype) if i in kept else x for i, x in enumerate(outs)]
    space = [pltpu.SMEM] * smem + [pltpu.VMEM] * (len(args) - smem)
    for i in late:
        space[i] = pltpu.HBM
    return pl.pallas_call(
        kernel,
        out_shape=outs,
        in_specs=[pl.BlockSpec(memory_space=s) for s in space],
        out_specs=[
            pl.BlockSpec(memory_space=pltpu.HBM if i in kept else pltpu.VMEM)
            for i in range(len(outs))
        ],
        scratch_shapes=[pltpu.VMEM(shape, F32) for shape in scratch]
        + [pltpu.VMEM(m.shape, m.dtype) for m in moved]
        + [pltpu.SemaphoreType.DMA] * len(moved),
        compiler_params=pltpu.CompilerParams(vmem_limit_bytes=40 * 2**20),
        cost_estimate=pl.CostEstimate(flops=flops, bytes_accessed=2**20, transcendentals=0),
        name=body.__name__,
    )(*args)


def dot(a, b):
    return jnp.dot(a, b, preferred_element_type=F32)


def dot_nt(a, b):
    return lax.dot_general(a, b, (((1,), (1,)), ((), ())), preferred_element_type=F32)


def low(v):
    return v.astype(BF16)


def iota(shape, axis):
    return lax.broadcasted_iota(jnp.int32, shape, axis)


def ones_where(mask):
    return jnp.where(mask, 1.0, 0.0).astype(BF16)


def onehot(count, row, first=0):
    return ones_where(iota((count, row.shape[1]), 0) + first == row)


def sigmoid(v):
    return 1.0 / (1.0 + jnp.exp(-v))


def silu_pair(v):
    s = sigmoid(v)
    return v * s, s * (1.0 + v * (1.0 - s))


def cut(value, width):
    count = FOLD // width
    length = value.shape[1] // count
    return jnp.concatenate([value[:, g * length : (g + 1) * length] for g in range(count)], axis=0)


def uncut(value, width):
    count = FOLD // width
    return jnp.concatenate([value[g * width : (g + 1) * width] for g in range(count)], axis=1)


def pick(folded, high, width):
    result = folded[:width]
    for g in range(1, FOLD // width):
        result = jnp.where(high == g, folded[g * width : (g + 1) * width], result)
    return result


def spread(value, high, width):
    return jnp.concatenate(
        [low(jnp.where(high == g, value, 0.0)) for g in range(FOLD // width)], axis=0
    )


def high_low(index, length):
    return index // length, index % length


def small_t(raw, offset, width, columns):
    count = 128 // width
    total = None
    for p in range(count):
        lane, d = iota((PAD, columns), 0), iota((PAD, columns), 1)
        sel = ones_where((d % count == p) & (lane == offset + d // count))
        part = dot(raw[p * width : (p + 1) * width], sel)
        total = part if total is None else total + part
    return low(total)


def small_plain(raw, offset, width, rows):
    count = 128 // width
    total = None
    for p in range(count):
        d, lane = iota((rows, PAD), 0), iota((rows, PAD), 1)
        sel = ones_where((d % count == p) & (lane == offset + d // count))
        part = dot_nt(sel, raw[p * width : (p + 1) * width])
        total = part if total is None else total + part
    return low(total)


def wide_t(raw, offset, rows):
    lane, d = iota((PAD, rows), 0), iota((PAD, rows), 1)
    return low(dot(raw, ones_where(lane == offset + d)))


def wide_plain(raw, offset, rows):
    d, lane = iota((rows, PAD), 0), iota((rows, PAD), 1)
    return low(dot_nt(ones_where(lane == offset + d), raw))


def double_plain(raw, rows):
    d, lane = iota((rows, 2 * rows), 0), iota((rows, 2 * rows), 1)
    return jnp.concatenate(
        [low(dot_nt(ones_where(lane == 2 * d + p), raw)) for p in range(2)], axis=1
    )


def put_small(grad_t, offset, width):
    count = 128 // width
    columns = grad_t.shape[1]
    value = low(grad_t)
    parts = []
    for p in range(count):
        d, lane = iota((columns, PAD), 0), iota((columns, PAD), 1)
        sel = ones_where((d % count == p) & (lane == offset + d // count))
        parts.append(dot(value, sel))
    return jnp.concatenate(parts, axis=0)


def put_wide(grad_t, offset):
    columns = grad_t.shape[1]
    d, lane = iota((columns, PAD), 0), iota((columns, PAD), 1)
    return dot(low(grad_t), ones_where(lane == offset + d))


def put_double(grad_t):
    rows = grad_t.shape[1]
    d, lane = iota((rows, 2 * rows), 0), iota((rows, 2 * rows), 1)
    value = low(grad_t)
    return low(
        dot(value[:128], ones_where(lane == 2 * d)) + dot(value[128:], ones_where(lane == 2 * d + 1))
    )


def small_matrices(raw):
    return (
        [small_t(raw, OFF_DOWN[w], w, D_EDGE) for w in (D_TRI, D_QUAD)]
        + [small_t(raw, OFF_BASIS[w], w, D_BASIS) for w in (D_TRI, D_QUAD)]
        + [wide_t(raw, OFF_UP[w], w) for w in (D_TRI, D_QUAD)]
        + [wide_t(raw, OFF_RADIAL, D_BASIS)]
    )


def back_matrices(raw):
    return [wide_plain(raw, OFF_UP[w], w) for w in (D_TRI, D_QUAD)] + [
        small_plain(raw, OFF_DOWN[w], w, D_EDGE) for w in (D_TRI, D_QUAD)
    ]


SMALL_SHAPES = [
    (D_TRI, D_EDGE), (D_QUAD, D_EDGE), (D_TRI, D_BASIS), (D_QUAD, D_BASIS), (D_EDGE, D_TRI),
    (D_EDGE, D_QUAD), (D_EDGE, D_BASIS),
]
BACK_SHAPES = [(D_TRI, D_EDGE), (D_QUAD, D_EDGE), (D_EDGE, D_TRI), (D_EDGE, D_QUAD)]


def slots(width):
    return -(-width // PAD)


def padded(value, rows, lanes):
    have, wide = value.shape
    if wide < lanes:
        value = jnp.concatenate([value, jnp.zeros((have, lanes - wide), value.dtype)], axis=1)
    if have < rows:
        value = jnp.concatenate([value, jnp.zeros((rows - have, lanes), value.dtype)], axis=0)
    return value


def pack_first(weights, out_ref):
    head = low(padded(weights[:, :SMALL], ROWS, PAD))
    for s in range(out_ref.shape[0]):
        out_ref[s] = head


def pack_cargo(me, weights, state, fixed, out_ref, hold):
    count = state.shape[0]
    free = (1 - fixed[...]).astype(F32)
    out_ref[0, :count] = state[...]
    out_ref[0, count : count + ROWS] = low(padded(free, ROWS, PAD))
    values = weights[...]
    half = SMALL + BIG
    gap = jnp.zeros((values.shape[0], PAD - SMALL), F32)
    one = jnp.concatenate([values[:, SMALL : half + SMALL], gap], axis=1)
    two = padded(values[:, half + SMALL :], values.shape[0], BIG + PAD)
    groups, _, width = hold.shape
    base = count + ROWS
    for side in (one, two):
        for g in range(groups):
            hold[g] = side[:, g * width : (g + 1) * width]
        mine = padded(hold[me[1]], ROWS, slots(width) * PAD)
        for k in range(slots(width)):
            out_ref[0, base : base + ROWS] = low(mine[:, k * PAD : (k + 1) * PAD])
            base = base + ROWS


def order_of(owners):
    order, step = [0], owners // 2
    while step:
        order = order + [k ^ step for k in order]
        step = step // 2
    return order


def collect(me, *refs):
    *cargo, one_ref, two_ref = refs
    rows = cargo[0].shape[1]
    owners = sum(c.shape[0] for c in cargo)
    full, width = one_ref.shape
    cols = full // owners
    count = slots(width)
    base = rows - 2 * count * ROWS
    order = order_of(owners)
    shape = (full, owners * ROWS)
    row, col = iota(shape, 0), iota(shape, 1)
    owner, inside = row // cols, row % cols
    sel = None
    for position, k in enumerate(order):
        hit = (col == position * ROWS + inside) & (owner == (me[0] ^ k))
        sel = hit if sel is None else sel | hit
    sel = ones_where(sel)
    for side, ref in ((0, one_ref), (1, two_ref)):
        for k in range(count):
            start = base + (side * count + k) * ROWS
            values = jnp.concatenate(
                [c[i, start : start + ROWS] for c in cargo for i in range(c.shape[0])], axis=0
            )
            lanes = min(PAD, width - k * PAD)
            ref[:, k * PAD : k * PAD + lanes] = low(dot(sel, values))[:, :lanes]


def joined(me, pieces, hold):
    for k, piece in enumerate(pieces):
        hold[me[1] ^ k] = piece[...].astype(F32)
    return low(jnp.concatenate([hold[g] for g in range(len(pieces))], axis=1))


def small_rows(pack, cols):
    owners = pack.shape[0]
    value = pack[...].reshape(owners * ROWS, PAD)
    if cols == ROWS:
        return value
    c, row = iota((owners * cols, owners * ROWS), 0), iota((owners * cols, owners * ROWS), 1)
    return low(dot(ones_where(row == c // cols * ROWS + c % cols), value))


def prepare_one(me, pack, *refs):
    *rest, hold = refs
    groups = hold.shape[0]
    wide = joined(me, rest[:groups], hold)
    raw_one = small_rows(pack, D_EDGE // pack.shape[0])
    raw_two = wide[:, BIG:]
    values = back_matrices(raw_one) + [wide_t(raw_one, OFF_RADIAL, D_BASIS)]
    values = values + small_matrices(raw_two) + back_matrices(raw_two)
    values = values + [double_plain(wide[:, :256], D_EDGE), double_plain(wide[:, 256:768], D_ATOM)]
    for ref, value in zip(rest[groups:], values + [wide[:, :BIG]]):
        ref[...] = value


def prepare_two(me, *refs):
    *rest, hold = refs
    groups = hold.shape[0]
    big = joined(me, rest[:groups], hold)
    first_ref, second_ref, big_ref = rest[groups:]
    first_ref[...] = double_plain(big[:, :256], D_EDGE)
    second_ref[...] = double_plain(big[:, 256:768], D_ATOM)
    big_ref[...] = big[:, :BIG]


LARGE_SHAPES = [(D_EDGE, D_ATOM), (D_ATOM, D_ATOM), (D_EDGE, BIG)]
PREPARED = BACK_SHAPES + [(D_EDGE, D_BASIS)] + SMALL_SHAPES + BACK_SHAPES + LARGE_SHAPES


def pair_forward(edge_t, basis_ref, in_ref, out_ref, down_t, basis_t, up_t, xg_ref, bt_ref):
    width, edges = down_t.shape[0], edge_t.shape[1]
    length = edges * width // FOLD
    act, slope_in = silu_pair(dot(down_t, edge_t))
    table = cut(low(act), width)
    total = jnp.zeros((FOLD, length), F32)
    items = in_ref.shape[1]
    chunk = min(CHUNK, items)
    for start in range(0, items, chunk):
        cols = slice(start, start + chunk)
        in_high, in_low = high_low(in_ref[:, cols], length)
        out_high, out_low = high_low(out_ref[:, cols], length)
        xg = pick(dot(table, onehot(length, in_low)), in_high, width)
        bt = dot(basis_t, basis_ref[:, cols])
        xg_ref[:, cols] = low(xg)
        bt_ref[:, cols] = low(bt)
        total = total + dot_nt(spread(xg * bt, out_high, width), onehot(length, out_low))
    send(xg_ref, bt_ref)
    agg_t = low(uncut(total, width) * pair_scale)
    value, slope_out = silu_pair(dot(up_t, agg_t))
    return value, slope_in, agg_t, slope_out


def pair_backward(
    grad_mid, edge_t, basis_ref, in_ref, out_ref, up, down, slope_out, agg_t, xg_ref, bt_ref, slope_in,
):
    width, edges = up.shape[0], slope_in.shape[1]
    length = edges * width // FOLD
    grad_out = low(grad_mid * slope_out[...].astype(F32))
    grad_up_t = dot_nt(grad_out, agg_t[...])
    table = cut(low(dot(up, grad_out) * pair_scale), width)
    total = jnp.zeros((FOLD, length), F32)
    grad_basis_t = jnp.zeros((width, D_BASIS), F32)
    items = in_ref.shape[1]
    chunk = min(CHUNK, items)
    for start in range(0, items, chunk):
        cols = slice(start, start + chunk)
        in_high, in_low = high_low(in_ref[:, cols], length)
        out_high, out_low = high_low(out_ref[:, cols], length)
        gy = pick(dot(table, onehot(length, out_low)), out_high, width)
        grad_bt = low(gy * xg_ref[:, cols].astype(F32))
        grad_basis_t = grad_basis_t + dot_nt(grad_bt, basis_ref[:, cols])
        moved = gy * bt_ref[:, cols].astype(F32)
        total = total + dot_nt(spread(moved, in_high, width), onehot(length, in_low))
    grad_in = low(uncut(total, width) * slope_in[...].astype(F32))
    grad_down_t = dot_nt(grad_in, edge_t[...])
    small = (
        put_small(grad_down_t, OFF_DOWN[width], width)
        + put_small(grad_basis_t, OFF_BASIS[width], width)
        + put_wide(grad_up_t, OFF_UP[width])
    )
    return dot(down, grad_in), small


def block_forward(state_t, matrices, graph, dst_row, out_refs):
    radial_basis, tri_basis, quad_basis, tri_in, tri_out, quad_in, quad_out = graph
    down_tri, down_quad, basis_tri, basis_quad, up_tri, up_quad, radial_t = matrices
    mid_ref, mid_low_ref = out_refs[:2]
    tri_refs, edge_ref, quad_refs, table_ref = out_refs[2:7], out_refs[7], out_refs[8:13], out_refs[13]
    edge_t = low(state_t)
    edge_ref[...] = edge_t
    send(edge_ref)
    mid = state_t
    for refs, basis, inner, outer, down, basis_t, up in (
        (tri_refs, tri_basis, tri_in, tri_out, down_tri, basis_tri, up_tri),
        (quad_refs, quad_basis, quad_in, quad_out, down_quad, basis_quad, up_quad),
    ):
        slope_out_ref, agg_ref, xg_ref, bt_ref, slope_in_ref = refs
        value, slope_in, agg, slope_out = pair_forward(
            edge_t, basis, inner, outer, down, basis_t, up, xg_ref, bt_ref
        )
        slope_in_ref[...] = low(slope_in)
        agg_ref[...] = agg
        slope_out_ref[...] = low(slope_out)
        send(slope_in_ref, agg_ref, slope_out_ref)
        mid = mid + value
    mid_ref[...] = mid
    mid_low_ref[...] = low(mid)
    send(mid_ref, mid_low_ref)
    message = low(mid * dot(radial_t, radial_basis[...]))
    atoms = table_ref.shape[0]
    step = min(512, atoms)
    for start in range(0, atoms, step):
        rows = slice(start, start + step)
        table_ref[rows] = low(dot_nt(onehot(step, dst_row[...], start), message))


def kept_shapes(edges, items):
    edge = ((D_EDGE, edges), BF16)
    tri, quad = [
        [edge, ((w, edges), BF16), ((w, items), BF16), ((w, items), BF16), ((w, edges), BF16)]
        for w in (D_TRI, D_QUAD)
    ]
    return [sds(*x) for x in [((D_EDGE, edges), F32), edge] + tri + [edge] + quad]


KEPT = 13


def first_half(edge_state, pack, *refs):
    graph, dst_row, out_refs = refs[:7], refs[7], refs[8:]
    eye = ones_where(iota((D_EDGE, D_EDGE), 0) == iota((D_EDGE, D_EDGE), 1))
    state_t = dot_nt(eye, edge_state[...])
    raw = small_rows(pack, D_EDGE // pack.shape[0])
    block_forward(state_t, small_matrices(raw), graph, dst_row, out_refs)


def atom_forward(near, far, state, free, first, second):
    atom_in = low((near[...].astype(F32) + far[...].astype(F32)) * edge_scale)
    act, slope = silu_pair(dot(atom_in, first[...]))
    hidden = low(act)
    new_state = state + free * dot(hidden, second[...])
    return atom_in, hidden, slope, new_state


def edge_pre(sent, big, src_row, dst_row):
    src_t = low(dot_nt(big[:, 768:1024], sent))
    dst_t = low(dot_nt(big[:, 1024:1280], sent))
    atoms = sent.shape[0]
    step = min(512, atoms)
    total = None
    for start in range(0, atoms, step):
        part = dot(src_t[:, start : start + step], onehot(step, src_row[...], start))
        part = part + dot(dst_t[:, start : start + step], onehot(step, dst_row[...], start))
        total = part if total is None else total + part
    return total


def middle_half(me, near, far, big, first, second, mid_in, *refs):
    matrices, graph, src_row, dst_row = refs[:7], refs[7:14], refs[14], refs[15]
    atoms = near.shape[0]
    cargo, refs = refs[16:], None
    split = 0
    owners = 0
    while len(cargo[split].shape) == 3:
        owners = owners + cargo[split].shape[0]
        split = split + 1
    cargo, rest = cargo[:split], cargo[split:]
    atom_in_ref, hidden_ref, slope_atom_ref, state_ref, sent_ref, free_ref, slope_edge_ref = rest[:7]
    *out_refs, free_wide = rest[7:]
    count = atoms // owners
    eye = iota((count, count), 0) == iota((count, count), 1)
    order = order_of(owners)
    position = 0
    for pieces in cargo:
        for i in range(pieces.shape[0]):
            rows = pl.ds(pl.multiple_of((me[0] ^ order[position]) * count, count), count)
            state_ref.ref[rows] = pieces[i, :count].astype(F32)
            flag = pieces[i, count : count + 1, :count].astype(F32)
            column = jnp.sum(jnp.where(eye, flag, 0.0), axis=1, keepdims=True)
            free_wide[rows] = jnp.broadcast_to(column, (count, D_ATOM))
            position = position + 1
    free_ref[...] = low(free_wide[...])
    send(free_ref)
    atom_in, hidden, slope, state = atom_forward(
        near, far, state_ref[...], free_wide[...], first, second
    )
    atom_in_ref[...] = atom_in
    hidden_ref[...] = hidden
    slope_atom_ref[...] = low(slope)
    state_ref[...] = state
    sent = low(state)
    sent_ref[...] = sent
    send(atom_in_ref, hidden_ref, slope_atom_ref, state_ref, sent_ref)
    act, slope_edge = silu_pair(edge_pre(sent, big, src_row, dst_row))
    slope_edge_ref[...] = low(slope_edge)
    send(slope_edge_ref)
    block_forward(mid_in[...] + act, [m[...] for m in matrices], graph, dst_row, out_refs)


def edge_tables(
    grad_pre, big, first, second, src_row, dst_row, free, slope_atom, grad_atoms, gain_ref, update_ref,
    pushed_ref,
):
    atoms = free.shape[0]
    step = min(512, atoms)
    src_t, dst_t = big[:, 768:1024], big[:, 1024:1280]
    for start in range(0, atoms, step):
        rows = slice(start, start + step)
        pick_src = onehot(step, src_row[...], start)
        pick_dst = onehot(step, dst_row[...], start)
        part = dot(low(dot_nt(pick_src, grad_pre)), src_t) + dot(low(dot_nt(pick_dst, grad_pre)), dst_t)
        grad_atoms[rows] = grad_atoms[rows] + part
    update = low(grad_atoms[...] * free)
    update_ref[...] = update
    send(update_ref)
    pushed = low(dot_nt(update, second[...]) * slope_atom)
    pushed_ref[...] = pushed
    send(pushed_ref)
    gain_ref[...] = low(dot_nt(first[...], pushed))


def turn(
    me, near, far, big, first, second, src_row, dst_row, edge_cotangent, own, state_in, free_ref, mid_in,
    atom_in_ref, hidden_ref, sent_ref, edge_ref, atom_out_ref, cotangent_ref, grad_pre_ref, atoms_ref,
    gain_ref, update_ref, pushed_ref, hold,
):
    free = free_ref[...].astype(F32)
    atom_in, hidden, slope, state = atom_forward(near, far, state_in[...], free, first, second)
    atom_in_ref[...] = atom_in
    hidden_ref[...] = hidden
    sent = low(state)
    sent_ref[...] = sent
    send(atom_in_ref, hidden_ref, sent_ref)
    hold[...] = state
    count = atom_out_ref.shape[0]
    mine = pl.ds(pl.multiple_of(me[0] * count, count), count)
    atom_out_ref[...] = low(hold[mine])
    act, slope_edge = silu_pair(edge_pre(sent, big, src_row, dst_row))
    edge_ref[...] = mid_in[...] + act
    send(edge_ref, atom_out_ref)
    eye = ones_where(iota((D_EDGE, D_EDGE), 0) == iota((D_EDGE, D_EDGE), 1))
    cotangent = dot_nt(eye, edge_cotangent[...])
    cotangent_ref[...] = cotangent
    grad_pre = low(cotangent * slope_edge)
    grad_pre_ref[...] = grad_pre
    send(cotangent_ref, grad_pre_ref)
    atoms_ref[...] = jnp.zeros(atoms_ref.shape, F32)
    atoms_ref.ref[mine] = own[...].astype(F32)
    edge_tables(
        grad_pre, big, first, second, src_row, dst_row, free, slope, atoms_ref, gain_ref, update_ref,
        pushed_ref,
    )


def large_grads(me, update, pushed, atom_in, hidden, sent, grad_pre, src_row, dst_row, small, out_ref, hold):
    atoms = sent.shape[0]
    step = min(512, atoms)
    grad_src = jnp.zeros((D_EDGE, D_ATOM), F32)
    grad_dst = jnp.zeros((D_EDGE, D_ATOM), F32)
    for start in range(0, atoms, step):
        rows = slice(start, start + step)
        grads = grad_pre[...]
        grad_src = grad_src + dot(low(dot_nt(grads, onehot(step, src_row[...], start))), sent[rows])
        grad_dst = grad_dst + dot(low(dot_nt(grads, onehot(step, dst_row[...], start))), sent[rows])
    grad_second_t = dot(low(jnp.transpose(update[...].astype(F32))), hidden[...])
    grad_first_t = dot(low(jnp.transpose(pushed[...].astype(F32))), atom_in[...])
    hold[:, :256] = small[...].astype(F32)
    hold[:, 256:512] = put_double(grad_first_t).astype(F32)
    hold[:, 512:1024] = put_double(grad_second_t).astype(F32)
    hold[:, 1024:1280] = grad_src
    hold[:, 1280:1536] = grad_dst
    pieces, _, width = out_ref.shape
    for g in range(pieces):
        out_ref[g ^ me[1]] = low(hold[:, g * width : (g + 1) * width])


def turned(value_ref, out_ref):
    out_ref[...] = jnp.transpose(value_ref[...]).astype(out_ref.dtype)


def block_backward(near, far, grad_in, *refs):
    mid, tri_refs, edge_ref, quad_refs = refs[0], refs[1:6], refs[6], refs[7:12]
    up_tri, up_quad, down_tri, down_quad, radial_t = refs[12:17]
    radial_basis, tri_basis, quad_basis, tri_in, tri_out, quad_in, quad_out = refs[17:24]
    dst_row, small_ref = refs[24], refs[25]
    gain_t = low(near[...].astype(F32) + far[...].astype(F32))
    atoms = gain_t.shape[1]
    step = min(512, atoms)
    grad_message = None
    for start in range(0, atoms, step):
        part = dot(gain_t[:, start : start + step], onehot(step, dst_row[...], start))
        grad_message = part if grad_message is None else grad_message + part
    grad_message = grad_message * edge_scale
    radial = dot(radial_t[...], radial_basis[...])
    grad_mid = grad_in[...] + grad_message * radial
    grad_radial = low(grad_message * mid[...].astype(F32))
    small = put_wide(dot_nt(grad_radial, radial_basis[...]), OFF_RADIAL)
    total = grad_mid
    for kept, basis, inner, outer, up, down in (
        (tri_refs, tri_basis, tri_in, tri_out, up_tri, down_tri),
        (quad_refs, quad_basis, quad_in, quad_out, up_quad, down_quad),
    ):
        value, more = pair_backward(grad_mid, edge_ref, basis, inner, outer, up[...], down[...], *kept)
        total = total + value
        small = small + more
    small_ref[...] = jnp.broadcast_to(low(small), small_ref.shape)
    send(small_ref)
    return total


BACK = 28


def back_last(*refs):
    refs[-1][...] = block_backward(*refs[:-1])


def back_middle(me, *refs):
    back, refs = refs[:BACK], refs[BACK:]
    big, first, second, src_row, slope_edge, free_ref, slope_atom, held = refs[:8]
    small_ref, gain_ref, update_ref, pushed_ref, grad_pre_ref, grad_ref, high_ref, low_ref, grad_atoms = refs[8:]
    grad = block_backward(*back, small_ref)
    grad_ref[...] = grad
    grad_pre = low(grad * slope_edge[...].astype(F32))
    grad_pre_ref[...] = grad_pre
    send(grad_ref, grad_pre_ref)
    grad_atoms[...] = held[...]
    edge_tables(
        grad_pre, big, first, second, src_row, back[-1], free_ref[...].astype(F32),
        slope_atom[...].astype(F32), grad_atoms, gain_ref, update_ref, pushed_ref,
    )
    half, count, _ = low_ref.shape
    for k in range(half):
        for ref, step in ((low_ref, k), (high_ref, half + k)):
            rows = pl.ds(pl.multiple_of((me[0] ^ step) * count, count), count)
            ref[k] = low(grad_atoms[rows])


def total_of(arrived):
    total = arrived[0].astype(F32)
    for s in range(1, arrived.shape[0]):
        total = total + arrived[s].astype(F32)
    return total


def sum_parts(arrived, out_ref):
    out_ref[...] = low(total_of(arrived))


def sum_pieces(*refs):
    *pieces, out_ref = refs
    count = len(pieces) // 2
    width = pieces[0].shape[1]
    for side in range(2):
        total = pieces[side * count][...].astype(F32)
        for piece in pieces[side * count + 1 : (side + 1) * count]:
            total = total + piece[...].astype(F32)
        out_ref[:, side * width : (side + 1) * width] = low(total)


def adam(me, last, weights, first, second, *refs):
    *pieces, grad_ref, weights_ref, first_ref, second_ref, low_ref, hold = refs
    width = pieces[0].shape[1] // 2
    for k, piece in enumerate(pieces):
        hold[me[1] ^ k] = piece[...].astype(F32)
    two, one = [
        jnp.concatenate([hold[g, :, side * width : (side + 1) * width] for g in range(len(pieces))], axis=1)
        for side in range(2)
    ]
    grad = jnp.concatenate(
        [total_of(last)[:, :SMALL], one[:, PAD:], one[:, :SMALL], two[:, PAD:]], axis=1
    )
    grad_ref[...] = grad
    old = weights[...]
    new_first = beta_one * first[...] + (1.0 - beta_one) * grad
    new_second = beta_two * second[...] + (1.0 - beta_two) * grad * grad
    first_ref[...] = new_first
    second_ref[...] = new_second
    first_hat = new_first / (1.0 - beta_one**adam_step)
    second_hat = new_second / (1.0 - beta_two**adam_step)
    new = old - learn_rate * (first_hat / (jnp.sqrt(second_hat) + epsilon) + decay_rate * old)
    weights_ref[...] = new
    low_ref[...] = low(new)


def exchange(pieces):
    return lax.all_to_all(pieces, "shard", split_axis=0, concat_axis=0)


def sum_pair(table, owners):
    rounds = []
    step = 1
    while step < owners:
        rounds.append([step])
        step = 2 * step
    if len(rounds) > 2:
        rounds = [[1, 2, 3]] + rounds[2:]
    for steps in rounds[:-1]:
        total = table.astype(F32)
        for k in steps:
            total = total + moved(table, k, owners).astype(F32)
        table = total.astype(BF16)
    return table, moved(table, rounds[-1][0], owners)


def moved(table, step, owners, axis="shard"):
    return lax.ppermute(table, axis, [(i, i ^ step) for i in range(owners)])


def per_device(
    edge_state, atom_state, radial_basis, triplet_basis, quad_basis, dst_owner, dst_local, src_owner,
    src_local, triplet_in, triplet_out, quad_in, quad_out, fixed_atoms, edge_cotangent,
    atom_cotangent, weights, first_moment, second_moment,
):
    owners = lax.axis_size("shard")
    groups = lax.axis_size("group")
    edges = edge_state.shape[0]
    count = atom_state.shape[0]
    atoms = count * owners
    items = triplet_in.shape[0]
    me = jnp.stack([lax.axis_index("shard"), lax.axis_index("group")]).astype(jnp.int32)
    weights_t = jnp.transpose(weights)
    cols = weights_t.shape[0]
    lanes = (BIG + PAD) // groups
    [pack] = call(pack_first, [sds((owners, ROWS, PAD), BF16)], [weights_t], flops=10**7)
    pack = exchange(pack)
    [cargo] = call(
        pack_cargo,
        [sds((1, count + ROWS * (1 + 2 * slots(lanes)), D_ATOM), BF16)],
        [me, weights_t, atom_state, fixed_atoms.reshape(1, count)],
        flops=10**7,
        smem=1,
        scratch=[(groups, cols, lanes)],
    )
    cargo = [cargo]
    step = owners // 2
    while step:
        cargo.append(moved(cargo[0] if len(cargo) == 1 else jnp.concatenate(cargo, axis=0), step, owners))
        step = step // 2
    lanes_shape = sds((D_EDGE, lanes), BF16)
    wide, big_two = call(collect, [lanes_shape, lanes_shape], [me] + cargo, flops=10**7, smem=1)
    dst_row = (dst_owner[:, 0] * count + dst_local).reshape(1, edges)
    src_row = (src_owner[:, 0] * count + src_local).reshape(1, edges)
    graph = [
        jnp.transpose(radial_basis),
        jnp.transpose(triplet_basis),
        jnp.transpose(quad_basis),
        triplet_in.reshape(1, items),
        triplet_out.reshape(1, items),
        quad_in.reshape(1, items),
        quad_out.reshape(1, items),
    ]
    kept = kept_shapes(edges, items)
    table_shape = sds((atoms, D_EDGE), BF16)
    edge_shape = sds((D_EDGE, edges), BF16)
    edge_wide = sds((D_EDGE, edges), F32)
    atom_shape = sds((atoms, D_ATOM), BF16)
    atom_wide = sds((atoms, D_ATOM), F32)
    gain_shape = sds((D_EDGE, atoms), BF16)
    *kept_one, table = call(
        first_half,
        kept + [table_shape],
        [edge_state, pack] + graph + [dst_row],
        flops=8 * 10**9,
        kept=range(KEPT),
    )
    near, far = sum_pair(table, owners)

    def everywhere(piece):
        return [piece] + [moved(piece, k, groups, "group") for k in range(1, groups)]

    prepared = list(
        call(
            prepare_one,
            [sds(s, BF16) for s in PREPARED],
            [me, pack] + everywhere(wide),
            flops=10**9,
            smem=1,
            scratch=[(groups, D_EDGE, lanes)],
        )
    )
    back_one, small_two, back_two = prepared[:5], prepared[5:12], prepared[12:16] + [prepared[11]]
    first_one, second_one, big_one = prepared[16:]
    (
        atom_in_one, hidden_one, slope_one, state_one, sent_one, free, slope_edge_one, *kept_two, table,
    ) = call(
        middle_half,
        [table_shape, atom_shape, atom_shape, atom_wide, atom_shape, atom_shape, edge_shape]
        + kept
        + [table_shape],
        [me, near, far, big_one, first_one, second_one, kept_one[0]]
        + small_two
        + graph
        + [src_row, dst_row]
        + cargo,
        flops=10 * 10**9,
        late=[6],
        kept=range(7 + KEPT),
        smem=1,
        scratch=[(atoms, D_ATOM)],
    )
    near, far = sum_pair(table, owners)
    first_two, second_two, big_two = call(
        prepare_two,
        [sds(s, BF16) for s in LARGE_SHAPES],
        [me] + everywhere(big_two),
        flops=10**9,
        smem=1,
        scratch=[(groups, D_EDGE, lanes)],
    )
    (
        atom_in_two, hidden_two, sent_two, edge_out_t, atom_out, grad_t, grad_pre, grad_atoms, gain, update,
        pushed,
    ) = call(
        turn,
        [table_shape, atom_shape, atom_shape, edge_wide, sds((count, D_ATOM), BF16), edge_wide, edge_shape,
         atom_wide, gain_shape, atom_shape, atom_shape],
        [me, near, far, big_two, first_two, second_two, src_row, dst_row, edge_cotangent,
         atom_cotangent, state_one, free, kept_two[0]],
        flops=2 * 10**9,
        late=[10, 11, 12],
        kept=[0, 1, 2, 3, 4, 5, 6, 7, 9, 10],
        smem=1,
        scratch=[(atoms, D_ATOM)],
    )

    def rows_first(value_t, dtype):
        return call(turned, [sds((edges, D_EDGE), dtype)], [value_t], flops=10**8, late=[0])[0]

    def large(update, pushed, atom_in, hidden, sent, grad_pre, small):
        [pieces] = call(
            large_grads,
            [sds((groups, D_EDGE, (PAD + BIG) // groups), BF16)],
            [me, update, pushed, atom_in, hidden, sent, grad_pre, src_row, dst_row, small],
            flops=10**9,
            late=[1, 2, 3, 4, 5, 6],
            smem=1,
            scratch=[(D_EDGE, PAD + BIG)],
        )
        return pieces

    def traded(pieces):
        return [pieces[0]] + [moved(pieces[k], k, groups, "group") for k in range(1, groups)]

    near, far = sum_pair(gain, owners)
    edge_out = rows_first(edge_out_t, BF16)
    pieces_two = large(
        update, pushed, atom_in_two, hidden_two, sent_two, grad_pre, jnp.zeros((D_EDGE, PAD), BF16)
    )
    near, pieces_two = lax.optimization_barrier((near, pieces_two))
    pieces_two = traded(pieces_two)
    half = owners // 2
    half_shape = sds((half, count, D_ATOM), BF16)
    grad_small_two, gain, update, pushed, grad_pre, grad_t, high, lower = call(
        back_middle,
        [sds((D_EDGE, PAD), BF16), gain_shape, atom_shape, atom_shape, edge_shape, edge_wide, half_shape,
         half_shape],
        [me, near, far, grad_t]
        + kept_two[1:]
        + back_two
        + graph
        + [dst_row, big_one, first_one, second_one, src_row, slope_edge_one, free, slope_one, grad_atoms],
        flops=10 * 10**9,
        late=list(range(3, 3 + KEPT)) + list(range(BACK + 5, BACK + 9)),
        kept=[0, 2, 3, 4, 5, 6, 7],
        smem=1,
        scratch=[(atoms, D_ATOM)],
    )
    near, far = sum_pair(gain, owners)
    pieces_one = traded(
        large(update, pushed, atom_in_one, hidden_one, sent_one, grad_pre, grad_small_two)
    )
    width = pieces_one[0].shape[1]
    [spreads] = call(
        sum_pieces, [sds((D_EDGE, 2 * width), BF16)], pieces_two + pieces_one, flops=10**7
    )
    arrived = exchange(spreads.reshape(owners, cols, 2 * width))
    [owned] = call(sum_parts, [sds((cols, 2 * width), BF16)], [arrived], flops=10**7)
    owned = [owned] + [moved(owned, k, groups, "group") for k in range(1, groups)]
    near, far, high = lax.optimization_barrier((near, far, high))
    while half > 1:
        lower = (lower.astype(F32) + moved(high, half, owners).astype(F32)).astype(BF16)
        half = half // 2
        high, lower = lower[half:], lower[:half]
    grad_atom = lower[0].astype(F32) + moved(high[0], 1, owners).astype(F32)
    grad_small_one, grad_edge_t = call(
        back_last,
        [sds((groups, D_EDGE, PAD), BF16), edge_wide],
        [near, far, grad_t] + kept_one[1:] + back_one + graph + [dst_row],
        flops=10 * 10**9,
        late=range(2, 2 + KEPT),
        kept=[0, 1],
    )
    grad_edge = rows_first(grad_edge_t, F32)
    last = lax.all_to_all(
        grad_small_one.reshape(groups * owners, cols, PAD), ("group", "shard"), split_axis=0, concat_axis=0
    )
    rows = weights.shape[0]
    results = call(
        adam,
        [sds((cols, rows), F32)] * 4 + [sds((cols, rows), BF16)],
        [me, last, weights_t, jnp.transpose(first_moment), jnp.transpose(second_moment)] + owned,
        flops=10**8,
        smem=1,
        scratch=[(groups, cols, 2 * width)],
    )
    return (edge_out, atom_out, grad_edge, grad_atom) + tuple(jnp.transpose(r) for r in results)


def solution(mesh):
    both = P(("group", "shard"), None)
    line = P(("group", "shard"))
    flat = P(None, "shard")
    in_specs = (both,) * 6 + (line, both) + (line,) * 6 + (both, both) + (flat,) * 3
    out_specs = (both,) * 4 + (flat,) * 5
    return jax.shard_map(
        per_device, mesh=mesh, in_specs=in_specs, out_specs=out_specs, check_vma=False
    )
```

```python
import jax
import jax.numpy as jnp
from jax import lax
from jax.experimental import pallas as pl
from jax.experimental.pallas import tpu as pltpu
from jax.sharding import PartitionSpec as P

D_EDGE = 128
D_ATOM = 256
D_TRI = 64
D_QUAD = 32
D_BASIS = 16
BLOCKS = 2
FOLD = 256
CHUNK = 1024
SMALL = 220
BIG = 1280
PAD = 256
ROWS = 16

edge_scale = 0.25
pair_scale = 0.5
beta_one = 0.5
beta_two = 0.5
learn_rate = 0.1
decay_rate = 0.01
epsilon = 1e-08
adam_step = 4

OFF_DOWN = {D_TRI: 0, D_QUAD: 136}
OFF_BASIS = {D_TRI: 64, D_QUAD: 168}
OFF_UP = {D_TRI: 72, D_QUAD: 172}
OFF_RADIAL = 204

F32 = jnp.float32
BF16 = jnp.bfloat16


def sds(shape, dtype):
    return jax.ShapeDtypeStruct(shape, dtype)


class Late:
    def __init__(self, source, ref, sem):
        self.ref, self.copy = ref, pltpu.make_async_copy(source, ref, sem)
        self.shape, self.begun, self.here = ref.shape, False, False

    def start(self):
        if not self.begun:
            self.copy.start()
            self.begun = True

    def wait(self):
        if not self.here:
            self.start()
            self.copy.wait()
            self.here = True

    def __getitem__(self, index):
        self.wait()
        return self.ref[index]


class Kept:
    def __init__(self, target, ref, sem):
        self.ref, self.copy, self.sent = ref, pltpu.make_async_copy(ref, target, sem), False
        self.shape, self.dtype = ref.shape, ref.dtype

    def __getitem__(self, index):
        return self.ref[index]

    def __setitem__(self, index, value):
        self.ref[index] = value

    def send(self):
        if not self.sent:
            self.copy.start()
            self.sent = True


def begin(*refs):
    for ref in refs:
        if isinstance(ref, Late):
            ref.start()


def arrive(*refs):
    for ref in refs:
        if isinstance(ref, Late):
            ref.wait()


def send(*refs):
    for ref in refs:
        if isinstance(ref, Kept):
            ref.send()


def call(body, outs, args, flops=10**9, late=(), kept=(), smem=0, scratch=(), early=None, alias=None):
    alias = alias or {}
    held = [i for i in kept if i not in alias.values()]
    moved = [args[i] for i in late] + [outs[i] for i in held]

    def kernel(*refs):
        refs = list(refs)
        ins, rest = refs[: len(args)], refs[len(args) :]
        results, rest = rest[: len(outs)], rest[len(outs) :]
        extra, rest = rest[: len(scratch)], rest[len(scratch) :]
        buffers, sems = rest[: len(moved)], rest[len(moved) :]
        for k, i in enumerate(late):
            ins[i] = Late(ins[i], buffers[k], sems[k])
        begin(*[ins[i] for i in (late if early is None else early)])
        for k, i in enumerate(held, len(late)):
            results[i] = Kept(results[i], buffers[k], sems[k])
        body(*ins, *results, *extra)
        for i in late:
            ins[i].wait()
        for i in held:
            results[i].send()
        for i in held:
            results[i].copy.wait()

    args = [pltpu.with_memory_space_constraint(x, pltpu.HBM) if i in late or i in alias else x for i, x in enumerate(args)]
    outs = [pltpu.HBM(x.shape, x.dtype) if i in kept else x for i, x in enumerate(outs)]
    space = [pltpu.SMEM] * smem + [pltpu.VMEM] * (len(args) - smem)
    for i in [*late, *alias]:
        space[i] = pltpu.HBM
    return pl.pallas_call(
        kernel,
        out_shape=outs,
        in_specs=[pl.BlockSpec(memory_space=s) for s in space],
        out_specs=[
            pl.BlockSpec(memory_space=pltpu.HBM if i in kept else pltpu.VMEM)
            for i in range(len(outs))
        ],
        scratch_shapes=[pltpu.VMEM(x, F32) if isinstance(x, tuple) else x for x in scratch]
        + [pltpu.VMEM(m.shape, m.dtype) for m in moved]
        + [pltpu.SemaphoreType.DMA] * len(moved),
        input_output_aliases=alias,
        compiler_params=pltpu.CompilerParams(vmem_limit_bytes=24 * 2**20),
        cost_estimate=pl.CostEstimate(flops=flops, bytes_accessed=2**20, transcendentals=0),
        name=body.__name__,
    )(*args)


def fetch(arrays):
    count = len(arrays)

    def kernel(*refs):
        copies = [
            pltpu.make_async_copy(refs[i], refs[count + i], refs[2 * count + i]) for i in range(count)
        ]
        for copy in copies:
            copy.start()
        for copy in copies:
            copy.wait()

    results = pl.pallas_call(
        kernel,
        out_shape=[sds(x.shape, x.dtype) for x in arrays],
        in_specs=[pl.BlockSpec(memory_space=pltpu.HBM)] * count,
        out_specs=[pl.BlockSpec(memory_space=pltpu.VMEM)] * count,
        scratch_shapes=[pltpu.SemaphoreType.DMA] * count,
        compiler_params=pltpu.CompilerParams(vmem_limit_bytes=2**20 * 20),
        cost_estimate=pl.CostEstimate(flops=10**9, bytes_accessed=2**20, transcendentals=0),
        name="fetch",
    )(*[pltpu.with_memory_space_constraint(x, pltpu.HBM) for x in arrays])
    return list(results)


def dot(a, b):
    return jnp.dot(a, b, preferred_element_type=F32)


def dot_nt(a, b):
    return lax.dot_general(a, b, (((1,), (1,)), ((), ())), preferred_element_type=F32)


def low(v):
    return v.astype(BF16)


def iota(shape, axis):
    return lax.broadcasted_iota(jnp.int32, shape, axis)


def ones_where(mask):
    return jnp.where(mask, 1.0, 0.0).astype(BF16)


def onehot(count, row, first=0):
    parts = []
    for start in range(0, count, 256):
        size = min(256, count - start)
        ids = iota((size, row.shape[1]), 0).astype(F32).astype(BF16)
        mask = ids == (row - (first + start)).astype(F32).astype(BF16)
        parts.append(jnp.where(mask, jnp.ones((), BF16), jnp.zeros((), BF16)))
    return parts[0] if len(parts) == 1 else jnp.concatenate(parts, axis=0)


def sigmoid(v):
    return 1.0 / (1.0 + jnp.exp(-v))


def silu_pair(v):
    s = sigmoid(v)
    return v * s, s * (1.0 + v * (1.0 - s))


def cut(value, width):
    count = FOLD // width
    length = value.shape[1] // count
    return jnp.concatenate([value[:, g * length : (g + 1) * length] for g in range(count)], axis=0)


def uncut(value, width):
    count = FOLD // width
    return jnp.concatenate([value[g * width : (g + 1) * width] for g in range(count)], axis=1)


def pick(folded, high, width):
    result = folded[:width]
    for g in range(1, FOLD // width):
        result = jnp.where(high == g, folded[g * width : (g + 1) * width], result)
    return result


def spread(value, high, width):
    value = low(value)
    high = high.astype(F32).astype(BF16)
    return jnp.concatenate(
        [jnp.where(high == g, value, jnp.zeros((), BF16)) for g in range(FOLD // width)], axis=0
    )


def high_low(index, length):
    return index // length, index % length


def small_t(raw, offset, width, columns):
    count = 128 // width
    total = None
    for p in range(count):
        lane, d = iota((PAD, columns), 0), iota((PAD, columns), 1)
        sel = ones_where((d % count == p) & (lane == offset + d // count))
        part = dot(raw[p * width : (p + 1) * width], sel)
        total = part if total is None else total + part
    return low(total)


def small_plain(raw, offset, width, rows):
    count = 128 // width
    total = None
    for p in range(count):
        d, lane = iota((rows, PAD), 0), iota((rows, PAD), 1)
        sel = ones_where((d % count == p) & (lane == offset + d // count))
        part = dot_nt(sel, raw[p * width : (p + 1) * width])
        total = part if total is None else total + part
    return low(total)


def wide_t(raw, offset, rows):
    lane, d = iota((PAD, rows), 0), iota((PAD, rows), 1)
    return low(dot(raw, ones_where(lane == offset + d)))


def wide_plain(raw, offset, rows):
    d, lane = iota((rows, PAD), 0), iota((rows, PAD), 1)
    return low(dot_nt(ones_where(lane == offset + d), raw))


def double_plain(raw, rows):
    d, lane = iota((rows, 2 * rows), 0), iota((rows, 2 * rows), 1)
    return jnp.concatenate(
        [low(dot_nt(ones_where(lane == 2 * d + p), raw)) for p in range(2)], axis=1
    )


def put_small(grad_t, offset, width):
    count = 128 // width
    columns = grad_t.shape[1]
    value = low(grad_t)
    parts = []
    for p in range(count):
        d, lane = iota((columns, PAD), 0), iota((columns, PAD), 1)
        sel = ones_where((d % count == p) & (lane == offset + d // count))
        parts.append(dot(value, sel))
    return jnp.concatenate(parts, axis=0)


def put_wide(grad_t, offset):
    columns = grad_t.shape[1]
    d, lane = iota((columns, PAD), 0), iota((columns, PAD), 1)
    return dot(low(grad_t), ones_where(lane == offset + d))


def put_double(grad_t):
    rows = grad_t.shape[1]
    d, lane = iota((rows, 2 * rows), 0), iota((rows, 2 * rows), 1)
    value = low(grad_t)
    return low(
        dot(value[:128], ones_where(lane == 2 * d)) + dot(value[128:], ones_where(lane == 2 * d + 1))
    )


def small_matrices(raw):
    return (
        [small_t(raw, OFF_DOWN[w], w, D_EDGE) for w in (D_TRI, D_QUAD)]
        + [small_t(raw, OFF_BASIS[w], w, D_BASIS) for w in (D_TRI, D_QUAD)]
        + [wide_t(raw, OFF_UP[w], w) for w in (D_TRI, D_QUAD)]
        + [wide_t(raw, OFF_RADIAL, D_BASIS)]
    )


def back_matrices(raw):
    return [wide_plain(raw, OFF_UP[w], w) for w in (D_TRI, D_QUAD)] + [
        small_plain(raw, OFF_DOWN[w], w, D_EDGE) for w in (D_TRI, D_QUAD)
    ]


SMALL_SHAPES = [
    (D_TRI, D_EDGE), (D_QUAD, D_EDGE), (D_TRI, D_BASIS), (D_QUAD, D_BASIS), (D_EDGE, D_TRI),
    (D_EDGE, D_QUAD), (D_EDGE, D_BASIS),
]
BACK_SHAPES = [(D_TRI, D_EDGE), (D_QUAD, D_EDGE), (D_EDGE, D_TRI), (D_EDGE, D_QUAD)]


def slots(width):
    return -(-width // PAD)


def padded(value, rows, lanes):
    have, wide = value.shape
    if wide < lanes:
        value = jnp.concatenate([value, jnp.zeros((have, lanes - wide), value.dtype)], axis=1)
    if have < rows:
        value = jnp.concatenate([value, jnp.zeros((rows - have, lanes), value.dtype)], axis=0)
    return value


def pack_first(weights, out_ref):
    head = low(padded(weights[:, :SMALL], ROWS, PAD))
    for s in range(out_ref.shape[0]):
        out_ref[s] = head


def pack_cargo(me, weights, state, fixed, out_ref, hold):
    count = state.shape[0]
    free = (1 - fixed[...]).astype(F32)
    out_ref[0, :count] = state[...]
    out_ref[0, count : count + ROWS] = low(padded(free, ROWS, PAD))
    values = weights[...]
    half = SMALL + BIG
    gap = jnp.zeros((values.shape[0], PAD - SMALL), F32)
    one = jnp.concatenate([values[:, SMALL : half + SMALL], gap], axis=1)
    two = padded(values[:, half + SMALL :], values.shape[0], BIG + PAD)
    groups, _, width = hold.shape
    base = count + ROWS
    for side in (one, two):
        for g in range(groups):
            hold[g] = side[:, g * width : (g + 1) * width]
        mine = padded(hold[me[1]], ROWS, slots(width) * PAD)
        for k in range(slots(width)):
            out_ref[0, base : base + ROWS] = low(mine[:, k * PAD : (k + 1) * PAD])
            base = base + ROWS


def order_of(owners):
    order = [0]
    for steps in gather_rounds(owners):
        order = order + [k ^ step for step in steps for k in order]
    return order


def gather_rounds(owners):
    rounds, step = [], owners // 2
    while step > 2:
        rounds.append([step])
        step = step // 2
    return rounds + ([[1, 2, 3]] if owners > 2 else [[1]])


def scatter_order(owners):
    order, step = [0], owners // 2
    while step > 2:
        order = order + [k ^ step for k in order]
        step = step // 2
    return [k ^ low_bits for low_bits in range(4) for k in order]


def collect(me, *refs):
    *cargo, one_ref, two_ref = refs
    rows = cargo[0].shape[1]
    owners = sum(c.shape[0] for c in cargo)
    full, width = one_ref.shape
    cols = full // owners
    count = slots(width)
    base = rows - 2 * count * ROWS
    order = order_of(owners)
    shape = (full, owners * ROWS)
    row, col = iota(shape, 0), iota(shape, 1)
    owner, inside = row // cols, row % cols
    sel = None
    for position, k in enumerate(order):
        hit = (col == position * ROWS + inside) & (owner == (me[0] ^ k))
        sel = hit if sel is None else sel | hit
    sel = ones_where(sel)
    for side, ref in ((0, one_ref), (1, two_ref)):
        for k in range(count):
            start = base + (side * count + k) * ROWS
            values = jnp.concatenate(
                [c[i, start : start + ROWS] for c in cargo for i in range(c.shape[0])], axis=0
            )
            lanes = min(PAD, width - k * PAD)
            ref[:, k * PAD : k * PAD + lanes] = low(dot(sel, values))[:, :lanes]


def joined(me, pieces, hold):
    for k, piece in enumerate(pieces):
        hold[me[1] ^ k] = piece[...].astype(F32)
    return low(jnp.concatenate([hold[g] for g in range(len(pieces))], axis=1))


def small_rows(pack, cols):
    owners = pack.shape[0]
    value = pack[...].reshape(owners * ROWS, PAD)
    if cols == ROWS:
        return value
    c, row = iota((owners * cols, owners * ROWS), 0), iota((owners * cols, owners * ROWS), 1)
    return low(dot(ones_where(row == c // cols * ROWS + c % cols), value))


def prepare_one(me, pack, *refs):
    *rest, hold = refs
    groups = hold.shape[0]
    wide = joined(me, rest[:groups], hold)
    raw_one = small_rows(pack, D_EDGE // pack.shape[0])
    raw_two = wide[:, BIG:]
    values = back_matrices(raw_one) + [wide_t(raw_one, OFF_RADIAL, D_BASIS)]
    values = values + small_matrices(raw_two) + back_matrices(raw_two)
    values = values + [double_plain(wide[:, :256], D_EDGE), double_plain(wide[:, 256:768], D_ATOM)]
    for ref, value in zip(rest[groups:], values + [wide[:, :BIG]]):
        ref[...] = value


def prepare_two(me, *refs):
    *rest, hold = refs
    groups = hold.shape[0]
    big = joined(me, rest[:groups], hold)
    first_ref, second_ref, big_ref = rest[groups:]
    first_ref[...] = double_plain(big[:, :256], D_EDGE)
    second_ref[...] = double_plain(big[:, 256:768], D_ATOM)
    big_ref[...] = big[:, :BIG]


LARGE_SHAPES = [(D_EDGE, D_ATOM), (D_ATOM, D_ATOM), (D_EDGE, BIG)]
PREPARED = BACK_SHAPES + [(D_EDGE, D_BASIS)] + SMALL_SHAPES + BACK_SHAPES + LARGE_SHAPES


def pair_forward(edge_t, basis_ref, in_ref, out_ref, down_t, basis_t, up_t, xg_ref, bt_ref):
    width, edges = down_t.shape[0], edge_t.shape[1]
    length = edges * width // FOLD
    act, slope_in = silu_pair(dot(down_t, edge_t))
    table = cut(low(act), width)
    total = jnp.zeros((FOLD, length), F32)
    items = in_ref.shape[1]
    chunk = min(CHUNK, items)
    for start in range(0, items, chunk):
        cols = slice(start, start + chunk)
        in_high, in_low = high_low(in_ref[:, cols], length)
        out_high, out_low = high_low(out_ref[:, cols], length)
        xg = pick(dot(table, onehot(length, in_low)), in_high, width)
        bt = dot(basis_t, basis_ref[:, cols])
        xg_ref[:, cols] = low(xg)
        bt_ref[:, cols] = low(bt)
        total = total + dot_nt(spread(xg * bt, out_high, width), onehot(length, out_low))
    send(xg_ref, bt_ref)
    agg_t = low(uncut(total, width) * pair_scale)
    value, slope_out = silu_pair(dot(up_t, agg_t))
    return value, slope_in, agg_t, slope_out


def pair_backward(
    grad_mid, edge_t, basis_ref, in_ref, out_ref, up, down, slope_out, agg_t, xg_ref, bt_ref, slope_in,
    following,
):
    width, edges = up.shape[0], slope_in.shape[1]
    length = edges * width // FOLD
    grad_out = low(grad_mid * slope_out[...].astype(F32))
    grad_up_t = dot_nt(grad_out, agg_t[...])
    table = cut(low(dot(up, grad_out) * pair_scale), width)
    begin(xg_ref, bt_ref)
    arrive(xg_ref, bt_ref)
    begin(*following)
    total = jnp.zeros((FOLD, length), F32)
    grad_basis_t = jnp.zeros((width, D_BASIS), F32)
    items = in_ref.shape[1]
    chunk = min(CHUNK, items)
    for start in range(0, items, chunk):
        cols = slice(start, start + chunk)
        in_high, in_low = high_low(in_ref[:, cols], length)
        out_high, out_low = high_low(out_ref[:, cols], length)
        gy = pick(dot(table, onehot(length, out_low)), out_high, width)
        grad_bt = low(gy * xg_ref[:, cols].astype(F32))
        grad_basis_t = grad_basis_t + dot_nt(grad_bt, basis_ref[:, cols])
        moved = gy * bt_ref[:, cols].astype(F32)
        total = total + dot_nt(spread(moved, in_high, width), onehot(length, in_low))
    grad_in = low(uncut(total, width) * slope_in[...].astype(F32))
    grad_down_t = dot_nt(grad_in, edge_t[...])
    small = (
        put_small(grad_down_t, OFF_DOWN[width], width)
        + put_small(grad_basis_t, OFF_BASIS[width], width)
        + put_wide(grad_up_t, OFF_UP[width])
    )
    return dot(down, grad_in), small


def block_forward(state_t, matrices, graph, dst_row, out_refs):
    radial_basis, tri_basis, quad_basis, tri_in, tri_out, quad_in, quad_out = graph
    down_tri, down_quad, basis_tri, basis_quad, up_tri, up_quad, radial_t = matrices
    mid_ref, mid_low_ref = out_refs[:2]
    tri_refs, edge_ref, quad_refs, table_ref = out_refs[2:7], out_refs[7], out_refs[8:13], out_refs[13]
    edge_t = low(state_t)
    edge_ref[...] = edge_t
    send(edge_ref)
    mid = state_t
    for refs, basis, inner, outer, down, basis_t, up in (
        (tri_refs, tri_basis, tri_in, tri_out, down_tri, basis_tri, up_tri),
        (quad_refs, quad_basis, quad_in, quad_out, down_quad, basis_quad, up_quad),
    ):
        slope_out_ref, agg_ref, xg_ref, bt_ref, slope_in_ref = refs
        value, slope_in, agg, slope_out = pair_forward(
            edge_t, basis, inner, outer, down, basis_t, up, xg_ref, bt_ref
        )
        slope_in_ref[...] = low(slope_in)
        agg_ref[...] = agg
        slope_out_ref[...] = low(slope_out)
        send(slope_in_ref, agg_ref, slope_out_ref)
        mid = mid + value
    mid_ref[...] = mid
    mid_low_ref[...] = low(mid)
    send(mid_ref, mid_low_ref)
    message = low(mid * dot(radial_t, radial_basis[...]))
    atoms = table_ref.shape[0]
    step = min(512, atoms)
    for start in range(0, atoms, step):
        rows = slice(start, start + step)
        table_ref[rows] = low(dot_nt(onehot(step, dst_row[...], start), message))


def kept_shapes(edges, items):
    edge = ((D_EDGE, edges), BF16)
    tri, quad = [
        [edge, ((w, edges), BF16), ((w, items), BF16), ((w, items), BF16), ((w, edges), BF16)]
        for w in (D_TRI, D_QUAD)
    ]
    return [sds(*x) for x in [((D_EDGE, edges), F32), edge] + tri + [edge] + quad]


KEPT = 13


def first_half(edge_state, pack, *refs):
    graph, dst_row, out_refs = refs[:7], refs[7], refs[8:]
    eye = ones_where(iota((D_EDGE, D_EDGE), 0) == iota((D_EDGE, D_EDGE), 1))
    state_t = dot_nt(eye, edge_state[...])
    raw = small_rows(pack, D_EDGE // pack.shape[0])
    block_forward(state_t, small_matrices(raw), graph, dst_row, out_refs)


def atom_forward(near, far, state, free, first, second):
    atom_in = low((near[...].astype(F32) + far[...].astype(F32)) * edge_scale)
    act, slope = silu_pair(dot(atom_in, first[...]))
    hidden = low(act)
    new_state = state + free * dot(hidden, second[...])
    return atom_in, hidden, slope, new_state


def edge_pre(sent, big, src_row, dst_row):
    src_t = low(dot_nt(big[:, 768:1024], sent))
    dst_t = low(dot_nt(big[:, 1024:1280], sent))
    atoms = sent.shape[0]
    step = min(512, atoms)
    total = None
    for start in range(0, atoms, step):
        part = dot(src_t[:, start : start + step], onehot(step, src_row[...], start))
        part = part + dot(dst_t[:, start : start + step], onehot(step, dst_row[...], start))
        total = part if total is None else total + part
    return total


def middle_half(me, near, far, big, first, second, mid_in, *refs):
    matrices, graph, src_row, dst_row = refs[:7], refs[7:14], refs[14], refs[15]
    atoms = near.shape[0]
    cargo, refs = refs[16:], None
    split = 0
    owners = 0
    while len(cargo[split].shape) == 3:
        owners = owners + cargo[split].shape[0]
        split = split + 1
    cargo, rest = cargo[:split], cargo[split:]
    atom_in_ref, hidden_ref, slope_atom_ref, state_ref, sent_ref, free_ref, slope_edge_ref = rest[:7]
    *out_refs, free_wide = rest[7:]
    count = atoms // owners
    eye = iota((count, count), 0) == iota((count, count), 1)
    order = order_of(owners)
    position = 0
    for pieces in cargo:
        for i in range(pieces.shape[0]):
            rows = pl.ds(pl.multiple_of((me[0] ^ order[position]) * count, count), count)
            state_ref.ref[rows] = pieces[i, :count].astype(F32)
            flag = pieces[i, count : count + 1, :count].astype(F32)
            column = jnp.sum(jnp.where(eye, flag, 0.0), axis=1, keepdims=True)
            free_wide[rows] = jnp.broadcast_to(column, (count, D_ATOM))
            position = position + 1
    free_ref[...] = low(free_wide[...])
    send(free_ref)
    atom_in, hidden, slope, state = atom_forward(
        near, far, state_ref[...], free_wide[...], first, second
    )
    atom_in_ref[...] = atom_in
    hidden_ref[...] = hidden
    slope_atom_ref[...] = low(slope)
    state_ref[...] = state
    sent = low(state)
    sent_ref[...] = sent
    send(atom_in_ref, hidden_ref, slope_atom_ref, state_ref, sent_ref)
    act, slope_edge = silu_pair(edge_pre(sent, big, src_row, dst_row))
    slope_edge_ref[...] = low(slope_edge)
    send(slope_edge_ref)
    block_forward(mid_in[...] + act, [m[...] for m in matrices], graph, dst_row, out_refs)


def edge_tables(
    grad_pre, big, first, second, src_row, dst_row, free, slope_atom, grad_atoms, gain_ref, update_ref,
    pushed_ref,
):
    atoms = free.shape[0]
    step = min(512, atoms)
    src_t, dst_t = big[:, 768:1024], big[:, 1024:1280]
    for start in range(0, atoms, step):
        rows = slice(start, start + step)
        pick_src = onehot(step, src_row[...], start)
        pick_dst = onehot(step, dst_row[...], start)
        part = dot(low(dot_nt(pick_src, grad_pre)), src_t) + dot(low(dot_nt(pick_dst, grad_pre)), dst_t)
        grad_atoms[rows] = grad_atoms[rows] + part
    update = low(grad_atoms[...] * free)
    update_ref[...] = update
    send(update_ref)
    pushed = low(dot_nt(update, second[...]) * slope_atom)
    pushed_ref[...] = pushed
    send(pushed_ref)
    gain_ref[...] = low(dot_nt(first[...], pushed))


def turn(
    me, near, far, big, first, second, src_row, dst_row, edge_cotangent, own, state_in, free_ref, mid_in,
    atom_in_ref, hidden_ref, sent_ref, edge_ref, atom_out_ref, cotangent_ref, grad_pre_ref, atoms_ref,
    gain_ref, update_ref, pushed_ref, hold,
):
    free = free_ref[...].astype(F32)
    begin(mid_in)
    atom_in, hidden, slope, state = atom_forward(near, far, state_in[...], free, first, second)
    atom_in_ref[...] = atom_in
    hidden_ref[...] = hidden
    sent = low(state)
    sent_ref[...] = sent
    send(atom_in_ref, hidden_ref, sent_ref)
    hold[...] = state
    count = atom_out_ref.shape[0]
    mine = pl.ds(pl.multiple_of(me[0] * count, count), count)
    atom_out_ref[...] = low(hold[mine])
    act, slope_edge = silu_pair(edge_pre(sent, big, src_row, dst_row))
    edge_ref[...] = mid_in[...] + act
    send(edge_ref, atom_out_ref)
    eye = ones_where(iota((D_EDGE, D_EDGE), 0) == iota((D_EDGE, D_EDGE), 1))
    cotangent = dot_nt(eye, edge_cotangent[...])
    cotangent_ref[...] = cotangent
    grad_pre = low(cotangent * slope_edge)
    grad_pre_ref[...] = grad_pre
    send(cotangent_ref, grad_pre_ref)
    atoms_ref[...] = jnp.zeros(atoms_ref.shape, F32)
    atoms_ref.ref[mine] = own[...].astype(F32)
    edge_tables(
        grad_pre, big, first, second, src_row, dst_row, free, slope, atoms_ref, gain_ref, update_ref,
        pushed_ref,
    )


def large_grads(update, pushed, grad_pre, src_row, dst_row, atom_in, hidden, sent, *refs):
    *small, out_ref = refs
    base = 2 * PAD * len(small)
    for ref in small:
        out_ref[:, PAD : 2 * PAD] = ref[...]
    for lanes, value in large_values(update, pushed, grad_pre, src_row, dst_row, atom_in, hidden, sent):
        out_ref[:, base + lanes.start : base + lanes.stop] = value
    send(out_ref)


def large_values(update, pushed, grad_pre, src_row, dst_row, atom_in, hidden, sent):
    atoms = sent.shape[0]
    step = min(512, atoms)
    grads = grad_pre[...]
    update_t = low(jnp.transpose(update[...].astype(F32)))
    pushed_t = low(jnp.transpose(pushed[...].astype(F32)))
    grad_src = jnp.zeros((D_EDGE, D_ATOM), F32)
    grad_dst = jnp.zeros((D_EDGE, D_ATOM), F32)
    for start in range(0, atoms, step):
        rows = slice(start, start + step)
        sums = [low(dot_nt(grads, onehot(step, row[...], start))) for row in (src_row, dst_row)]
        grad_src = grad_src + dot(sums[0], sent[rows])
        grad_dst = grad_dst + dot(sums[1], sent[rows])
    grad_second_t = dot(update_t, hidden[...])
    grad_first_t = dot(pushed_t, atom_in[...])
    return [
        (slice(0, 256), put_double(grad_first_t)),
        (slice(256, 768), put_double(grad_second_t)),
        (slice(768, 1024), low(grad_src)),
        (slice(1024, 1280), low(grad_dst)),
    ]


def turned(value_ref, out_ref):
    out_ref[...] = jnp.transpose(value_ref[...]).astype(out_ref.dtype)


def block_backward(near, far, grad_in, *refs, more_refs=()):
    mid, tri_refs, edge_ref, quad_refs = refs[0], refs[1:6], refs[6], refs[7:12]
    up_tri, up_quad, down_tri, down_quad, radial_t = refs[12:17]
    radial_basis, tri_basis, quad_basis, tri_in, tri_out, quad_in, quad_out = refs[17:24]
    dst_row = refs[24]
    gain_t = low(near[...].astype(F32) + far[...].astype(F32))
    atoms = gain_t.shape[1]
    step = min(512, atoms)
    grad_message = None
    for start in range(0, atoms, step):
        part = dot(gain_t[:, start : start + step], onehot(step, dst_row[...], start))
        grad_message = part if grad_message is None else grad_message + part
    grad_message = grad_message * edge_scale
    radial = dot(radial_t[...], radial_basis[...])
    grad_mid = grad_in[...] + grad_message * radial
    grad_radial = low(grad_message * mid[...].astype(F32))
    begin(*tri_refs[2:], edge_ref)
    small = put_wide(dot_nt(grad_radial, radial_basis[...]), OFF_RADIAL)
    total = grad_mid
    for kept, basis, inner, outer, up, down, following in (
        (tri_refs, tri_basis, tri_in, tri_out, up_tri, down_tri, quad_refs),
        (quad_refs, quad_basis, quad_in, quad_out, up_quad, down_quad, more_refs),
    ):
        value, more = pair_backward(
            grad_mid, edge_ref, basis, inner, outer, up[...], down[...], *kept, following
        )
        total = total + value
        small = small + more
    return total, low(small)


BACK = 28


def back_last(*refs):
    _, grad_ref, all_ref, hold, sem = refs[BACK:]
    grad, small = block_backward(*refs[:BACK])
    hold[...] = small
    copy = pltpu.make_async_copy(hold, all_ref.at[:, :PAD], sem)
    copy.start()
    grad_ref[...] = grad
    copy.wait()


def back_middle(me, *refs):
    back, refs = refs[:BACK], refs[BACK:]
    big, first, second, src_row, slope_edge, free_ref, slope_atom, held = refs[:8]
    small_ref, gain_ref, update_ref, pushed_ref, grad_pre_ref, grad_ref = refs[8:14]
    *parts, grad_atoms = refs[14:]
    grad, small = block_backward(*back, more_refs=(slope_edge, free_ref, slope_atom, held))
    small_ref[...] = small
    grad_ref[...] = grad
    grad_pre = low(grad * slope_edge[...].astype(F32))
    grad_pre_ref[...] = grad_pre
    send(grad_ref, grad_pre_ref)
    grad_atoms[...] = held[...]
    edge_tables(
        grad_pre, big, first, second, src_row, back[-1], free_ref[...].astype(F32),
        slope_atom[...].astype(F32), grad_atoms, gain_ref, update_ref, pushed_ref,
    )
    quarter, count, _ = parts[0].shape
    for k, step in enumerate(scatter_order(4 * quarter)):
        rows = pl.ds(pl.multiple_of((me[0] ^ step) * count, count), count)
        parts[k // quarter][k % quarter] = low(grad_atoms[rows])


def total_of(arrived):
    total = arrived[0].astype(F32)
    for s in range(1, arrived.shape[0]):
        total = total + arrived[s].astype(F32)
    return total


def sum_list(pieces):
    total = pieces[0][...].astype(F32)
    for piece in pieces[1:]:
        total = total + piece[...].astype(F32)
    return total


def sum_parts(one, two, out_ref):
    width = one.shape[2]
    out_ref[:, :width] = low(total_of(one))
    out_ref[:, width:] = low(total_of(two))


def adam(weights, first, second, *refs):
    *pieces, grad_ref, weights_ref, first_ref, second_ref, low_ref = refs
    total = sum_list(pieces)
    grad = jnp.concatenate(
        [
            total[:, :SMALL],
            total[:, 2 * PAD : 2 * PAD + BIG],
            total[:, PAD : PAD + SMALL],
            total[:, 2 * PAD + BIG :],
        ],
        axis=1,
    )
    grad_ref[...] = grad
    old = weights[...]
    new_first = beta_one * first[...] + (1.0 - beta_one) * grad
    new_second = beta_two * second[...] + (1.0 - beta_two) * grad * grad
    first_ref[...] = new_first
    second_ref[...] = new_second
    first_hat = new_first / (1.0 - beta_one**adam_step)
    second_hat = new_second / (1.0 - beta_two**adam_step)
    new = old - learn_rate * (first_hat / (jnp.sqrt(second_hat) + epsilon) + decay_rate * old)
    weights_ref[...] = new
    low_ref[...] = low(new)


def exchange(pieces):
    return lax.all_to_all(pieces, "shard", split_axis=0, concat_axis=0)


def sum_pair(table, owners, beside=None):
    rounds = []
    step = 1
    while step < owners:
        rounds.append([step])
        step = 2 * step
    if len(rounds) > 2:
        rounds = [[1, 2, 3]] + rounds[2:]
    for steps in rounds[:-1]:
        others = [moved(table, k, owners) for k in steps]
        if beside is not None:
            table, beside = lax.optimization_barrier((table, beside))
        total = table.astype(F32)
        for other in others:
            total = total + other.astype(F32)
        table = total.astype(BF16)
    return table, moved(table, rounds[-1][0], owners), beside


def moved(table, step, owners, axis="shard"):
    return lax.ppermute(table, axis, [(i, i ^ step) for i in range(owners)])


def per_device(
    edge_state, atom_state, radial_basis, triplet_basis, quad_basis, dst_owner, dst_local, src_owner,
    src_local, triplet_in, triplet_out, quad_in, quad_out, fixed_atoms, edge_cotangent,
    atom_cotangent, weights, first_moment, second_moment,
):
    owners = lax.axis_size("shard")
    groups = lax.axis_size("group")
    edges = edge_state.shape[0]
    count = atom_state.shape[0]
    atoms = count * owners
    items = triplet_in.shape[0]
    me = jnp.stack([lax.axis_index("shard"), lax.axis_index("group")]).astype(jnp.int32)
    weights_t = jnp.transpose(weights)
    cols = weights_t.shape[0]
    lanes = (BIG + PAD) // groups
    [pack] = call(pack_first, [sds((owners, ROWS, PAD), BF16)], [weights_t], flops=10**7, late=[0])
    pack, state = lax.optimization_barrier((pack, atom_state))
    pack = exchange(pack)
    [cargo] = call(
        pack_cargo,
        [sds((1, count + ROWS * (1 + 2 * slots(lanes)), D_ATOM), BF16)],
        [me, weights_t, state, fixed_atoms.reshape(1, count)],
        flops=10**7,
        late=[1, 2],
        smem=1,
        scratch=[(groups, cols, lanes)],
    )
    cargo = [cargo]
    for steps in gather_rounds(owners):
        held = cargo[0] if len(cargo) == 1 else jnp.concatenate(cargo, axis=0)
        cargo = cargo + [moved(held, step, owners) for step in steps]
    lanes_shape = sds((D_EDGE, lanes), BF16)
    wide, big_two = call(collect, [lanes_shape, lanes_shape], [me] + cargo, flops=10**7, smem=1)
    dst_row = (dst_owner[:, 0] * count + dst_local).reshape(1, edges)
    src_row = (src_owner[:, 0] * count + src_local).reshape(1, edges)
    graph = [
        jnp.transpose(radial_basis),
        jnp.transpose(triplet_basis),
        jnp.transpose(quad_basis),
        triplet_in.reshape(1, items),
        triplet_out.reshape(1, items),
        quad_in.reshape(1, items),
        quad_out.reshape(1, items),
    ]
    kept = kept_shapes(edges, items)
    table_shape = sds((atoms, D_EDGE), BF16)
    edge_shape = sds((D_EDGE, edges), BF16)
    edge_wide = sds((D_EDGE, edges), F32)
    atom_shape = sds((atoms, D_ATOM), BF16)
    atom_wide = sds((atoms, D_ATOM), F32)
    gain_shape = sds((D_EDGE, atoms), BF16)
    *kept_one, table = call(
        first_half,
        kept + [table_shape],
        [edge_state, pack] + graph + [dst_row],
        flops=8 * 10**9,
        kept=range(KEPT),
    )
    near, far, _ = sum_pair(table, owners)

    def everywhere(piece):
        return [piece] + [moved(piece, k, groups, "group") for k in range(1, groups)]

    prepared = list(
        call(
            prepare_one,
            [sds(s, BF16) for s in PREPARED],
            [me, pack] + everywhere(wide),
            flops=10**9,
            smem=1,
            scratch=[(groups, D_EDGE, lanes)],
        )
    )
    back_one, small_two, back_two = prepared[:5], prepared[5:12], prepared[12:16] + [prepared[11]]
    first_one, second_one, big_one = prepared[16:]
    (
        atom_in_one, hidden_one, slope_one, state_one, sent_one, free, slope_edge_one, *kept_two, table,
    ) = call(
        middle_half,
        [table_shape, atom_shape, atom_shape, atom_wide, atom_shape, atom_shape, edge_shape]
        + kept
        + [table_shape],
        [me, near, far, big_one, first_one, second_one, kept_one[0]]
        + small_two
        + graph
        + [src_row, dst_row]
        + cargo,
        flops=10 * 10**9,
        late=[6],
        kept=range(7 + KEPT),
        smem=1,
        scratch=[(atoms, D_ATOM)],
    )
    near, far, _ = sum_pair(table, owners)
    first_two, second_two, big_two = call(
        prepare_two,
        [sds(s, BF16) for s in LARGE_SHAPES],
        [me] + everywhere(big_two),
        flops=10**9,
        smem=1,
        scratch=[(groups, D_EDGE, lanes)],
    )
    (
        atom_in_two, hidden_two, sent_two, edge_out_t, atom_out, grad_t, grad_pre, grad_atoms, gain, update,
        pushed,
    ) = call(
        turn,
        [table_shape, atom_shape, atom_shape, edge_wide, sds((count, D_ATOM), BF16), edge_wide, edge_shape,
         atom_wide, gain_shape, atom_shape, atom_shape],
        [me, near, far, big_two, first_two, second_two, src_row, dst_row, edge_cotangent,
         atom_cotangent, state_one, free, kept_two[0]],
        flops=2 * 10**9,
        late=[10, 11, 12],
        early=[10, 11],
        kept=[4, 5, 7],
        smem=1,
        scratch=[(atoms, D_ATOM)],
    )

    def rows_first(value_t, dtype):
        return call(turned, [sds((edges, D_EDGE), dtype)], [value_t], flops=10**8)[0]

    near, far, grads_two = sum_pair(
        gain,
        owners,
        call(
            large_grads,
            [sds((D_EDGE, BIG), BF16)],
            [update, pushed, grad_pre, src_row, dst_row, atom_in_two, hidden_two, sent_two],
            flops=10**9,
        )[0],
    )
    arrived_two = exchange(grads_two.reshape(owners, cols, BIG))
    edge_out = rows_first(edge_out_t, BF16)
    near, edge_out = lax.optimization_barrier((near, edge_out))
    fetched = fetch([grad_t] + kept_two[1:] + [slope_edge_one, free, slope_one, grad_atoms])
    half = owners // 4
    grad_small_two, gain, update, pushed, grad_pre, grad_t, *parts = call(
        back_middle,
        [sds((D_EDGE, PAD), BF16), gain_shape, atom_shape, atom_shape, edge_shape, edge_wide,
         *[sds((half, count, D_ATOM), BF16)] * 4],
        [me, near, far]
        + fetched[:KEPT]
        + back_two
        + graph
        + [dst_row, big_one, first_one, second_one, src_row]
        + fetched[KEPT:],
        flops=10 * 10**9,
        kept=[5],
        smem=1,
        scratch=[(atoms, D_ATOM)],
    )
    [grads_one] = call(
        large_grads,
        [sds((D_EDGE, 2 * PAD + BIG), BF16)],
        [update, pushed, grad_pre, src_row, dst_row, atom_in_one, hidden_one, sent_one, grad_small_two],
        flops=10**9,
        late=[5, 6, 7],
        kept=[0],
    )
    near, far, (grads_one, arrived_two) = sum_pair(gain, owners, (grads_one, arrived_two))
    mine = parts[0].astype(F32)
    for k in range(1, 4):
        mine = mine + moved(parts[k], k, owners).astype(F32)
    near, mine, grad_t = lax.optimization_barrier((near, mine.astype(BF16), grad_t))
    step = 4
    while half > 2:
        high, mine = mine[half // 2 :], mine[: half // 2]
        mine = (mine.astype(F32) + moved(high, step, owners).astype(F32)).astype(BF16)
        half, step = half // 2, 2 * step
    grad_atom = mine[0].astype(F32) + moved(mine[1], step, owners).astype(F32)
    grad_edge_t, grads_one = call(
        back_last,
        [edge_wide, sds((D_EDGE, 2 * PAD + BIG), BF16)],
        [near, far] + fetch([grad_t] + kept_one[1:]) + back_one + graph + [dst_row, grads_one],
        flops=10 * 10**9,
        kept=[1],
        alias={BACK: 1},
        scratch=[pltpu.VMEM((D_EDGE, PAD), BF16), pltpu.SemaphoreType.DMA],
    )
    grad_edge = rows_first(grad_edge_t, F32)
    arrived_one = exchange(grads_one.reshape(owners, cols, 2 * PAD + BIG))
    [owned] = call(
        sum_parts, [sds((cols, 2 * (PAD + BIG)), BF16)], [arrived_one, arrived_two], flops=10**7
    )
    owned = [owned] + [moved(owned, k, groups, "group") for k in range(1, groups)]
    rows = weights.shape[0]
    results = call(
        adam,
        [sds((cols, rows), F32)] * 4 + [sds((cols, rows), BF16)],
        [weights_t, jnp.transpose(first_moment), jnp.transpose(second_moment)] + owned,
        flops=10**8,
    )
    return (edge_out, atom_out, grad_edge, grad_atom) + tuple(jnp.transpose(r) for r in results)


def solution(mesh):
    both = P(("group", "shard"), None)
    line = P(("group", "shard"))
    flat = P(None, "shard")
    in_specs = (both,) * 6 + (line, both) + (line,) * 6 + (both, both) + (flat,) * 3
    out_specs = (both,) * 4 + (flat,) * 5
    return jax.shard_map(
        per_device, mesh=mesh, in_specs=in_specs, out_specs=out_specs, check_vma=False
    )
```

```python
import jax
import jax.numpy as jnp
from jax import lax
from jax.experimental import pallas as pl
from jax.experimental.pallas import tpu as pltpu
from jax.sharding import PartitionSpec as P

D_EDGE = 128
D_ATOM = 256
D_TRI = 64
D_QUAD = 32
D_BASIS = 16
BLOCKS = 2
FOLD = 256
CHUNK = 1024
SMALL = 220
BIG = 1280
PAD = 256
ROWS = 16

edge_scale = 0.25
pair_scale = 0.5
beta_one = 0.5
beta_two = 0.5
learn_rate = 0.1
decay_rate = 0.01
epsilon = 1e-08
adam_step = 4

OFF_DOWN = {D_TRI: 0, D_QUAD: 136}
OFF_BASIS = {D_TRI: 64, D_QUAD: 168}
OFF_UP = {D_TRI: 72, D_QUAD: 172}
OFF_RADIAL = 204

F32 = jnp.float32
BF16 = jnp.bfloat16


def sds(shape, dtype):
    return jax.ShapeDtypeStruct(shape, dtype)


class Late:
    def __init__(self, source, ref, sem):
        self.ref, self.copy = ref, pltpu.make_async_copy(source, ref, sem)
        self.shape, self.begun, self.here = ref.shape, False, False

    def start(self):
        if not self.begun:
            self.copy.start()
            self.begun = True

    def wait(self):
        if not self.here:
            self.start()
            self.copy.wait()
            self.here = True

    def __getitem__(self, index):
        self.wait()
        return self.ref[index]


class Kept:
    def __init__(self, target, ref, sem):
        self.ref, self.copy, self.sent = ref, pltpu.make_async_copy(ref, target, sem), False
        self.shape, self.dtype = ref.shape, ref.dtype

    def __getitem__(self, index):
        return self.ref[index]

    def __setitem__(self, index, value):
        self.ref[index] = value

    def send(self):
        if not self.sent:
            self.copy.start()
            self.sent = True


def begin(*refs):
    for ref in refs:
        if isinstance(ref, Late):
            ref.start()


def arrive(*refs):
    for ref in refs:
        if isinstance(ref, Late):
            ref.wait()


def send(*refs):
    for ref in refs:
        if isinstance(ref, Kept):
            ref.send()


def call(body, outs, args, flops=10**9, late=(), kept=(), smem=0, scratch=(), early=None, alias=None, raw=()):
    alias = alias or {}
    held = [i for i in kept if i not in alias.values()]
    moved = [args[i] for i in late] + [outs[i] for i in held]

    def kernel(*refs):
        refs = list(refs)
        ins, rest = refs[: len(args)], refs[len(args) :]
        results, rest = rest[: len(outs)], rest[len(outs) :]
        extra, rest = rest[: len(scratch)], rest[len(scratch) :]
        buffers, sems = rest[: len(moved)], rest[len(moved) :]
        for k, i in enumerate(late):
            ins[i] = Late(ins[i], buffers[k], sems[k])
        begin(*[ins[i] for i in (late if early is None else early)])
        for k, i in enumerate(held, len(late)):
            results[i] = Kept(results[i], buffers[k], sems[k])
        body(*ins, *results, *extra)
        for i in late:
            ins[i].wait()
        for i in held:
            results[i].send()
        for i in held:
            results[i].copy.wait()

    args = [pltpu.with_memory_space_constraint(x, pltpu.HBM) if i in late or i in alias or i in raw else x for i, x in enumerate(args)]
    outs = [pltpu.HBM(x.shape, x.dtype) if i in kept else x for i, x in enumerate(outs)]
    space = [pltpu.SMEM] * smem + [pltpu.VMEM] * (len(args) - smem)
    for i in [*late, *alias, *raw]:
        space[i] = pltpu.HBM
    return pl.pallas_call(
        kernel,
        out_shape=outs,
        in_specs=[pl.BlockSpec(memory_space=s) for s in space],
        out_specs=[
            pl.BlockSpec(memory_space=pltpu.HBM if i in kept else pltpu.VMEM)
            for i in range(len(outs))
        ],
        scratch_shapes=[pltpu.VMEM(x, F32) if isinstance(x, tuple) else x for x in scratch]
        + [pltpu.VMEM(m.shape, m.dtype) for m in moved]
        + [pltpu.SemaphoreType.DMA] * len(moved),
        input_output_aliases=alias,
        compiler_params=pltpu.CompilerParams(vmem_limit_bytes=24 * 2**20),
        cost_estimate=pl.CostEstimate(flops=flops, bytes_accessed=2**20, transcendentals=0),
        name=body.__name__,
    )(*args)


def fetch(arrays):
    count = len(arrays)

    def kernel(*refs):
        copies = [
            pltpu.make_async_copy(refs[i], refs[count + i], refs[2 * count + i]) for i in range(count)
        ]
        for copy in copies:
            copy.start()
        for copy in copies:
            copy.wait()

    results = pl.pallas_call(
        kernel,
        out_shape=[sds(x.shape, x.dtype) for x in arrays],
        in_specs=[pl.BlockSpec(memory_space=pltpu.HBM)] * count,
        out_specs=[pl.BlockSpec(memory_space=pltpu.VMEM)] * count,
        scratch_shapes=[pltpu.SemaphoreType.DMA] * count,
        compiler_params=pltpu.CompilerParams(vmem_limit_bytes=2**20 * 20),
        cost_estimate=pl.CostEstimate(flops=10**9, bytes_accessed=2**20, transcendentals=0),
        name="fetch",
    )(*[pltpu.with_memory_space_constraint(x, pltpu.HBM) for x in arrays])
    return list(results)


def dot(a, b):
    return jnp.dot(a, b, preferred_element_type=F32)


def dot_nt(a, b):
    return lax.dot_general(a, b, (((1,), (1,)), ((), ())), preferred_element_type=F32)


def low(v):
    return v.astype(BF16)


def iota(shape, axis):
    return lax.broadcasted_iota(jnp.int32, shape, axis)


def ones_where(mask):
    return jnp.where(mask, 1.0, 0.0).astype(BF16)


def onehot(count, row, first=0):
    parts = []
    for start in range(0, count, 256):
        size = min(256, count - start)
        ids = iota((size, row.shape[1]), 0).astype(F32).astype(BF16)
        mask = ids == (row - (first + start)).astype(F32).astype(BF16)
        parts.append(jnp.where(mask, jnp.ones((), BF16), jnp.zeros((), BF16)))
    return parts[0] if len(parts) == 1 else jnp.concatenate(parts, axis=0)


def sigmoid(v):
    return 0.5 + 0.5 * jnp.tanh(0.5 * v)


def silu_pair(v):
    s = sigmoid(v)
    return v * s, s * (1.0 + v * (1.0 - s))


def cut(value, width):
    count = FOLD // width
    length = value.shape[1] // count
    return jnp.concatenate([value[:, g * length : (g + 1) * length] for g in range(count)], axis=0)


def uncut(value, width):
    count = FOLD // width
    return jnp.concatenate([value[g * width : (g + 1) * width] for g in range(count)], axis=1)


def pick(folded, high, width):
    result = folded[:width]
    for g in range(1, FOLD // width):
        result = jnp.where(high == g, folded[g * width : (g + 1) * width], result)
    return result


def spread(value, high, width):
    value = low(value)
    high = high.astype(F32).astype(BF16)
    return jnp.concatenate(
        [jnp.where(high == g, value, jnp.zeros((), BF16)) for g in range(FOLD // width)], axis=0
    )


def high_low(index, length):
    return index >> (length.bit_length() - 1), index & (length - 1)


def small_t(raw, offset, width, columns):
    count = 128 // width
    total = None
    for p in range(count):
        lane, d = iota((PAD, columns), 0), iota((PAD, columns), 1)
        high, rest = high_low(d, count)
        sel = ones_where((rest == p) & (lane == offset + high))
        part = dot(raw[p * width : (p + 1) * width], sel)
        total = part if total is None else total + part
    return low(total)


def small_plain(raw, offset, width, rows):
    count = 128 // width
    total = None
    for p in range(count):
        d, lane = iota((rows, PAD), 0), iota((rows, PAD), 1)
        high, rest = high_low(d, count)
        sel = ones_where((rest == p) & (lane == offset + high))
        part = dot_nt(sel, raw[p * width : (p + 1) * width])
        total = part if total is None else total + part
    return low(total)


def wide_t(raw, offset, rows):
    lane, d = iota((PAD, rows), 0), iota((PAD, rows), 1)
    return low(dot(raw, ones_where(lane == offset + d)))


def wide_plain(raw, offset, rows):
    d, lane = iota((rows, PAD), 0), iota((rows, PAD), 1)
    return low(dot_nt(ones_where(lane == offset + d), raw))


def double_plain(raw, rows):
    d, lane = iota((rows, 2 * rows), 0), iota((rows, 2 * rows), 1)
    return jnp.concatenate(
        [low(dot_nt(ones_where(lane == 2 * d + p), raw)) for p in range(2)], axis=1
    )


def put_small(grad_t, offset, width):
    count = 128 // width
    columns = grad_t.shape[1]
    value = low(grad_t)
    parts = []
    for p in range(count):
        d, lane = iota((columns, PAD), 0), iota((columns, PAD), 1)
        high, rest = high_low(d, count)
        sel = ones_where((rest == p) & (lane == offset + high))
        parts.append(dot(value, sel))
    return jnp.concatenate(parts, axis=0)


def put_wide(grad_t, offset):
    columns = grad_t.shape[1]
    d, lane = iota((columns, PAD), 0), iota((columns, PAD), 1)
    return dot(low(grad_t), ones_where(lane == offset + d))


def put_double(grad_t):
    rows = grad_t.shape[1]
    d, lane = iota((rows, 2 * rows), 0), iota((rows, 2 * rows), 1)
    value = low(grad_t)
    return low(
        dot(value[:128], ones_where(lane == 2 * d)) + dot(value[128:], ones_where(lane == 2 * d + 1))
    )


def small_matrices(raw):
    return (
        [small_t(raw, OFF_DOWN[w], w, D_EDGE) for w in (D_TRI, D_QUAD)]
        + [small_t(raw, OFF_BASIS[w], w, D_BASIS) for w in (D_TRI, D_QUAD)]
        + [wide_t(raw, OFF_UP[w], w) for w in (D_TRI, D_QUAD)]
        + [wide_t(raw, OFF_RADIAL, D_BASIS)]
    )


def back_matrices(raw):
    return [wide_plain(raw, OFF_UP[w], w) for w in (D_TRI, D_QUAD)] + [
        small_plain(raw, OFF_DOWN[w], w, D_EDGE) for w in (D_TRI, D_QUAD)
    ]


SMALL_SHAPES = [
    (D_TRI, D_EDGE), (D_QUAD, D_EDGE), (D_TRI, D_BASIS), (D_QUAD, D_BASIS), (D_EDGE, D_TRI),
    (D_EDGE, D_QUAD), (D_EDGE, D_BASIS),
]
BACK_SHAPES = [(D_TRI, D_EDGE), (D_QUAD, D_EDGE), (D_EDGE, D_TRI), (D_EDGE, D_QUAD)]


def slots(width):
    return -(-width // PAD)


def padded(value, rows, lanes):
    have, wide = value.shape
    if wide < lanes:
        value = jnp.concatenate([value, jnp.zeros((have, lanes - wide), value.dtype)], axis=1)
    if have < rows:
        value = jnp.concatenate([value, jnp.zeros((rows - have, lanes), value.dtype)], axis=0)
    return value


def pack_first(weights, out_ref, hold, sem):
    copy = pltpu.make_async_copy(weights.at[:, :PAD], hold, sem)
    copy.start()
    copy.wait()
    head = low(padded(hold[...], ROWS, PAD))
    for s in range(out_ref.shape[0]):
        out_ref[s] = head


def pack_cargo(me, weights, state, fixed, out_ref, hold):
    count = state.shape[0]
    free = (1 - fixed[...]).astype(F32)
    out_ref[0, :count] = state[...]
    out_ref[0, count : count + ROWS] = low(padded(free, ROWS, PAD))
    values = weights[...]
    half = SMALL + BIG
    gap = jnp.zeros((values.shape[0], PAD - SMALL), F32)
    one = jnp.concatenate([values[:, SMALL : half + SMALL], gap], axis=1)
    two = padded(values[:, half + SMALL :], values.shape[0], BIG + PAD)
    groups, _, width = hold.shape
    base = count + ROWS
    for side in (one, two):
        for g in range(groups):
            hold[g] = side[:, g * width : (g + 1) * width]
        mine = padded(hold[me[1]], ROWS, slots(width) * PAD)
        for k in range(slots(width)):
            out_ref[0, base : base + ROWS] = low(mine[:, k * PAD : (k + 1) * PAD])
            base = base + ROWS


def order_of(owners):
    order = [0]
    for steps in gather_rounds(owners):
        order = order + [k ^ step for step in steps for k in order]
    return order


def gather_rounds(owners):
    rounds, step = [], owners // 2
    while step > 2:
        rounds.append([step])
        step = step // 2
    return rounds + ([[1, 2, 3]] if owners > 2 else [[1]])


def scatter_order(owners):
    order, step = [0], owners // 2
    while step > 2:
        order = order + [k ^ step for k in order]
        step = step // 2
    return [k ^ low_bits for low_bits in range(4) for k in order]


def collect(me, *refs):
    *cargo, one_ref, two_ref = refs
    rows = cargo[0].shape[1]
    owners = sum(c.shape[0] for c in cargo)
    full, width = one_ref.shape
    cols = full // owners
    count = slots(width)
    base = rows - 2 * count * ROWS
    order = order_of(owners)
    shape = (full, owners * ROWS)
    row, col = iota(shape, 0), iota(shape, 1)
    owner, inside = row // cols, row % cols
    sel = None
    for position, k in enumerate(order):
        hit = (col == position * ROWS + inside) & (owner == (me[0] ^ k))
        sel = hit if sel is None else sel | hit
    sel = ones_where(sel)
    for side, ref in ((0, one_ref), (1, two_ref)):
        for k in range(count):
            start = base + (side * count + k) * ROWS
            values = jnp.concatenate(
                [c[i, start : start + ROWS] for c in cargo for i in range(c.shape[0])], axis=0
            )
            lanes = min(PAD, width - k * PAD)
            ref[:, k * PAD : k * PAD + lanes] = low(dot(sel, values))[:, :lanes]


def joined(me, pieces, hold):
    for k, piece in enumerate(pieces):
        hold[me[1] ^ k] = piece[...].astype(F32)
    return low(jnp.concatenate([hold[g] for g in range(len(pieces))], axis=1))


def small_rows(pack, cols):
    owners = pack.shape[0]
    value = pack[...].reshape(owners * ROWS, PAD)
    if cols == ROWS:
        return value
    c, row = iota((owners * cols, owners * ROWS), 0), iota((owners * cols, owners * ROWS), 1)
    return low(dot(ones_where(row == c // cols * ROWS + c % cols), value))


def prepare_one(me, pack, *refs):
    *rest, hold = refs
    groups = hold.shape[0]
    wide = joined(me, rest[:groups], hold)
    raw_one = small_rows(pack, D_EDGE // pack.shape[0])
    raw_two = wide[:, BIG:]
    values = back_matrices(raw_one) + [wide_t(raw_one, OFF_RADIAL, D_BASIS)]
    values = values + small_matrices(raw_two) + back_matrices(raw_two)
    values = values + [double_plain(wide[:, :256], D_EDGE), double_plain(wide[:, 256:768], D_ATOM)]
    for ref, value in zip(rest[groups:], values + [wide[:, :BIG]]):
        ref[...] = value


def prepare_two(me, *refs):
    *rest, hold = refs
    groups = hold.shape[0]
    big = joined(me, rest[:groups], hold)
    first_ref, second_ref, big_ref = rest[groups:]
    first_ref[...] = double_plain(big[:, :256], D_EDGE)
    second_ref[...] = double_plain(big[:, 256:768], D_ATOM)
    big_ref[...] = big[:, :BIG]


LARGE_SHAPES = [(D_EDGE, D_ATOM), (D_ATOM, D_ATOM), (D_EDGE, BIG)]
PREPARED = BACK_SHAPES + [(D_EDGE, D_BASIS)] + SMALL_SHAPES + BACK_SHAPES + LARGE_SHAPES


def pair_forward(edge_t, basis_ref, in_ref, out_ref, down_t, basis_t, up_t, xg_ref, bt_ref):
    width, edges = down_t.shape[0], edge_t.shape[1]
    length = edges * width // FOLD
    act, slope_in = silu_pair(dot(down_t, edge_t))
    table = cut(low(act), width)
    total = jnp.zeros((FOLD, length), F32)
    items = in_ref.shape[1]
    chunk = min(CHUNK, items)
    for start in range(0, items, chunk):
        cols = slice(start, start + chunk)
        in_high, in_low = high_low(in_ref[:, cols], length)
        out_high, out_low = high_low(out_ref[:, cols], length)
        xg = pick(dot(table, onehot(length, in_low)), in_high, width)
        bt = dot(basis_t, basis_ref[:, cols])
        xg_ref[:, cols] = low(xg)
        bt_ref[:, cols] = low(bt)
        total = total + dot_nt(spread(xg * bt, out_high, width), onehot(length, out_low))
    send(xg_ref, bt_ref)
    agg_t = low(uncut(total, width) * pair_scale)
    value, slope_out = silu_pair(dot(up_t, agg_t))
    return value, slope_in, agg_t, slope_out


def pair_backward(
    grad_mid, edge_t, basis_ref, in_ref, out_ref, up, down, slope_out, agg_t, xg_ref, bt_ref, slope_in,
    following,
):
    width, edges = up.shape[0], slope_in.shape[1]
    length = edges * width // FOLD
    grad_out = low(grad_mid * slope_out[...].astype(F32))
    grad_up_t = dot_nt(grad_out, agg_t[...])
    table = cut(low(dot(up, grad_out) * pair_scale), width)
    begin(xg_ref, bt_ref)
    arrive(xg_ref, bt_ref)
    begin(*following)
    total = jnp.zeros((FOLD, length), F32)
    grad_basis_t = jnp.zeros((width, D_BASIS), F32)
    items = in_ref.shape[1]
    chunk = min(CHUNK, items)
    for start in range(0, items, chunk):
        cols = slice(start, start + chunk)
        in_high, in_low = high_low(in_ref[:, cols], length)
        out_high, out_low = high_low(out_ref[:, cols], length)
        gy = pick(dot(table, onehot(length, out_low)), out_high, width)
        grad_bt = low(gy * xg_ref[:, cols].astype(F32))
        grad_basis_t = grad_basis_t + dot_nt(grad_bt, basis_ref[:, cols])
        moved = gy * bt_ref[:, cols].astype(F32)
        total = total + dot_nt(spread(moved, in_high, width), onehot(length, in_low))
    grad_in = low(uncut(total, width) * slope_in[...].astype(F32))
    grad_down_t = dot_nt(grad_in, edge_t[...])
    small = (
        put_small(grad_down_t, OFF_DOWN[width], width)
        + put_small(grad_basis_t, OFF_BASIS[width], width)
        + put_wide(grad_up_t, OFF_UP[width])
    )
    return dot(down, grad_in), small


def block_forward(state_t, matrices, graph, dst_row, out_refs):
    radial_basis, tri_basis, quad_basis, tri_in, tri_out, quad_in, quad_out = graph
    down_tri, down_quad, basis_tri, basis_quad, up_tri, up_quad, radial_t = matrices
    mid_ref, mid_low_ref = out_refs[:2]
    tri_refs, edge_ref, quad_refs, table_ref = out_refs[2:7], out_refs[7], out_refs[8:13], out_refs[13]
    edge_t = low(state_t)
    edge_ref[...] = edge_t
    send(edge_ref)
    mid = state_t
    for refs, basis, inner, outer, down, basis_t, up in (
        (tri_refs, tri_basis, tri_in, tri_out, down_tri, basis_tri, up_tri),
        (quad_refs, quad_basis, quad_in, quad_out, down_quad, basis_quad, up_quad),
    ):
        slope_out_ref, agg_ref, xg_ref, bt_ref, slope_in_ref = refs
        value, slope_in, agg, slope_out = pair_forward(
            edge_t, basis, inner, outer, down, basis_t, up, xg_ref, bt_ref
        )
        slope_in_ref[...] = low(slope_in)
        agg_ref[...] = agg
        slope_out_ref[...] = low(slope_out)
        send(slope_in_ref, agg_ref, slope_out_ref)
        mid = mid + value
    mid_ref[...] = mid
    mid_low_ref[...] = low(mid)
    send(mid_ref, mid_low_ref)
    message = low(mid * dot(radial_t, radial_basis[...]))
    atoms = table_ref.shape[0]
    step = min(512, atoms)
    for start in range(0, atoms, step):
        rows = slice(start, start + step)
        table_ref[rows] = low(dot_nt(onehot(step, dst_row[...], start), message))


def kept_shapes(edges, items):
    edge = ((D_EDGE, edges), BF16)
    tri, quad = [
        [edge, ((w, edges), BF16), ((w, items), BF16), ((w, items), BF16), ((w, edges), BF16)]
        for w in (D_TRI, D_QUAD)
    ]
    return [sds(*x) for x in [((D_EDGE, edges), F32), edge] + tri + [edge] + quad]


KEPT = 13


def first_half(edge_state, pack, *refs):
    graph, dst_row, out_refs = refs[:7], refs[7], refs[8:]
    eye = ones_where(iota((D_EDGE, D_EDGE), 0) == iota((D_EDGE, D_EDGE), 1))
    state_t = dot_nt(eye, edge_state[...])
    raw = small_rows(pack, D_EDGE // pack.shape[0])
    block_forward(state_t, small_matrices(raw), graph, dst_row, out_refs)


def atom_forward(near, far, state, free, first, second):
    atom_in = low((near[...].astype(F32) + far[...].astype(F32)) * edge_scale)
    act, slope = silu_pair(dot(atom_in, first[...]))
    hidden = low(act)
    new_state = state + free * dot(hidden, second[...])
    return atom_in, hidden, slope, new_state


def edge_pre(sent, big, src_row, dst_row):
    src_t = low(dot_nt(big[:, 768:1024], sent))
    dst_t = low(dot_nt(big[:, 1024:1280], sent))
    atoms = sent.shape[0]
    step = min(512, atoms)
    total = None
    for start in range(0, atoms, step):
        part = dot(src_t[:, start : start + step], onehot(step, src_row[...], start))
        part = part + dot(dst_t[:, start : start + step], onehot(step, dst_row[...], start))
        total = part if total is None else total + part
    return total


def middle_half(me, near, far, big, first, second, mid_in, *refs):
    matrices, graph, src_row, dst_row = refs[:7], refs[7:14], refs[14], refs[15]
    atoms = near.shape[0]
    cargo, refs = refs[16:], None
    split = 0
    owners = 0
    while len(cargo[split].shape) == 3:
        owners = owners + cargo[split].shape[0]
        split = split + 1
    cargo, rest = cargo[:split], cargo[split:]
    atom_in_ref, hidden_ref, slope_atom_ref, state_ref, sent_ref, free_ref, slope_edge_ref = rest[:7]
    *out_refs, free_wide = rest[7:]
    count = atoms // owners
    eye = iota((count, count), 0) == iota((count, count), 1)
    order = order_of(owners)
    position = 0
    for pieces in cargo:
        for i in range(pieces.shape[0]):
            rows = pl.ds(pl.multiple_of((me[0] ^ order[position]) * count, count), count)
            state_ref.ref[rows] = pieces[i, :count].astype(F32)
            flag = pieces[i, count : count + 1, :count].astype(F32)
            column = jnp.sum(jnp.where(eye, flag, 0.0), axis=1, keepdims=True)
            free_wide[rows] = jnp.broadcast_to(column, (count, D_ATOM))
            position = position + 1
    free_ref[...] = low(free_wide[...])
    send(free_ref)
    atom_in, hidden, slope, state = atom_forward(
        near, far, state_ref[...], free_wide[...], first, second
    )
    atom_in_ref[...] = atom_in
    hidden_ref[...] = hidden
    slope_atom_ref[...] = low(slope)
    state_ref[...] = state
    sent = low(state)
    sent_ref[...] = sent
    send(atom_in_ref, hidden_ref, slope_atom_ref, state_ref, sent_ref)
    act, slope_edge = silu_pair(edge_pre(sent, big, src_row, dst_row))
    slope_edge_ref[...] = low(slope_edge)
    send(slope_edge_ref)
    block_forward(mid_in[...] + act, [m[...] for m in matrices], graph, dst_row, out_refs)


def edge_tables(
    grad_pre, big, first, second, src_row, dst_row, free, slope_atom, grad_atoms, gain_ref, update_ref,
    pushed_ref,
):
    atoms = free.shape[0]
    step = min(512, atoms)
    src_t, dst_t = big[:, 768:1024], big[:, 1024:1280]
    for start in range(0, atoms, step):
        rows = slice(start, start + step)
        pick_src = onehot(step, src_row[...], start)
        pick_dst = onehot(step, dst_row[...], start)
        part = dot(low(dot_nt(pick_src, grad_pre)), src_t) + dot(low(dot_nt(pick_dst, grad_pre)), dst_t)
        grad_atoms[rows] = grad_atoms[rows] + part
    update = low(grad_atoms[...] * free)
    update_ref[...] = update
    send(update_ref)
    pushed = low(dot_nt(update, second[...]) * slope_atom)
    pushed_ref[...] = pushed
    send(pushed_ref)
    gain_ref[...] = low(dot_nt(first[...], pushed))


def turn(
    me, near, far, big, first, second, src_row, dst_row, edge_cotangent, own, state_in, free_ref, mid_in,
    atom_in_ref, hidden_ref, sent_ref, edge_ref, atom_out_ref, cotangent_ref, grad_pre_ref, atoms_ref,
    gain_ref, update_ref, pushed_ref, hold,
):
    free = free_ref[...].astype(F32)
    begin(mid_in)
    atom_in, hidden, slope, state = atom_forward(near, far, state_in[...], free, first, second)
    atom_in_ref[...] = atom_in
    hidden_ref[...] = hidden
    sent = low(state)
    sent_ref[...] = sent
    send(atom_in_ref, hidden_ref, sent_ref)
    hold[...] = state
    count = atom_out_ref.shape[0]
    mine = pl.ds(pl.multiple_of(me[0] * count, count), count)
    atom_out_ref[...] = low(hold[mine])
    act, slope_edge = silu_pair(edge_pre(sent, big, src_row, dst_row))
    edge_ref[...] = mid_in[...] + act
    send(edge_ref, atom_out_ref)
    eye = ones_where(iota((D_EDGE, D_EDGE), 0) == iota((D_EDGE, D_EDGE), 1))
    cotangent = dot_nt(eye, edge_cotangent[...])
    cotangent_ref[...] = cotangent
    grad_pre = low(cotangent * slope_edge)
    grad_pre_ref[...] = grad_pre
    send(cotangent_ref, grad_pre_ref)
    atoms_ref[...] = jnp.zeros(atoms_ref.shape, F32)
    atoms_ref.ref[mine] = own[...].astype(F32)
    edge_tables(
        grad_pre, big, first, second, src_row, dst_row, free, slope, atoms_ref, gain_ref, update_ref,
        pushed_ref,
    )


def large_grads(update, pushed, grad_pre, src_row, dst_row, atom_in, hidden, sent, out_ref):
    for lanes, value in large_values(update, pushed, grad_pre, src_row, dst_row, atom_in, hidden, sent):
        out_ref[:, lanes] = value


def large_pieces(
    me, update, pushed, grad_pre, src_row, dst_row, atom_in, hidden, sent, small, out_ref, hold
):
    hold[:, :PAD] = small[...].astype(F32)
    for lanes, value in large_values(update, pushed, grad_pre, src_row, dst_row, atom_in, hidden, sent):
        hold[:, PAD + lanes.start : PAD + lanes.stop] = value.astype(F32)
    groups, _, width = out_ref.shape
    for g in range(groups):
        out_ref[g ^ me[1]] = low(hold[:, g * width : (g + 1) * width])


def large_values(update, pushed, grad_pre, src_row, dst_row, atom_in, hidden, sent):
    atoms = sent.shape[0]
    step = min(512, atoms)
    grads = grad_pre[...]
    update_t = low(jnp.transpose(update[...].astype(F32)))
    pushed_t = low(jnp.transpose(pushed[...].astype(F32)))
    grad_src = jnp.zeros((D_EDGE, D_ATOM), F32)
    grad_dst = jnp.zeros((D_EDGE, D_ATOM), F32)
    for start in range(0, atoms, step):
        rows = slice(start, start + step)
        sums = [low(dot_nt(grads, onehot(step, row[...], start))) for row in (src_row, dst_row)]
        grad_src = grad_src + dot(sums[0], sent[rows])
        grad_dst = grad_dst + dot(sums[1], sent[rows])
    grad_second_t = dot(update_t, hidden[...])
    grad_first_t = dot(pushed_t, atom_in[...])
    return [
        (slice(0, 256), put_double(grad_first_t)),
        (slice(256, 768), put_double(grad_second_t)),
        (slice(768, 1024), low(grad_src)),
        (slice(1024, 1280), low(grad_dst)),
    ]


def turned(value_ref, out_ref):
    out_ref[...] = jnp.transpose(value_ref[...]).astype(out_ref.dtype)


def block_backward(near, far, grad_in, *refs, more_refs=()):
    mid, tri_refs, edge_ref, quad_refs = refs[0], refs[1:6], refs[6], refs[7:12]
    up_tri, up_quad, down_tri, down_quad, radial_t = refs[12:17]
    radial_basis, tri_basis, quad_basis, tri_in, tri_out, quad_in, quad_out = refs[17:24]
    dst_row = refs[24]
    gain_t = low(near[...].astype(F32) + far[...].astype(F32))
    atoms = gain_t.shape[1]
    step = min(512, atoms)
    grad_message = None
    for start in range(0, atoms, step):
        part = dot(gain_t[:, start : start + step], onehot(step, dst_row[...], start))
        grad_message = part if grad_message is None else grad_message + part
    grad_message = grad_message * edge_scale
    radial = dot(radial_t[...], radial_basis[...])
    grad_mid = grad_in[...] + grad_message * radial
    grad_radial = low(grad_message * mid[...].astype(F32))
    begin(*tri_refs[2:], edge_ref)
    small = put_wide(dot_nt(grad_radial, radial_basis[...]), OFF_RADIAL)
    total = grad_mid
    for kept, basis, inner, outer, up, down, following in (
        (tri_refs, tri_basis, tri_in, tri_out, up_tri, down_tri, quad_refs),
        (quad_refs, quad_basis, quad_in, quad_out, up_quad, down_quad, more_refs),
    ):
        value, more = pair_backward(
            grad_mid, edge_ref, basis, inner, outer, up[...], down[...], *kept, following
        )
        total = total + value
        small = small + more
    return total, low(small)


BACK = 28


def back_last(*refs):
    _, grad_ref, all_ref, hold, sem = refs[BACK:]
    grad, small = block_backward(*refs[:BACK])
    hold[...] = small
    copy = pltpu.make_async_copy(hold, all_ref.at[:, :PAD], sem)
    copy.start()
    grad_ref[...] = grad
    copy.wait()


def back_middle(me, *refs):
    back, refs = refs[:BACK], refs[BACK:]
    big, first, second, src_row, slope_edge, free_ref, slope_atom, held = refs[:8]
    small_ref, gain_ref, update_ref, pushed_ref, grad_pre_ref, grad_ref = refs[8:14]
    *parts, grad_atoms = refs[14:]
    grad, small = block_backward(*back, more_refs=(slope_edge, free_ref, slope_atom, held))
    small_ref[...] = small
    grad_ref[...] = grad
    grad_pre = low(grad * slope_edge[...].astype(F32))
    grad_pre_ref[...] = grad_pre
    send(grad_ref, grad_pre_ref)
    grad_atoms[...] = held[...]
    edge_tables(
        grad_pre, big, first, second, src_row, back[-1], free_ref[...].astype(F32),
        slope_atom[...].astype(F32), grad_atoms, gain_ref, update_ref, pushed_ref,
    )
    quarter, count, _ = parts[0].shape
    for k, step in enumerate(scatter_order(4 * quarter)):
        rows = pl.ds(pl.multiple_of((me[0] ^ step) * count, count), count)
        parts[k // quarter][k % quarter] = low(grad_atoms[rows])


def total_of(arrived):
    total = arrived[0].astype(F32)
    for s in range(1, arrived.shape[0]):
        total = total + arrived[s].astype(F32)
    return total


def sum_list(pieces):
    total = pieces[0][...].astype(F32)
    for piece in pieces[1:]:
        total = total + piece[...].astype(F32)
    return total


def sum_pieces(*refs):
    *pieces, out_ref = refs
    out_ref[:, :PAD] = jnp.zeros((out_ref.shape[0], PAD), BF16)
    out_ref[:, PAD:] = low(sum_list(pieces))
    send(out_ref)


def sum_parts(one, two, out_ref):
    width = one.shape[2]
    out_ref[:, :width] = low(total_of(one))
    out_ref[:, width:] = low(total_of(two))


def adam(me, weights, first, second, *refs):
    *pieces, grad_ref, weights_ref, first_ref, second_ref, low_ref, hold = refs
    groups, _, lanes = hold.shape
    total = sum_list(pieces)
    for k, piece in enumerate(pieces):
        hold[me[1] ^ k] = piece[:, PAD : PAD + lanes].astype(F32)
    joint = jnp.concatenate([hold[g] for g in range(groups)], axis=1)
    grad = jnp.concatenate(
        [total[:, :SMALL], joint[:, PAD:], joint[:, :SMALL], total[:, PAD + lanes :]], axis=1
    )
    grad_ref[...] = grad
    old = weights[...]
    new_first = beta_one * first[...] + (1.0 - beta_one) * grad
    new_second = beta_two * second[...] + (1.0 - beta_two) * grad * grad
    first_ref[...] = new_first
    second_ref[...] = new_second
    first_hat = new_first / (1.0 - beta_one**adam_step)
    second_hat = new_second / (1.0 - beta_two**adam_step)
    new = old - learn_rate * (first_hat / (jnp.sqrt(second_hat) + epsilon) + decay_rate * old)
    weights_ref[...] = new
    low_ref[...] = low(new)


def exchange(pieces):
    return lax.all_to_all(pieces, "shard", split_axis=0, concat_axis=0)


def sum_pair(table, owners, beside=None):
    rounds = []
    step = 1
    while step < owners:
        rounds.append([step])
        step = 2 * step
    if len(rounds) > 2:
        rounds = [[1, 2, 3]] + rounds[2:]
    for steps in rounds[:-1]:
        others = [moved(table, k, owners) for k in steps]
        if beside is not None:
            table, beside = lax.optimization_barrier((table, beside))
        total = table.astype(F32)
        for other in others:
            total = total + other.astype(F32)
        table = total.astype(BF16)
    return table, moved(table, rounds[-1][0], owners), beside


def moved(table, step, owners, axis="shard"):
    return lax.ppermute(table, axis, [(i, i ^ step) for i in range(owners)])


def per_device(
    edge_state, atom_state, radial_basis, triplet_basis, quad_basis, dst_owner, dst_local, src_owner,
    src_local, triplet_in, triplet_out, quad_in, quad_out, fixed_atoms, edge_cotangent,
    atom_cotangent, weights, first_moment, second_moment,
):
    owners = lax.axis_size("shard")
    groups = lax.axis_size("group")
    edges = edge_state.shape[0]
    count = atom_state.shape[0]
    atoms = count * owners
    items = triplet_in.shape[0]
    me = jnp.stack([lax.axis_index("shard"), lax.axis_index("group")]).astype(jnp.int32)
    weights_t = jnp.transpose(weights)
    cols = weights_t.shape[0]
    lanes = (BIG + PAD) // groups
    [pack] = call(
        pack_first,
        [sds((owners, ROWS, PAD), BF16)],
        [weights_t],
        flops=10**7,
        raw=[0],
        scratch=[pltpu.VMEM((cols, PAD), F32), pltpu.SemaphoreType.DMA],
    )
    pack, state = lax.optimization_barrier((pack, atom_state))
    pack = exchange(pack)
    [cargo] = call(
        pack_cargo,
        [sds((1, count + ROWS * (1 + 2 * slots(lanes)), D_ATOM), BF16)],
        [me, weights_t, state, fixed_atoms.reshape(1, count)],
        flops=10**7,
        late=[1, 2, 3],
        smem=1,
        scratch=[(groups, cols, lanes)],
    )
    cargo = [cargo]
    for steps in gather_rounds(owners):
        held = cargo[0] if len(cargo) == 1 else jnp.concatenate(cargo, axis=0)
        cargo = cargo + [moved(held, step, owners) for step in steps]
    lanes_shape = sds((D_EDGE, lanes), BF16)
    wide, big_two = call(collect, [lanes_shape, lanes_shape], [me] + cargo, flops=10**7, smem=1)
    dst_row = (dst_owner[:, 0] * count + dst_local).reshape(1, edges)
    src_row = (src_owner[:, 0] * count + src_local).reshape(1, edges)
    graph = [
        jnp.transpose(radial_basis),
        jnp.transpose(triplet_basis),
        jnp.transpose(quad_basis),
        triplet_in.reshape(1, items),
        triplet_out.reshape(1, items),
        quad_in.reshape(1, items),
        quad_out.reshape(1, items),
    ]
    kept = kept_shapes(edges, items)
    table_shape = sds((atoms, D_EDGE), BF16)
    edge_shape = sds((D_EDGE, edges), BF16)
    edge_wide = sds((D_EDGE, edges), F32)
    atom_shape = sds((atoms, D_ATOM), BF16)
    atom_wide = sds((atoms, D_ATOM), F32)
    gain_shape = sds((D_EDGE, atoms), BF16)
    *kept_one, table = call(
        first_half,
        kept + [table_shape],
        [edge_state, pack] + graph + [dst_row],
        flops=8 * 10**9,
        kept=range(KEPT),
    )
    near, far, _ = sum_pair(table, owners)

    def everywhere(piece):
        return [piece] + [moved(piece, k, groups, "group") for k in range(1, groups)]

    prepared = list(
        call(
            prepare_one,
            [sds(s, BF16) for s in PREPARED],
            [me, pack] + everywhere(wide),
            flops=10**9,
            smem=1,
            scratch=[(groups, D_EDGE, lanes)],
        )
    )
    back_one, small_two, back_two = prepared[:5], prepared[5:12], prepared[12:16] + [prepared[11]]
    first_one, second_one, big_one = prepared[16:]
    (
        atom_in_one, hidden_one, slope_one, state_one, sent_one, free, slope_edge_one, *kept_two, table,
    ) = call(
        middle_half,
        [table_shape, atom_shape, atom_shape, atom_wide, atom_shape, atom_shape, edge_shape]
        + kept
        + [table_shape],
        [me, near, far, big_one, first_one, second_one, kept_one[0]]
        + small_two
        + graph
        + [src_row, dst_row]
        + cargo,
        flops=10 * 10**9,
        late=[6],
        kept=range(7 + KEPT),
        smem=1,
        scratch=[(atoms, D_ATOM)],
    )
    near, far, _ = sum_pair(table, owners)
    near, state_one, kept_two[0] = lax.optimization_barrier((near, state_one, kept_two[0]))
    first_two, second_two, big_two = call(
        prepare_two,
        [sds(s, BF16) for s in LARGE_SHAPES],
        [me] + everywhere(big_two),
        flops=10**9,
        smem=1,
        scratch=[(groups, D_EDGE, lanes)],
    )
    (
        atom_in_two, hidden_two, sent_two, edge_out_t, atom_out, grad_t, grad_pre, grad_atoms, gain, update,
        pushed,
    ) = call(
        turn,
        [table_shape, atom_shape, atom_shape, edge_wide, sds((count, D_ATOM), BF16), edge_wide, edge_shape,
         atom_wide, gain_shape, atom_shape, atom_shape],
        [me, near, far, big_two, first_two, second_two, src_row, dst_row, edge_cotangent,
         atom_cotangent] + fetch([state_one, free, kept_two[0]]),
        flops=2 * 10**9,
        kept=[4, 5, 7],
        smem=1,
        scratch=[(atoms, D_ATOM)],
    )

    def rows_first(value_t, dtype):
        return call(turned, [sds((edges, D_EDGE), dtype)], [value_t], flops=10**8)[0]

    edge_out = rows_first(edge_out_t, BF16)
    near, far, (grads_two, edge_out) = sum_pair(
        gain,
        owners,
        (call(
            large_grads,
            [sds((D_EDGE, BIG), BF16)],
            [update, pushed, grad_pre, src_row, dst_row, atom_in_two, hidden_two, sent_two],
            flops=10**9,
        )[0], edge_out),
    )
    arrived_two = exchange(grads_two.reshape(owners, cols, BIG))
    fetched = fetch([grad_t] + kept_two[1:] + [slope_edge_one, free, slope_one, grad_atoms])
    half = owners // 4
    grad_small_two, gain, update, pushed, grad_pre, grad_t, *parts = call(
        back_middle,
        [sds((D_EDGE, PAD), BF16), gain_shape, atom_shape, atom_shape, edge_shape, edge_wide,
         *[sds((half, count, D_ATOM), BF16)] * 4],
        [me, near, far]
        + fetched[:KEPT]
        + back_two
        + graph
        + [dst_row, big_one, first_one, second_one, src_row]
        + fetched[KEPT:],
        flops=10 * 10**9,
        kept=[5],
        smem=1,
        scratch=[(atoms, D_ATOM)],
    )
    [pieces] = call(
        large_pieces,
        [sds((groups, D_EDGE, lanes), BF16)],
        [me, update, pushed, grad_pre, src_row, dst_row, atom_in_one, hidden_one, sent_one, grad_small_two],
        flops=10**9,
        late=[6, 7, 8],
        smem=1,
        scratch=[(D_EDGE, PAD + BIG)],
    )
    near, far, (pieces, arrived_two) = sum_pair(gain, owners, (pieces, arrived_two))
    pieces = [pieces[0]] + [moved(pieces[k], k, groups, "group") for k in range(1, groups)]
    [grads_one] = call(sum_pieces, [sds((D_EDGE, PAD + lanes), BF16)], pieces, flops=10**7, kept=[0])
    grads_one, grad_t = lax.optimization_barrier((grads_one, grad_t))
    mine = parts[0].astype(F32)
    for k in range(1, 4):
        mine = mine + moved(parts[k], k, owners).astype(F32)
    mine = mine.astype(BF16)
    step = 4
    while half > 2:
        high, mine = mine[half // 2 :], mine[: half // 2]
        mine = (mine.astype(F32) + moved(high, step, owners).astype(F32)).astype(BF16)
        half, step = half // 2, 2 * step
    grad_atom = mine[0].astype(F32) + moved(mine[1], step, owners).astype(F32)
    grad_edge_t, grads_one = call(
        back_last,
        [edge_wide, sds((D_EDGE, PAD + lanes), BF16)],
        [near, far] + fetch([grad_t] + kept_one[1:]) + back_one + graph + [dst_row, grads_one],
        flops=10 * 10**9,
        kept=[1],
        alias={BACK: 1},
        scratch=[pltpu.VMEM((D_EDGE, PAD), BF16), pltpu.SemaphoreType.DMA],
    )
    grad_edge = rows_first(grad_edge_t, F32)
    arrived_one = exchange(grads_one.reshape(owners, cols, PAD + lanes))
    [owned] = call(
        sum_parts, [sds((cols, PAD + lanes + BIG), BF16)], [arrived_one, arrived_two], flops=10**7
    )
    owned = [owned] + [moved(owned, k, groups, "group") for k in range(1, groups)]
    rows = weights.shape[0]
    results = call(
        adam,
        [sds((cols, rows), F32)] * 4 + [sds((cols, rows), BF16)],
        [me, weights_t, jnp.transpose(first_moment), jnp.transpose(second_moment)] + owned,
        flops=10**8,
        smem=1,
        scratch=[(groups, cols, lanes)],
    )
    return (edge_out, atom_out, grad_edge, grad_atom) + tuple(jnp.transpose(r) for r in results)


def solution(mesh):
    both = P(("group", "shard"), None)
    line = P(("group", "shard"))
    flat = P(None, "shard")
    in_specs = (both,) * 6 + (line, both) + (line,) * 6 + (both, both) + (flat,) * 3
    out_specs = (both,) * 4 + (flat,) * 5
    return jax.shard_map(
        per_device, mesh=mesh, in_specs=in_specs, out_specs=out_specs, check_vma=False
    )
```

```python
import jax
import jax.numpy as jnp
from jax import lax
from jax.experimental import pallas as pl
from jax.experimental.pallas import tpu as pltpu
from jax.sharding import PartitionSpec as P

D_EDGE = 128
D_ATOM = 256
D_TRI = 64
D_QUAD = 32
D_BASIS = 16
BLOCKS = 2
FOLD = 256
CHUNK = 1024
SMALL = 220
BIG = 1280
PAD = 256
ROWS = 16

edge_scale = 0.25
pair_scale = 0.5
beta_one = 0.5
beta_two = 0.5
learn_rate = 0.1
decay_rate = 0.01
epsilon = 1e-08
adam_step = 4

OFF_DOWN = {D_TRI: 0, D_QUAD: 136}
OFF_BASIS = {D_TRI: 64, D_QUAD: 168}
OFF_UP = {D_TRI: 72, D_QUAD: 172}
OFF_RADIAL = 204

F32 = jnp.float32
BF16 = jnp.bfloat16


def sds(shape, dtype):
    return jax.ShapeDtypeStruct(shape, dtype)


class Late:
    def __init__(self, source, ref, sem):
        self.ref, self.copy = ref, pltpu.make_async_copy(source, ref, sem)
        self.shape, self.begun, self.here = ref.shape, False, False

    def start(self):
        if not self.begun:
            self.copy.start()
            self.begun = True

    def wait(self):
        if not self.here:
            self.start()
            self.copy.wait()
            self.here = True

    def __getitem__(self, index):
        self.wait()
        return self.ref[index]


class Kept:
    def __init__(self, target, ref, sem):
        self.ref, self.copy, self.sent = ref, pltpu.make_async_copy(ref, target, sem), False
        self.shape, self.dtype = ref.shape, ref.dtype

    def __getitem__(self, index):
        return self.ref[index]

    def __setitem__(self, index, value):
        self.ref[index] = value

    def send(self):
        if not self.sent:
            self.copy.start()
            self.sent = True


def begin(*refs):
    for ref in refs:
        if isinstance(ref, Late):
            ref.start()


def arrive(*refs):
    for ref in refs:
        if isinstance(ref, Late):
            ref.wait()


def send(*refs):
    for ref in refs:
        if isinstance(ref, Kept):
            ref.send()


def call(body, outs, args, flops=10**9, late=(), kept=(), smem=0, scratch=(), early=None, alias=None, raw=()):
    alias = alias or {}
    held = [i for i in kept if i not in alias.values()]
    moved = [args[i] for i in late] + [outs[i] for i in held]

    def kernel(*refs):
        refs = list(refs)
        ins, rest = refs[: len(args)], refs[len(args) :]
        results, rest = rest[: len(outs)], rest[len(outs) :]
        extra, rest = rest[: len(scratch)], rest[len(scratch) :]
        buffers, sems = rest[: len(moved)], rest[len(moved) :]
        for k, i in enumerate(late):
            ins[i] = Late(ins[i], buffers[k], sems[k])
        begin(*[ins[i] for i in (late if early is None else early)])
        for k, i in enumerate(held, len(late)):
            results[i] = Kept(results[i], buffers[k], sems[k])
        body(*ins, *results, *extra)
        for i in late:
            ins[i].wait()
        for i in held:
            results[i].send()
        for i in held:
            results[i].copy.wait()

    args = [pltpu.with_memory_space_constraint(x, pltpu.HBM) if i in late or i in alias or i in raw else x for i, x in enumerate(args)]
    outs = [pltpu.HBM(x.shape, x.dtype) if i in kept else x for i, x in enumerate(outs)]
    space = [pltpu.SMEM] * smem + [pltpu.VMEM] * (len(args) - smem)
    for i in [*late, *alias, *raw]:
        space[i] = pltpu.HBM
    return pl.pallas_call(
        kernel,
        out_shape=outs,
        in_specs=[pl.BlockSpec(memory_space=s) for s in space],
        out_specs=[
            pl.BlockSpec(memory_space=pltpu.HBM if i in kept else pltpu.VMEM)
            for i in range(len(outs))
        ],
        scratch_shapes=[pltpu.VMEM(x, F32) if isinstance(x, tuple) else x for x in scratch]
        + [pltpu.VMEM(m.shape, m.dtype) for m in moved]
        + [pltpu.SemaphoreType.DMA] * len(moved),
        input_output_aliases=alias,
        compiler_params=pltpu.CompilerParams(vmem_limit_bytes=24 * 2**20),
        cost_estimate=pl.CostEstimate(flops=flops, bytes_accessed=2**20, transcendentals=0),
        name=body.__name__,
    )(*args)


def fetch(arrays):
    count = len(arrays)

    def kernel(*refs):
        copies = [
            pltpu.make_async_copy(refs[i], refs[count + i], refs[2 * count + i]) for i in range(count)
        ]
        for copy in copies:
            copy.start()
        for copy in copies:
            copy.wait()

    results = pl.pallas_call(
        kernel,
        out_shape=[sds(x.shape, x.dtype) for x in arrays],
        in_specs=[pl.BlockSpec(memory_space=pltpu.HBM)] * count,
        out_specs=[pl.BlockSpec(memory_space=pltpu.VMEM)] * count,
        scratch_shapes=[pltpu.SemaphoreType.DMA] * count,
        compiler_params=pltpu.CompilerParams(vmem_limit_bytes=2**20 * 20),
        cost_estimate=pl.CostEstimate(flops=10**9, bytes_accessed=2**20, transcendentals=0),
        name="fetch",
    )(*[pltpu.with_memory_space_constraint(x, pltpu.HBM) for x in arrays])
    return list(results)


def dot(a, b):
    return jnp.dot(a, b, preferred_element_type=F32)


def dot_nt(a, b):
    return lax.dot_general(a, b, (((1,), (1,)), ((), ())), preferred_element_type=F32)


def low(v):
    return v.astype(BF16)


def iota(shape, axis):
    return lax.broadcasted_iota(jnp.int32, shape, axis)


def ones_where(mask):
    return jnp.where(mask, 1.0, 0.0).astype(BF16)


def onehot(count, row, first=0):
    parts = []
    for start in range(0, count, 256):
        size = min(256, count - start)
        ids = iota((size, row.shape[1]), 0).astype(F32).astype(BF16)
        mask = ids == (row - (first + start)).astype(F32).astype(BF16)
        parts.append(jnp.where(mask, jnp.ones((), BF16), jnp.zeros((), BF16)))
    return parts[0] if len(parts) == 1 else jnp.concatenate(parts, axis=0)


def sigmoid(v):
    return 0.5 + 0.5 * jnp.tanh(0.5 * v)


def silu_pair(v):
    s = sigmoid(v)
    return v * s, s * (1.0 + v * (1.0 - s))


def cut(value, width):
    count = FOLD // width
    length = value.shape[1] // count
    return jnp.concatenate([value[:, g * length : (g + 1) * length] for g in range(count)], axis=0)


def uncut(value, width):
    count = FOLD // width
    return jnp.concatenate([value[g * width : (g + 1) * width] for g in range(count)], axis=1)


def pick(folded, high, width):
    result = folded[:width]
    for g in range(1, FOLD // width):
        result = jnp.where(high == g, folded[g * width : (g + 1) * width], result)
    return result


def spread(value, high, width):
    value = low(value)
    high = high.astype(F32).astype(BF16)
    return jnp.concatenate(
        [jnp.where(high == g, value, jnp.zeros((), BF16)) for g in range(FOLD // width)], axis=0
    )


def high_low(index, length):
    return index >> (length.bit_length() - 1), index & (length - 1)


def small_t(raw, offset, width, columns):
    count = 128 // width
    total = None
    for p in range(count):
        lane, d = iota((PAD, columns), 0), iota((PAD, columns), 1)
        high, rest = high_low(d, count)
        sel = ones_where((rest == p) & (lane == offset + high))
        part = dot(raw[p * width : (p + 1) * width], sel)
        total = part if total is None else total + part
    return low(total)


def small_plain(raw, offset, width, rows):
    count = 128 // width
    total = None
    for p in range(count):
        d, lane = iota((rows, PAD), 0), iota((rows, PAD), 1)
        high, rest = high_low(d, count)
        sel = ones_where((rest == p) & (lane == offset + high))
        part = dot_nt(sel, raw[p * width : (p + 1) * width])
        total = part if total is None else total + part
    return low(total)


def wide_t(raw, offset, rows):
    lane, d = iota((PAD, rows), 0), iota((PAD, rows), 1)
    return low(dot(raw, ones_where(lane == offset + d)))


def wide_plain(raw, offset, rows):
    d, lane = iota((rows, PAD), 0), iota((rows, PAD), 1)
    return low(dot_nt(ones_where(lane == offset + d), raw))


def double_plain(raw, rows):
    d, lane = iota((rows, 2 * rows), 0), iota((rows, 2 * rows), 1)
    return jnp.concatenate(
        [low(dot_nt(ones_where(lane == 2 * d + p), raw)) for p in range(2)], axis=1
    )


def put_small(grad_t, offset, width):
    count = 128 // width
    columns = grad_t.shape[1]
    value = low(grad_t)
    parts = []
    for p in range(count):
        d, lane = iota((columns, PAD), 0), iota((columns, PAD), 1)
        high, rest = high_low(d, count)
        sel = ones_where((rest == p) & (lane == offset + high))
        parts.append(dot(value, sel))
    return jnp.concatenate(parts, axis=0)


def put_wide(grad_t, offset):
    columns = grad_t.shape[1]
    d, lane = iota((columns, PAD), 0), iota((columns, PAD), 1)
    return dot(low(grad_t), ones_where(lane == offset + d))


def put_double(grad_t):
    rows = grad_t.shape[1]
    d, lane = iota((rows, 2 * rows), 0), iota((rows, 2 * rows), 1)
    value = low(grad_t)
    return low(
        dot(value[:128], ones_where(lane == 2 * d)) + dot(value[128:], ones_where(lane == 2 * d + 1))
    )


def small_matrices(raw):
    return (
        [small_t(raw, OFF_DOWN[w], w, D_EDGE) for w in (D_TRI, D_QUAD)]
        + [small_t(raw, OFF_BASIS[w], w, D_BASIS) for w in (D_TRI, D_QUAD)]
        + [wide_t(raw, OFF_UP[w], w) for w in (D_TRI, D_QUAD)]
        + [wide_t(raw, OFF_RADIAL, D_BASIS)]
    )


def back_matrices(raw):
    return [wide_plain(raw, OFF_UP[w], w) for w in (D_TRI, D_QUAD)] + [
        small_plain(raw, OFF_DOWN[w], w, D_EDGE) for w in (D_TRI, D_QUAD)
    ]


SMALL_SHAPES = [
    (D_TRI, D_EDGE), (D_QUAD, D_EDGE), (D_TRI, D_BASIS), (D_QUAD, D_BASIS), (D_EDGE, D_TRI),
    (D_EDGE, D_QUAD), (D_EDGE, D_BASIS),
]
BACK_SHAPES = [(D_TRI, D_EDGE), (D_QUAD, D_EDGE), (D_EDGE, D_TRI), (D_EDGE, D_QUAD)]


def slots(width):
    return -(-width // PAD)


def padded(value, rows, lanes):
    have, wide = value.shape
    if wide < lanes:
        value = jnp.concatenate([value, jnp.zeros((have, lanes - wide), value.dtype)], axis=1)
    if have < rows:
        value = jnp.concatenate([value, jnp.zeros((rows - have, lanes), value.dtype)], axis=0)
    return value


def pack_first(weights, out_ref, hold, sem):
    copy = pltpu.make_async_copy(weights.at[:, :PAD], hold, sem)
    copy.start()
    copy.wait()
    out_ref[0] = low(padded(hold[...], ROWS, PAD))


def pack_cargo(me, weights, state, fixed, out_ref, hold):
    count = state.shape[0]
    free = (1 - fixed[...]).astype(F32)
    out_ref[0, :count] = state[...]
    out_ref[0, count : count + ROWS] = low(padded(free, ROWS, PAD))
    values = weights[...]
    half = SMALL + BIG
    gap = jnp.zeros((values.shape[0], PAD - SMALL), F32)
    one = jnp.concatenate([values[:, SMALL : half + SMALL], gap], axis=1)
    two = padded(values[:, half + SMALL :], values.shape[0], BIG + PAD)
    groups, _, width = hold.shape
    base = count + ROWS
    for side in (one, two):
        for g in range(groups):
            hold[g] = side[:, g * width : (g + 1) * width]
        mine = padded(hold[me[1]], ROWS, slots(width) * PAD)
        for k in range(slots(width)):
            out_ref[0, base : base + ROWS] = low(mine[:, k * PAD : (k + 1) * PAD])
            base = base + ROWS


def order_of(owners):
    order = [0]
    for steps in gather_rounds(owners):
        order = order + [k ^ step for step in steps for k in order]
    return order


def gather_rounds(owners):
    rounds, step = [], owners // 2
    while step > 2:
        rounds.append([step])
        step = step // 2
    return rounds + ([[1, 2, 3]] if owners > 2 else [[1]])


def scatter_order(owners):
    order, step = [0], owners // 2
    while step > 2:
        order = order + [k ^ step for k in order]
        step = step // 2
    return [k ^ low_bits for low_bits in range(4) for k in order]


def arrivals(pieces):
    return [piece[i] for piece in pieces for i in range(piece.shape[0])]


def arrival_pick(me, order, cols):
    col = iota((1, len(order) * ROWS), 1)
    block, inside = high_low(col, ROWS)
    owner = jnp.zeros(col.shape, jnp.int32)
    for position, k in enumerate(order):
        owner = jnp.where(block == position, me ^ k, owner)
    return onehot(len(order) * cols, jnp.where(inside < cols, owner * cols + inside, -1))


def collect(me, *refs):
    *cargo, one_ref, two_ref, state_ref, free_ref = refs
    cargo = arrivals(cargo)
    owners = len(cargo)
    full, width = one_ref.shape
    count = state_ref.shape[0] // owners
    order = order_of(owners)
    sel = arrival_pick(me[0], order, full // owners)
    for side, ref in ((0, one_ref), (1, two_ref)):
        for k in range(slots(width)):
            start = count + ROWS * (1 + side * slots(width) + k)
            values = jnp.concatenate([c[start : start + ROWS] for c in cargo], axis=0)
            lanes = min(PAD, width - k * PAD)
            ref[:, k * PAD : k * PAD + lanes] = low(dot(sel, values))[:, :lanes]
    eye = iota((count, count), 0) == iota((count, count), 1)
    for piece, k in zip(cargo, order):
        rows = pl.ds(pl.multiple_of((me[0] ^ k) * count, count), count)
        state_ref[rows] = piece[:count]
        flag = piece[count : count + 1, :count].astype(F32)
        column = jnp.sum(jnp.where(eye, flag, 0.0), axis=1, keepdims=True)
        free_ref[rows] = low(jnp.broadcast_to(column, (count, D_ATOM)))


def joined(me, pieces, hold):
    for k, piece in enumerate(pieces):
        hold[me[1] ^ k] = piece[...].astype(F32)
    return low(jnp.concatenate([hold[g] for g in range(len(pieces))], axis=1))


def prepare_one(me, raw, *refs):
    *rest, hold = refs
    groups = hold.shape[0]
    wide = joined(me, rest[:groups], hold)
    raw_one = raw[...]
    raw_two = wide[:, BIG:]
    values = back_matrices(raw_one) + [wide_t(raw_one, OFF_RADIAL, D_BASIS)]
    values = values + small_matrices(raw_two) + back_matrices(raw_two)
    values = values + [double_plain(wide[:, :256], D_EDGE), double_plain(wide[:, 256:768], D_ATOM)]
    for ref, value in zip(rest[groups:], values + [wide[:, :BIG]]):
        ref[...] = value


def prepare_two(me, *refs):
    *rest, hold = refs
    groups = hold.shape[0]
    big = joined(me, rest[:groups], hold)
    first_ref, second_ref, big_ref = rest[groups:]
    first_ref[...] = double_plain(big[:, :256], D_EDGE)
    second_ref[...] = double_plain(big[:, 256:768], D_ATOM)
    big_ref[...] = big[:, :BIG]


LARGE_SHAPES = [(D_EDGE, D_ATOM), (D_ATOM, D_ATOM), (D_EDGE, BIG)]
PREPARED = BACK_SHAPES + [(D_EDGE, D_BASIS)] + SMALL_SHAPES + BACK_SHAPES + LARGE_SHAPES


def pair_forward(edge_t, basis_ref, in_ref, out_ref, down_t, basis_t, up_t, xg_ref, bt_ref):
    width, edges = down_t.shape[0], edge_t.shape[1]
    length = edges * width // FOLD
    act, slope_in = silu_pair(dot(down_t, edge_t))
    table = cut(low(act), width)
    total = jnp.zeros((FOLD, length), F32)
    items = in_ref.shape[1]
    chunk = min(CHUNK, items)
    for start in range(0, items, chunk):
        cols = slice(start, start + chunk)
        in_high, in_low = high_low(in_ref[:, cols], length)
        out_high, out_low = high_low(out_ref[:, cols], length)
        xg = pick(dot(table, onehot(length, in_low)), in_high, width)
        bt = dot(basis_t, basis_ref[:, cols])
        xg_ref[:, cols] = low(xg)
        bt_ref[:, cols] = low(bt)
        total = total + dot_nt(spread(xg * bt, out_high, width), onehot(length, out_low))
    send(xg_ref, bt_ref)
    agg_t = low(uncut(total, width) * pair_scale)
    value, slope_out = silu_pair(dot(up_t, agg_t))
    return value, slope_in, agg_t, slope_out


def pair_backward(
    grad_mid, edge_t, basis_ref, in_ref, out_ref, up, down, slope_out, agg_t, xg_ref, bt_ref, slope_in,
    following,
):
    width, edges = up.shape[0], slope_in.shape[1]
    length = edges * width // FOLD
    grad_out = low(grad_mid * slope_out[...].astype(F32))
    grad_up_t = dot_nt(grad_out, agg_t[...])
    table = cut(low(dot(up, grad_out) * pair_scale), width)
    begin(xg_ref, bt_ref)
    arrive(xg_ref, bt_ref)
    begin(*following)
    total = jnp.zeros((FOLD, length), F32)
    grad_basis_t = jnp.zeros((width, D_BASIS), F32)
    items = in_ref.shape[1]
    chunk = min(CHUNK, items)
    for start in range(0, items, chunk):
        cols = slice(start, start + chunk)
        in_high, in_low = high_low(in_ref[:, cols], length)
        out_high, out_low = high_low(out_ref[:, cols], length)
        gy = pick(dot(table, onehot(length, out_low)), out_high, width)
        grad_bt = low(gy * xg_ref[:, cols].astype(F32))
        grad_basis_t = grad_basis_t + dot_nt(grad_bt, basis_ref[:, cols])
        moved = gy * bt_ref[:, cols].astype(F32)
        total = total + dot_nt(spread(moved, in_high, width), onehot(length, in_low))
    grad_in = low(uncut(total, width) * slope_in[...].astype(F32))
    grad_down_t = dot_nt(grad_in, edge_t[...])
    small = (
        put_small(grad_down_t, OFF_DOWN[width], width)
        + put_small(grad_basis_t, OFF_BASIS[width], width)
        + put_wide(grad_up_t, OFF_UP[width])
    )
    return dot(down, grad_in), small


def block_forward(state_t, matrices, graph, dst_row, out_refs):
    radial_basis, tri_basis, quad_basis, tri_in, tri_out, quad_in, quad_out = graph
    down_tri, down_quad, basis_tri, basis_quad, up_tri, up_quad, radial_t = matrices
    mid_ref, mid_low_ref = out_refs[:2]
    tri_refs, edge_ref, quad_refs, table_ref = out_refs[2:7], out_refs[7], out_refs[8:13], out_refs[13]
    edge_t = low(state_t)
    edge_ref[...] = edge_t
    send(edge_ref)
    mid = state_t
    for refs, basis, inner, outer, down, basis_t, up in (
        (tri_refs, tri_basis, tri_in, tri_out, down_tri, basis_tri, up_tri),
        (quad_refs, quad_basis, quad_in, quad_out, down_quad, basis_quad, up_quad),
    ):
        slope_out_ref, agg_ref, xg_ref, bt_ref, slope_in_ref = refs
        value, slope_in, agg, slope_out = pair_forward(
            edge_t, basis, inner, outer, down, basis_t, up, xg_ref, bt_ref
        )
        slope_in_ref[...] = low(slope_in)
        agg_ref[...] = agg
        slope_out_ref[...] = low(slope_out)
        send(slope_in_ref, agg_ref, slope_out_ref)
        mid = mid + value
    mid_ref[...] = mid
    mid_low_ref[...] = low(mid)
    send(mid_ref, mid_low_ref)
    message = low(mid * dot(radial_t, radial_basis[...]))
    atoms = table_ref.shape[0]
    step = min(512, atoms)
    for start in range(0, atoms, step):
        rows = slice(start, start + step)
        table_ref[rows] = low(dot_nt(onehot(step, dst_row[...], start), message))


def kept_shapes(edges, items):
    edge = ((D_EDGE, edges), BF16)
    tri, quad = [
        [edge, ((w, edges), BF16), ((w, items), BF16), ((w, items), BF16), ((w, edges), BF16)]
        for w in (D_TRI, D_QUAD)
    ]
    return [sds(*x) for x in [((D_EDGE, edges), F32), edge] + tri + [edge] + quad]


KEPT = 13


def first_half(me, edge_state, *refs):
    graph, dst_row, rest = refs[:7], refs[7], refs[8:]
    pack = [ref for ref in rest if len(ref.shape) == 3]
    raw_ref, *out_refs = rest[len(pack) :]
    blocks = arrivals(pack)
    owners = len(blocks)
    sel = arrival_pick(me[0], order_of(owners), D_EDGE // owners)
    raw = low(dot(sel, jnp.concatenate(blocks, axis=0)))
    raw_ref[...] = raw
    eye = ones_where(iota((D_EDGE, D_EDGE), 0) == iota((D_EDGE, D_EDGE), 1))
    state_t = dot_nt(eye, edge_state[...])
    block_forward(state_t, small_matrices(raw), graph, dst_row, out_refs)


def atom_forward(near, far, state, free, first, second):
    atom_in = low((near[...].astype(F32) + far[...].astype(F32)) * edge_scale)
    act, slope = silu_pair(dot(atom_in, first[...]))
    hidden = low(act)
    new_state = state + free * dot(hidden, second[...])
    return atom_in, hidden, slope, new_state


def edge_pre(sent, big, src_row, dst_row):
    src_t = low(dot_nt(big[:, 768:1024], sent))
    dst_t = low(dot_nt(big[:, 1024:1280], sent))
    atoms = sent.shape[0]
    step = min(512, atoms)
    total = None
    for start in range(0, atoms, step):
        part = dot(src_t[:, start : start + step], onehot(step, src_row[...], start))
        part = part + dot(dst_t[:, start : start + step], onehot(step, dst_row[...], start))
        total = part if total is None else total + part
    return total


def middle_half(near, far, big, first, second, mid_in, *refs):
    matrices, graph, src_row, dst_row = refs[:7], refs[7:14], refs[14], refs[15]
    old_state, old_free = refs[16:18]
    atom_in_ref, hidden_ref, slope_atom_ref, state_ref, sent_ref, free_ref, slope_edge_ref = refs[18:25]
    out_refs = refs[25:]
    free = old_free[...]
    free_ref[...] = free
    send(free_ref)
    atom_in, hidden, slope, state = atom_forward(
        near, far, old_state[...].astype(F32), free.astype(F32), first, second
    )
    atom_in_ref[...] = atom_in
    hidden_ref[...] = hidden
    slope_atom_ref[...] = low(slope)
    state_ref[...] = state
    sent = low(state)
    sent_ref[...] = sent
    send(atom_in_ref, hidden_ref, slope_atom_ref, state_ref, sent_ref)
    act, slope_edge = silu_pair(edge_pre(sent, big, src_row, dst_row))
    slope_edge_ref[...] = low(slope_edge)
    send(slope_edge_ref)
    block_forward(mid_in[...] + act, [m[...] for m in matrices], graph, dst_row, out_refs)


def edge_tables(
    grad_pre, big, first, second, src_row, dst_row, free, slope_atom, grad_atoms, gain_ref, update_ref,
    pushed_ref,
):
    atoms = free.shape[0]
    step = min(512, atoms)
    src_t, dst_t = big[:, 768:1024], big[:, 1024:1280]
    for start in range(0, atoms, step):
        rows = slice(start, start + step)
        pick_src = onehot(step, src_row[...], start)
        pick_dst = onehot(step, dst_row[...], start)
        part = dot(low(dot_nt(pick_src, grad_pre)), src_t) + dot(low(dot_nt(pick_dst, grad_pre)), dst_t)
        grad_atoms[rows] = grad_atoms[rows] + part
    update = low(grad_atoms[...] * free)
    update_ref[...] = update
    send(update_ref)
    pushed = low(dot_nt(update, second[...]) * slope_atom)
    pushed_ref[...] = pushed
    send(pushed_ref)
    gain_ref[...] = low(dot_nt(first[...], pushed))


def turn(
    me, near, far, big, first, second, src_row, dst_row, edge_cotangent, own, state_in, free_ref, mid_in,
    atom_in_ref, hidden_ref, sent_ref, edge_ref, atom_out_ref, cotangent_ref, grad_pre_ref, atoms_ref,
    gain_ref, update_ref, pushed_ref, hold,
):
    free = free_ref[...].astype(F32)
    begin(mid_in)
    atom_in, hidden, slope, state = atom_forward(near, far, state_in[...], free, first, second)
    atom_in_ref[...] = atom_in
    hidden_ref[...] = hidden
    sent = low(state)
    sent_ref[...] = sent
    send(atom_in_ref, hidden_ref, sent_ref)
    hold[...] = state
    count = atom_out_ref.shape[0]
    mine = pl.ds(pl.multiple_of(me[0] * count, count), count)
    atom_out_ref[...] = low(hold[mine])
    act, slope_edge = silu_pair(edge_pre(sent, big, src_row, dst_row))
    edge_ref[...] = mid_in[...] + act
    send(edge_ref, atom_out_ref)
    eye = ones_where(iota((D_EDGE, D_EDGE), 0) == iota((D_EDGE, D_EDGE), 1))
    cotangent = dot_nt(eye, edge_cotangent[...])
    cotangent_ref[...] = cotangent
    grad_pre = low(cotangent * slope_edge)
    grad_pre_ref[...] = grad_pre
    send(cotangent_ref, grad_pre_ref)
    atoms_ref[...] = jnp.zeros(atoms_ref.shape, F32)
    atoms_ref.ref[mine] = own[...].astype(F32)
    edge_tables(
        grad_pre, big, first, second, src_row, dst_row, free, slope, atoms_ref, gain_ref, update_ref,
        pushed_ref,
    )


def large_grads(update, pushed, grad_pre, src_row, dst_row, atom_in, hidden, sent, out_ref):
    for lanes, value in large_values(update, pushed, grad_pre, src_row, dst_row, atom_in, hidden, sent):
        out_ref[:, lanes] = value


def large_pieces(
    me, update, pushed, grad_pre, src_row, dst_row, atom_in, hidden, sent, small, out_ref, hold
):
    hold[:, :PAD] = small[...].astype(F32)
    for lanes, value in large_values(update, pushed, grad_pre, src_row, dst_row, atom_in, hidden, sent):
        hold[:, PAD + lanes.start : PAD + lanes.stop] = value.astype(F32)
    groups, _, width = out_ref.shape
    for g in range(groups):
        out_ref[g ^ me[1]] = low(hold[:, g * width : (g + 1) * width])


def large_values(update, pushed, grad_pre, src_row, dst_row, atom_in, hidden, sent):
    atoms = sent.shape[0]
    step = min(512, atoms)
    grads = grad_pre[...]
    update_t = low(jnp.transpose(update[...].astype(F32)))
    pushed_t = low(jnp.transpose(pushed[...].astype(F32)))
    grad_src = jnp.zeros((D_EDGE, D_ATOM), F32)
    grad_dst = jnp.zeros((D_EDGE, D_ATOM), F32)
    for start in range(0, atoms, step):
        rows = slice(start, start + step)
        sums = [low(dot_nt(grads, onehot(step, row[...], start))) for row in (src_row, dst_row)]
        grad_src = grad_src + dot(sums[0], sent[rows])
        grad_dst = grad_dst + dot(sums[1], sent[rows])
    grad_second_t = dot(update_t, hidden[...])
    grad_first_t = dot(pushed_t, atom_in[...])
    return [
        (slice(0, 256), put_double(grad_first_t)),
        (slice(256, 768), put_double(grad_second_t)),
        (slice(768, 1024), low(grad_src)),
        (slice(1024, 1280), low(grad_dst)),
    ]


def turned(value_ref, out_ref):
    out_ref[...] = jnp.transpose(value_ref[...]).astype(out_ref.dtype)


def block_backward(near, far, grad_in, *refs, more_refs=()):
    mid, tri_refs, edge_ref, quad_refs = refs[0], refs[1:6], refs[6], refs[7:12]
    up_tri, up_quad, down_tri, down_quad, radial_t = refs[12:17]
    radial_basis, tri_basis, quad_basis, tri_in, tri_out, quad_in, quad_out = refs[17:24]
    dst_row = refs[24]
    gain_t = low(near[...].astype(F32) + far[...].astype(F32))
    atoms = gain_t.shape[1]
    step = min(512, atoms)
    grad_message = None
    for start in range(0, atoms, step):
        part = dot(gain_t[:, start : start + step], onehot(step, dst_row[...], start))
        grad_message = part if grad_message is None else grad_message + part
    grad_message = grad_message * edge_scale
    radial = dot(radial_t[...], radial_basis[...])
    grad_mid = grad_in[...] + grad_message * radial
    grad_radial = low(grad_message * mid[...].astype(F32))
    begin(*tri_refs[2:], edge_ref)
    small = put_wide(dot_nt(grad_radial, radial_basis[...]), OFF_RADIAL)
    total = grad_mid
    for kept, basis, inner, outer, up, down, following in (
        (tri_refs, tri_basis, tri_in, tri_out, up_tri, down_tri, quad_refs),
        (quad_refs, quad_basis, quad_in, quad_out, up_quad, down_quad, more_refs),
    ):
        value, more = pair_backward(
            grad_mid, edge_ref, basis, inner, outer, up[...], down[...], *kept, following
        )
        total = total + value
        small = small + more
    return total, low(small)


BACK = 28


def back_last(*refs):
    _, grad_ref, all_ref, hold, sem = refs[BACK:]
    grad, small = block_backward(*refs[:BACK])
    hold[...] = small
    copy = pltpu.make_async_copy(hold, all_ref.at[:, :PAD], sem)
    copy.start()
    grad_ref[...] = grad
    copy.wait()


def back_middle(me, *refs):
    back, refs = refs[:BACK], refs[BACK:]
    big, first, second, src_row, slope_edge, free_ref, slope_atom, held = refs[:8]
    small_ref, gain_ref, update_ref, pushed_ref, grad_pre_ref, grad_ref = refs[8:14]
    *parts, grad_atoms = refs[14:]
    grad, small = block_backward(*back, more_refs=(slope_edge, free_ref, slope_atom, held))
    small_ref[...] = small
    grad_ref[...] = grad
    grad_pre = low(grad * slope_edge[...].astype(F32))
    grad_pre_ref[...] = grad_pre
    send(grad_ref, grad_pre_ref)
    grad_atoms[...] = held[...]
    edge_tables(
        grad_pre, big, first, second, src_row, back[-1], free_ref[...].astype(F32),
        slope_atom[...].astype(F32), grad_atoms, gain_ref, update_ref, pushed_ref,
    )
    quarter, count, _ = parts[0].shape
    for k, step in enumerate(scatter_order(4 * quarter)):
        rows = pl.ds(pl.multiple_of((me[0] ^ step) * count, count), count)
        parts[k // quarter][k % quarter] = low(grad_atoms[rows])


def total_of(arrived):
    total = arrived[0].astype(F32)
    for s in range(1, arrived.shape[0]):
        total = total + arrived[s].astype(F32)
    return total


def sum_list(pieces):
    total = pieces[0][...].astype(F32)
    for piece in pieces[1:]:
        total = total + piece[...].astype(F32)
    return total


def sum_pieces(*refs):
    *pieces, out_ref = refs
    out_ref[:, :PAD] = jnp.zeros((out_ref.shape[0], PAD), BF16)
    out_ref[:, PAD:] = low(sum_list(pieces))
    send(out_ref)


def sum_parts(one, two, out_ref):
    width = one.shape[2]
    out_ref[:, :width] = low(total_of(one))
    out_ref[:, width:] = low(total_of(two))


def adam(me, weights, first, second, *refs):
    *pieces, grad_ref, weights_ref, first_ref, second_ref, low_ref, hold = refs
    groups, _, lanes = hold.shape
    total = sum_list(pieces)
    for k, piece in enumerate(pieces):
        hold[me[1] ^ k] = piece[:, PAD : PAD + lanes].astype(F32)
    joint = jnp.concatenate([hold[g] for g in range(groups)], axis=1)
    grad = jnp.concatenate(
        [total[:, :SMALL], joint[:, PAD:], joint[:, :SMALL], total[:, PAD + lanes :]], axis=1
    )
    grad_ref[...] = grad
    old = weights[...]
    new_first = beta_one * first[...] + (1.0 - beta_one) * grad
    new_second = beta_two * second[...] + (1.0 - beta_two) * grad * grad
    first_ref[...] = new_first
    second_ref[...] = new_second
    first_hat = new_first / (1.0 - beta_one**adam_step)
    second_hat = new_second / (1.0 - beta_two**adam_step)
    new = old - learn_rate * (first_hat / (jnp.sqrt(second_hat) + epsilon) + decay_rate * old)
    weights_ref[...] = new
    low_ref[...] = low(new)


def exchange(pieces):
    return lax.all_to_all(pieces, "shard", split_axis=0, concat_axis=0)


def sum_pair(table, owners, beside=None):
    rounds = []
    step = 1
    while step < owners:
        rounds.append([step])
        step = 2 * step
    if len(rounds) > 2:
        rounds = [[1, 2, 3]] + rounds[2:]
    for steps in rounds[:-1]:
        others = [moved(table, k, owners) for k in steps]
        if beside is not None:
            table, beside = lax.optimization_barrier((table, beside))
        total = table.astype(F32)
        for other in others:
            total = total + other.astype(F32)
        table = total.astype(BF16)
    return table, moved(table, rounds[-1][0], owners), beside


def moved(table, step, owners, axis="shard"):
    return lax.ppermute(table, axis, [(i, i ^ step) for i in range(owners)])


def per_device(
    edge_state, atom_state, radial_basis, triplet_basis, quad_basis, dst_owner, dst_local, src_owner,
    src_local, triplet_in, triplet_out, quad_in, quad_out, fixed_atoms, edge_cotangent,
    atom_cotangent, weights, first_moment, second_moment,
):
    owners = lax.axis_size("shard")
    groups = lax.axis_size("group")
    edges = edge_state.shape[0]
    count = atom_state.shape[0]
    atoms = count * owners
    items = triplet_in.shape[0]
    me = jnp.stack([lax.axis_index("shard"), lax.axis_index("group")]).astype(jnp.int32)
    weights_t = jnp.transpose(weights)
    cols = weights_t.shape[0]
    lanes = (BIG + PAD) // groups
    def gathered(piece):
        arrays = [piece]
        for steps in gather_rounds(owners):
            held = arrays[0] if len(arrays) == 1 else jnp.concatenate(arrays, axis=0)
            arrays = arrays + [moved(held, step, owners) for step in steps]
        return arrays

    [pack] = call(
        pack_first,
        [sds((1, ROWS, PAD), BF16)],
        [weights_t],
        flops=10**7,
        raw=[0],
        scratch=[pltpu.VMEM((cols, PAD), F32), pltpu.SemaphoreType.DMA],
    )
    pack, state = lax.optimization_barrier((pack, atom_state))
    pack = gathered(pack)
    [cargo] = call(
        pack_cargo,
        [sds((1, count + ROWS * (1 + 2 * slots(lanes)), D_ATOM), BF16)],
        [me, weights_t, state, fixed_atoms.reshape(1, count)],
        flops=10**7,
        late=[1, 2, 3],
        smem=1,
        scratch=[(groups, cols, lanes)],
    )
    cargo = gathered(cargo)
    dst_row = (dst_owner[:, 0] * count + dst_local).reshape(1, edges)
    src_row = (src_owner[:, 0] * count + src_local).reshape(1, edges)
    graph = [
        jnp.transpose(radial_basis),
        jnp.transpose(triplet_basis),
        jnp.transpose(quad_basis),
        triplet_in.reshape(1, items),
        triplet_out.reshape(1, items),
        quad_in.reshape(1, items),
        quad_out.reshape(1, items),
    ]
    kept = kept_shapes(edges, items)
    table_shape = sds((atoms, D_EDGE), BF16)
    edge_shape = sds((D_EDGE, edges), BF16)
    edge_wide = sds((D_EDGE, edges), F32)
    atom_shape = sds((atoms, D_ATOM), BF16)
    atom_wide = sds((atoms, D_ATOM), F32)
    gain_shape = sds((D_EDGE, atoms), BF16)
    raw_one, *kept_one, table = call(
        first_half,
        [sds((D_EDGE, PAD), BF16)] + kept + [table_shape],
        [me, edge_state] + graph + [dst_row] + pack,
        flops=8 * 10**9,
        kept=range(1, 1 + KEPT),
        smem=1,
    )
    table, cargo = lax.optimization_barrier((table, cargo))
    lanes_shape = sds((D_EDGE, lanes), BF16)
    wide, big_two, old_state, old_free = call(
        collect,
        [lanes_shape, lanes_shape] + [sds((atoms, D_ATOM), BF16)] * 2,
        [me] + cargo,
        flops=10**7,
        smem=1,
    )
    near, far, _ = sum_pair(table, owners)

    def everywhere(piece):
        return [piece] + [moved(piece, k, groups, "group") for k in range(1, groups)]

    prepared = list(
        call(
            prepare_one,
            [sds(s, BF16) for s in PREPARED],
            [me, raw_one] + everywhere(wide),
            flops=10**9,
            smem=1,
            scratch=[(groups, D_EDGE, lanes)],
        )
    )
    back_one, small_two, back_two = prepared[:5], prepared[5:12], prepared[12:16] + [prepared[11]]
    first_one, second_one, big_one = prepared[16:]
    (
        atom_in_one, hidden_one, slope_one, state_one, sent_one, free, slope_edge_one, *kept_two, table,
    ) = call(
        middle_half,
        [table_shape, atom_shape, atom_shape, atom_wide, atom_shape, atom_shape, edge_shape]
        + kept
        + [table_shape],
        [near, far, big_one, first_one, second_one, kept_one[0]]
        + small_two
        + graph
        + [src_row, dst_row, old_state, old_free],
        flops=10 * 10**9,
        late=[5],
        kept=range(7 + KEPT),
    )
    near, far, _ = sum_pair(table, owners)
    near, state_one, kept_two[0] = lax.optimization_barrier((near, state_one, kept_two[0]))
    first_two, second_two, big_two = call(
        prepare_two,
        [sds(s, BF16) for s in LARGE_SHAPES],
        [me] + everywhere(big_two),
        flops=10**9,
        smem=1,
        scratch=[(groups, D_EDGE, lanes)],
    )
    (
        atom_in_two, hidden_two, sent_two, edge_out_t, atom_out, grad_t, grad_pre, grad_atoms, gain, update,
        pushed,
    ) = call(
        turn,
        [table_shape, atom_shape, atom_shape, edge_wide, sds((count, D_ATOM), BF16), edge_wide, edge_shape,
         atom_wide, gain_shape, atom_shape, atom_shape],
        [me, near, far, big_two, first_two, second_two, src_row, dst_row, edge_cotangent,
         atom_cotangent] + fetch([state_one, free, kept_two[0]]),
        flops=2 * 10**9,
        kept=[4, 5, 7],
        smem=1,
        scratch=[(atoms, D_ATOM)],
    )

    def rows_first(value_t, dtype):
        return call(turned, [sds((edges, D_EDGE), dtype)], [value_t], flops=10**8)[0]

    edge_out = rows_first(edge_out_t, BF16)
    near, far, (grads_two, edge_out) = sum_pair(
        gain,
        owners,
        (call(
            large_grads,
            [sds((D_EDGE, BIG), BF16)],
            [update, pushed, grad_pre, src_row, dst_row, atom_in_two, hidden_two, sent_two],
            flops=10**9,
        )[0], edge_out),
    )
    arrived_two = exchange(grads_two.reshape(owners, cols, BIG))
    fetched = fetch([grad_t] + kept_two[1:] + [slope_edge_one, free, slope_one, grad_atoms])
    half = owners // 4
    grad_small_two, gain, update, pushed, grad_pre, grad_t, *parts = call(
        back_middle,
        [sds((D_EDGE, PAD), BF16), gain_shape, atom_shape, atom_shape, edge_shape, edge_wide,
         *[sds((half, count, D_ATOM), BF16)] * 4],
        [me, near, far]
        + fetched[:KEPT]
        + back_two
        + graph
        + [dst_row, big_one, first_one, second_one, src_row]
        + fetched[KEPT:],
        flops=10 * 10**9,
        kept=[5],
        smem=1,
        scratch=[(atoms, D_ATOM)],
    )
    [pieces] = call(
        large_pieces,
        [sds((groups, D_EDGE, lanes), BF16)],
        [me, update, pushed, grad_pre, src_row, dst_row, atom_in_one, hidden_one, sent_one, grad_small_two],
        flops=10**9,
        late=[6, 7, 8],
        smem=1,
        scratch=[(D_EDGE, PAD + BIG)],
    )
    near, far, (pieces, arrived_two) = sum_pair(gain, owners, (pieces, arrived_two))
    pieces = [pieces[0]] + [moved(pieces[k], k, groups, "group") for k in range(1, groups)]
    [grads_one] = call(sum_pieces, [sds((D_EDGE, PAD + lanes), BF16)], pieces, flops=10**7, kept=[0])
    grads_one, grad_t = lax.optimization_barrier((grads_one, grad_t))
    mine = parts[0].astype(F32)
    for k in range(1, 4):
        mine = mine + moved(parts[k], k, owners).astype(F32)
    mine = mine.astype(BF16)
    step = 4
    while half > 2:
        high, mine = mine[half // 2 :], mine[: half // 2]
        mine = (mine.astype(F32) + moved(high, step, owners).astype(F32)).astype(BF16)
        half, step = half // 2, 2 * step
    grad_atom = mine[0].astype(F32) + moved(mine[1], step, owners).astype(F32)
    grad_edge_t, grads_one = call(
        back_last,
        [edge_wide, sds((D_EDGE, PAD + lanes), BF16)],
        [near, far] + fetch([grad_t] + kept_one[1:]) + back_one + graph + [dst_row, grads_one],
        flops=10 * 10**9,
        kept=[1],
        alias={BACK: 1},
        scratch=[pltpu.VMEM((D_EDGE, PAD), BF16), pltpu.SemaphoreType.DMA],
    )
    grad_edge = rows_first(grad_edge_t, F32)
    arrived_one = exchange(grads_one.reshape(owners, cols, PAD + lanes))
    [owned] = call(
        sum_parts, [sds((cols, PAD + lanes + BIG), BF16)], [arrived_one, arrived_two], flops=10**7
    )
    owned = [owned] + [moved(owned, k, groups, "group") for k in range(1, groups)]
    rows = weights.shape[0]
    results = call(
        adam,
        [sds((cols, rows), F32)] * 4 + [sds((cols, rows), BF16)],
        [me, weights_t, jnp.transpose(first_moment), jnp.transpose(second_moment)] + owned,
        flops=10**8,
        smem=1,
        scratch=[(groups, cols, lanes)],
    )
    return (edge_out, atom_out, grad_edge, grad_atom) + tuple(jnp.transpose(r) for r in results)


def solution(mesh):
    both = P(("group", "shard"), None)
    line = P(("group", "shard"))
    flat = P(None, "shard")
    in_specs = (both,) * 6 + (line, both) + (line,) * 6 + (both, both) + (flat,) * 3
    out_specs = (both,) * 4 + (flat,) * 5
    return jax.shard_map(
        per_device, mesh=mesh, in_specs=in_specs, out_specs=out_specs, check_vma=False
    )
```

```python
import jax
import jax.numpy as jnp
from jax import lax
from jax.experimental import pallas as pl
from jax.experimental.pallas import tpu as pltpu
from jax.sharding import PartitionSpec as P

D_EDGE = 128
D_ATOM = 256
D_TRI = 64
D_QUAD = 32
D_BASIS = 16
BLOCKS = 2
FOLD = 256
CHUNK = 1024
SMALL = 220
BIG = 1280
PAD = 256
ROWS = 16

edge_scale = 0.25
pair_scale = 0.5
beta_one = 0.5
beta_two = 0.5
learn_rate = 0.1
decay_rate = 0.01
epsilon = 1e-08
adam_step = 4

OFF_DOWN = {D_TRI: 0, D_QUAD: 136}
OFF_BASIS = {D_TRI: 64, D_QUAD: 168}
OFF_UP = {D_TRI: 72, D_QUAD: 172}
OFF_RADIAL = 204

F32 = jnp.float32
BF16 = jnp.bfloat16


def sds(shape, dtype):
    return jax.ShapeDtypeStruct(shape, dtype)


class Late:
    def __init__(self, source, ref, sem):
        self.ref, self.copy = ref, pltpu.make_async_copy(source, ref, sem)
        self.shape, self.begun, self.here = ref.shape, False, False

    def start(self):
        if not self.begun:
            self.copy.start()
            self.begun = True

    def wait(self):
        if not self.here:
            self.start()
            self.copy.wait()
            self.here = True

    def __getitem__(self, index):
        self.wait()
        return self.ref[index]


class Kept:
    def __init__(self, target, ref, sem):
        self.ref, self.copy, self.sent = ref, pltpu.make_async_copy(ref, target, sem), False
        self.shape, self.dtype = ref.shape, ref.dtype

    def __getitem__(self, index):
        return self.ref[index]

    def __setitem__(self, index, value):
        self.ref[index] = value

    def send(self):
        if not self.sent:
            self.copy.start()
            self.sent = True


def begin(*refs):
    for ref in refs:
        if isinstance(ref, Late):
            ref.start()


def arrive(*refs):
    for ref in refs:
        if isinstance(ref, Late):
            ref.wait()


def send(*refs):
    for ref in refs:
        if isinstance(ref, Kept):
            ref.send()


def call(body, outs, args, flops=10**9, late=(), kept=(), smem=0, scratch=(), early=None, alias=None, raw=()):
    alias = alias or {}
    held = [i for i in kept if i not in alias.values()]
    moved = [args[i] for i in late] + [outs[i] for i in held]

    def kernel(*refs):
        refs = list(refs)
        ins, rest = refs[: len(args)], refs[len(args) :]
        results, rest = rest[: len(outs)], rest[len(outs) :]
        extra, rest = rest[: len(scratch)], rest[len(scratch) :]
        buffers, sems = rest[: len(moved)], rest[len(moved) :]
        for k, i in enumerate(late):
            ins[i] = Late(ins[i], buffers[k], sems[k])
        begin(*[ins[i] for i in (late if early is None else early)])
        for k, i in enumerate(held, len(late)):
            results[i] = Kept(results[i], buffers[k], sems[k])
        body(*ins, *results, *extra)
        for i in late:
            ins[i].wait()
        for i in held:
            results[i].send()
        for i in held:
            results[i].copy.wait()

    args = [pltpu.with_memory_space_constraint(x, pltpu.HBM) if i in late or i in alias or i in raw else x for i, x in enumerate(args)]
    outs = [pltpu.HBM(x.shape, x.dtype) if i in kept else x for i, x in enumerate(outs)]
    space = [pltpu.SMEM] * smem + [pltpu.VMEM] * (len(args) - smem)
    for i in [*late, *alias, *raw]:
        space[i] = pltpu.HBM
    return pl.pallas_call(
        kernel,
        out_shape=outs,
        in_specs=[pl.BlockSpec(memory_space=s) for s in space],
        out_specs=[
            pl.BlockSpec(memory_space=pltpu.HBM if i in kept else pltpu.VMEM)
            for i in range(len(outs))
        ],
        scratch_shapes=[pltpu.VMEM(x, F32) if isinstance(x, tuple) else x for x in scratch]
        + [pltpu.VMEM(m.shape, m.dtype) for m in moved]
        + [pltpu.SemaphoreType.DMA] * len(moved),
        input_output_aliases=alias,
        compiler_params=pltpu.CompilerParams(vmem_limit_bytes=24 * 2**20),
        cost_estimate=pl.CostEstimate(flops=flops, bytes_accessed=2**20, transcendentals=0),
        name=body.__name__,
    )(*args)


def fetch(arrays):
    count = len(arrays)

    def kernel(*refs):
        copies = [
            pltpu.make_async_copy(refs[i], refs[count + i], refs[2 * count + i]) for i in range(count)
        ]
        for copy in copies:
            copy.start()
        for copy in copies:
            copy.wait()

    results = pl.pallas_call(
        kernel,
        out_shape=[sds(x.shape, x.dtype) for x in arrays],
        in_specs=[pl.BlockSpec(memory_space=pltpu.HBM)] * count,
        out_specs=[pl.BlockSpec(memory_space=pltpu.VMEM)] * count,
        scratch_shapes=[pltpu.SemaphoreType.DMA] * count,
        compiler_params=pltpu.CompilerParams(vmem_limit_bytes=2**20 * 20),
        cost_estimate=pl.CostEstimate(flops=10**9, bytes_accessed=2**20, transcendentals=0),
        name="fetch",
    )(*[pltpu.with_memory_space_constraint(x, pltpu.HBM) for x in arrays])
    return list(results)


def dot(a, b):
    return jnp.dot(a, b, preferred_element_type=F32)


def dot_nt(a, b):
    return lax.dot_general(a, b, (((1,), (1,)), ((), ())), preferred_element_type=F32)


def low(v):
    return v.astype(BF16)


def iota(shape, axis):
    return lax.broadcasted_iota(jnp.int32, shape, axis)


def ones_where(mask):
    return jnp.where(mask, 1.0, 0.0).astype(BF16)


def onehot(count, row, first=0):
    parts = []
    for start in range(0, count, 256):
        size = min(256, count - start)
        ids = iota((size, row.shape[1]), 0).astype(F32).astype(BF16)
        mask = ids == (row - (first + start)).astype(F32).astype(BF16)
        parts.append(jnp.where(mask, jnp.ones((), BF16), jnp.zeros((), BF16)))
    return parts[0] if len(parts) == 1 else jnp.concatenate(parts, axis=0)


def sigmoid(v):
    return 0.5 + 0.5 * jnp.tanh(0.5 * v)


def silu_pair(v):
    s = sigmoid(v)
    return v * s, s * (1.0 + v * (1.0 - s))


def cut(value, width):
    count = FOLD // width
    length = value.shape[1] // count
    return jnp.concatenate([value[:, g * length : (g + 1) * length] for g in range(count)], axis=0)


def uncut(value, width):
    count = FOLD // width
    return jnp.concatenate([value[g * width : (g + 1) * width] for g in range(count)], axis=1)


def pick(folded, high, width):
    result = folded[:width]
    for g in range(1, FOLD // width):
        result = jnp.where(high == g, folded[g * width : (g + 1) * width], result)
    return result


def spread(value, high, width):
    value = low(value)
    high = high.astype(F32).astype(BF16)
    return jnp.concatenate(
        [jnp.where(high == g, value, jnp.zeros((), BF16)) for g in range(FOLD // width)], axis=0
    )


def high_low(index, length):
    return index >> (length.bit_length() - 1), index & (length - 1)


def small_t(raw, offset, width, columns):
    count = 128 // width
    total = None
    for p in range(count):
        lane, d = iota((PAD, columns), 0), iota((PAD, columns), 1)
        high, rest = high_low(d, count)
        sel = ones_where((rest == p) & (lane == offset + high))
        part = dot(raw[p * width : (p + 1) * width], sel)
        total = part if total is None else total + part
    return low(total)


def small_plain(raw, offset, width, rows):
    count = 128 // width
    total = None
    for p in range(count):
        d, lane = iota((rows, PAD), 0), iota((rows, PAD), 1)
        high, rest = high_low(d, count)
        sel = ones_where((rest == p) & (lane == offset + high))
        part = dot_nt(sel, raw[p * width : (p + 1) * width])
        total = part if total is None else total + part
    return low(total)


def wide_t(raw, offset, rows):
    lane, d = iota((PAD, rows), 0), iota((PAD, rows), 1)
    return low(dot(raw, ones_where(lane == offset + d)))


def wide_plain(raw, offset, rows):
    d, lane = iota((rows, PAD), 0), iota((rows, PAD), 1)
    return low(dot_nt(ones_where(lane == offset + d), raw))


def double_plain(raw, rows):
    d, lane = iota((rows, 2 * rows), 0), iota((rows, 2 * rows), 1)
    return jnp.concatenate(
        [low(dot_nt(ones_where(lane == 2 * d + p), raw)) for p in range(2)], axis=1
    )


def put_small(grad_t, offset, width):
    count = 128 // width
    columns = grad_t.shape[1]
    value = low(grad_t)
    parts = []
    for p in range(count):
        d, lane = iota((columns, PAD), 0), iota((columns, PAD), 1)
        high, rest = high_low(d, count)
        sel = ones_where((rest == p) & (lane == offset + high))
        parts.append(dot(value, sel))
    return jnp.concatenate(parts, axis=0)


def put_wide(grad_t, offset):
    columns = grad_t.shape[1]
    d, lane = iota((columns, PAD), 0), iota((columns, PAD), 1)
    return dot(low(grad_t), ones_where(lane == offset + d))


def put_double(grad_t):
    rows = grad_t.shape[1]
    d, lane = iota((rows, 2 * rows), 0), iota((rows, 2 * rows), 1)
    value = low(grad_t)
    return low(
        dot(value[:128], ones_where(lane == 2 * d)) + dot(value[128:], ones_where(lane == 2 * d + 1))
    )


def small_matrices(raw):
    return (
        [small_t(raw, OFF_DOWN[w], w, D_EDGE) for w in (D_TRI, D_QUAD)]
        + [small_t(raw, OFF_BASIS[w], w, D_BASIS) for w in (D_TRI, D_QUAD)]
        + [wide_t(raw, OFF_UP[w], w) for w in (D_TRI, D_QUAD)]
        + [wide_t(raw, OFF_RADIAL, D_BASIS)]
    )


def back_matrices(raw):
    return [wide_plain(raw, OFF_UP[w], w) for w in (D_TRI, D_QUAD)] + [
        small_plain(raw, OFF_DOWN[w], w, D_EDGE) for w in (D_TRI, D_QUAD)
    ]


SMALL_SHAPES = [
    (D_TRI, D_EDGE), (D_QUAD, D_EDGE), (D_TRI, D_BASIS), (D_QUAD, D_BASIS), (D_EDGE, D_TRI),
    (D_EDGE, D_QUAD), (D_EDGE, D_BASIS),
]
BACK_SHAPES = [(D_TRI, D_EDGE), (D_QUAD, D_EDGE), (D_EDGE, D_TRI), (D_EDGE, D_QUAD)]


def slots(width):
    return -(-width // PAD)


def padded(value, rows, lanes):
    have, wide = value.shape
    if wide < lanes:
        value = jnp.concatenate([value, jnp.zeros((have, lanes - wide), value.dtype)], axis=1)
    if have < rows:
        value = jnp.concatenate([value, jnp.zeros((rows - have, lanes), value.dtype)], axis=0)
    return value


def pack_first(weights, out_ref, hold, sem):
    copy = pltpu.make_async_copy(weights.at[:, :PAD], hold, sem)
    copy.start()
    copy.wait()
    out_ref[0] = low(padded(hold[...], ROWS, PAD))


def pack_cargo(me, weights, state, fixed, out_ref, hold):
    count = state.shape[0]
    free = (1 - fixed[...]).astype(F32)
    out_ref[0, :count] = state[...]
    out_ref[0, count : count + ROWS] = low(padded(free, ROWS, PAD))
    values = weights[...]
    half = SMALL + BIG
    gap = jnp.zeros((values.shape[0], PAD - SMALL), F32)
    one = jnp.concatenate([values[:, SMALL : half + SMALL], gap], axis=1)
    two = padded(values[:, half + SMALL :], values.shape[0], BIG + PAD)
    groups, _, width = hold.shape
    base = count + ROWS
    for side in (one, two):
        for g in range(groups):
            hold[g] = side[:, g * width : (g + 1) * width]
        mine = padded(hold[me[1]], ROWS, slots(width) * PAD)
        for k in range(slots(width)):
            out_ref[0, base : base + ROWS] = low(mine[:, k * PAD : (k + 1) * PAD])
            base = base + ROWS


def order_of(owners):
    order = [0]
    for steps in gather_rounds(owners):
        order = order + [k ^ step for step in steps for k in order]
    return order


def gather_rounds(owners):
    rounds, step = [], owners // 2
    while step > 2:
        rounds.append([step])
        step = step // 2
    return rounds + ([[1, 2, 3]] if owners > 2 else [[1]])


def scatter_order(owners):
    order, step = [0], owners // 2
    while step > 2:
        order = order + [k ^ step for k in order]
        step = step // 2
    return [k ^ low_bits for low_bits in range(4) for k in order]


def arrivals(pieces):
    return [piece[i] for piece in pieces for i in range(piece.shape[0])]


def arrival_pick(me, order, cols):
    col = iota((1, len(order) * ROWS), 1)
    block, inside = high_low(col, ROWS)
    owner = jnp.zeros(col.shape, jnp.int32)
    for position, k in enumerate(order):
        owner = jnp.where(block == position, me ^ k, owner)
    return onehot(len(order) * cols, jnp.where(inside < cols, owner * cols + inside, -1))


def collect(me, *refs):
    *cargo, one_ref, two_ref, state_ref, free_ref = refs
    cargo = arrivals(cargo)
    owners = len(cargo)
    full, width = one_ref.shape
    count = state_ref.shape[0] // owners
    order = order_of(owners)
    sel = arrival_pick(me[0], order, full // owners)
    for side, ref in ((0, one_ref), (1, two_ref)):
        for k in range(slots(width)):
            start = count + ROWS * (1 + side * slots(width) + k)
            values = jnp.concatenate([c[start : start + ROWS] for c in cargo], axis=0)
            lanes = min(PAD, width - k * PAD)
            ref[:, k * PAD : k * PAD + lanes] = low(dot(sel, values))[:, :lanes]
    eye = iota((count, count), 0) == iota((count, count), 1)
    for piece, k in zip(cargo, order):
        rows = pl.ds(pl.multiple_of((me[0] ^ k) * count, count), count)
        state_ref[rows] = piece[:count]
        flag = piece[count : count + 1, :count].astype(F32)
        column = jnp.sum(jnp.where(eye, flag, 0.0), axis=1, keepdims=True)
        free_ref[rows] = low(jnp.broadcast_to(column, (count, D_ATOM)))


def joined(me, pieces, hold):
    for k, piece in enumerate(pieces):
        hold[me[1] ^ k] = piece[...].astype(F32)
    return low(jnp.concatenate([hold[g] for g in range(len(pieces))], axis=1))


def prepare_one(me, raw, *refs):
    *rest, hold = refs
    groups = hold.shape[0]
    wide = joined(me, rest[:groups], hold)
    raw_one = raw[...]
    raw_two = wide[:, BIG:]
    values = back_matrices(raw_one) + [wide_t(raw_one, OFF_RADIAL, D_BASIS)]
    values = values + small_matrices(raw_two) + back_matrices(raw_two)
    values = values + [double_plain(wide[:, :256], D_EDGE), double_plain(wide[:, 256:768], D_ATOM)]
    for ref, value in zip(rest[groups:], values + [wide[:, :BIG]]):
        ref[...] = value


def prepare_two(me, *refs):
    *rest, hold = refs
    groups = hold.shape[0]
    big = joined(me, rest[:groups], hold)
    first_ref, second_ref, big_ref = rest[groups:]
    first_ref[...] = double_plain(big[:, :256], D_EDGE)
    second_ref[...] = double_plain(big[:, 256:768], D_ATOM)
    big_ref[...] = big[:, :BIG]


LARGE_SHAPES = [(D_EDGE, D_ATOM), (D_ATOM, D_ATOM), (D_EDGE, BIG)]
PREPARED = BACK_SHAPES + [(D_EDGE, D_BASIS)] + SMALL_SHAPES + BACK_SHAPES + LARGE_SHAPES


def pair_forward(edge_t, basis_ref, in_ref, out_ref, down_t, basis_t, up_t, xg_ref, bt_ref):
    width, edges = down_t.shape[0], edge_t.shape[1]
    length = edges * width // FOLD
    act, slope_in = silu_pair(dot(down_t, edge_t))
    table = cut(low(act), width)
    total = jnp.zeros((FOLD, length), F32)
    items = in_ref.shape[1]
    chunk = min(CHUNK, items)
    for start in range(0, items, chunk):
        cols = slice(start, start + chunk)
        in_high, in_low = high_low(in_ref[:, cols], length)
        out_high, out_low = high_low(out_ref[:, cols], length)
        xg = pick(dot(table, onehot(length, in_low)), in_high, width)
        bt = dot(basis_t, basis_ref[:, cols])
        xg_ref[:, cols] = low(xg)
        bt_ref[:, cols] = low(bt)
        total = total + dot_nt(spread(xg * bt, out_high, width), onehot(length, out_low))
    send(xg_ref, bt_ref)
    agg_t = low(uncut(total, width) * pair_scale)
    value, slope_out = silu_pair(dot(up_t, agg_t))
    return value, slope_in, agg_t, slope_out


def pair_backward(
    grad_mid, edge_t, basis_ref, in_ref, out_ref, up, down, slope_out, agg_t, xg_ref, bt_ref, slope_in,
    following,
):
    width, edges = up.shape[0], slope_in.shape[1]
    length = edges * width // FOLD
    grad_out = low(grad_mid * slope_out[...].astype(F32))
    grad_up_t = dot_nt(grad_out, agg_t[...])
    table = cut(low(dot(up, grad_out) * pair_scale), width)
    begin(xg_ref, bt_ref)
    arrive(xg_ref, bt_ref)
    begin(*following)
    total = jnp.zeros((FOLD, length), F32)
    grad_basis_t = jnp.zeros((width, D_BASIS), F32)
    items = in_ref.shape[1]
    chunk = min(CHUNK, items)
    for start in range(0, items, chunk):
        cols = slice(start, start + chunk)
        in_high, in_low = high_low(in_ref[:, cols], length)
        out_high, out_low = high_low(out_ref[:, cols], length)
        gy = pick(dot(table, onehot(length, out_low)), out_high, width)
        grad_bt = low(gy * xg_ref[:, cols].astype(F32))
        grad_basis_t = grad_basis_t + dot_nt(grad_bt, basis_ref[:, cols])
        moved = gy * bt_ref[:, cols].astype(F32)
        total = total + dot_nt(spread(moved, in_high, width), onehot(length, in_low))
    grad_in = low(uncut(total, width) * slope_in[...].astype(F32))
    grad_down_t = dot_nt(grad_in, edge_t[...])
    small = (
        put_small(grad_down_t, OFF_DOWN[width], width)
        + put_small(grad_basis_t, OFF_BASIS[width], width)
        + put_wide(grad_up_t, OFF_UP[width])
    )
    return dot(down, grad_in), small


def block_forward(state_t, matrices, graph, dst_row, out_refs):
    radial_basis, tri_basis, quad_basis, tri_in, tri_out, quad_in, quad_out = graph
    down_tri, down_quad, basis_tri, basis_quad, up_tri, up_quad, radial_t = matrices
    mid_ref, mid_low_ref = out_refs[:2]
    tri_refs, edge_ref, quad_refs, table_ref = out_refs[2:7], out_refs[7], out_refs[8:13], out_refs[13]
    edge_t = low(state_t)
    edge_ref[...] = edge_t
    send(edge_ref)
    mid = state_t
    for refs, basis, inner, outer, down, basis_t, up in (
        (tri_refs, tri_basis, tri_in, tri_out, down_tri, basis_tri, up_tri),
        (quad_refs, quad_basis, quad_in, quad_out, down_quad, basis_quad, up_quad),
    ):
        slope_out_ref, agg_ref, xg_ref, bt_ref, slope_in_ref = refs
        value, slope_in, agg, slope_out = pair_forward(
            edge_t, basis, inner, outer, down, basis_t, up, xg_ref, bt_ref
        )
        slope_in_ref[...] = low(slope_in)
        agg_ref[...] = agg
        slope_out_ref[...] = low(slope_out)
        send(slope_in_ref, agg_ref, slope_out_ref)
        mid = mid + value
    mid_ref[...] = mid
    mid_low_ref[...] = low(mid)
    send(mid_ref, mid_low_ref)
    message = low(mid * dot(radial_t, radial_basis[...]))
    atoms = table_ref.shape[0]
    step = min(512, atoms)
    for start in range(0, atoms, step):
        rows = slice(start, start + step)
        table_ref[rows] = low(dot_nt(onehot(step, dst_row[...], start), message))


def kept_shapes(edges, items):
    edge = ((D_EDGE, edges), BF16)
    tri, quad = [
        [edge, ((w, edges), BF16), ((w, items), BF16), ((w, items), BF16), ((w, edges), BF16)]
        for w in (D_TRI, D_QUAD)
    ]
    return [sds(*x) for x in [((D_EDGE, edges), F32), edge] + tri + [edge] + quad]


KEPT = 13


def first_half(me, edge_state, *refs):
    graph, dst_row, rest = refs[:7], refs[7], refs[8:]
    pack = [ref for ref in rest if len(ref.shape) == 3]
    raw_ref, *out_refs = rest[len(pack) :]
    blocks = arrivals(pack)
    owners = len(blocks)
    sel = arrival_pick(me[0], order_of(owners), D_EDGE // owners)
    raw = low(dot(sel, jnp.concatenate(blocks, axis=0)))
    raw_ref[...] = raw
    eye = ones_where(iota((D_EDGE, D_EDGE), 0) == iota((D_EDGE, D_EDGE), 1))
    state_t = dot_nt(eye, edge_state[...])
    block_forward(state_t, small_matrices(raw), graph, dst_row, out_refs)


def atom_forward(near, far, state, free, first, second):
    atom_in = low((near[...].astype(F32) + far[...].astype(F32)) * edge_scale)
    act, slope = silu_pair(dot(atom_in, first[...]))
    hidden = low(act)
    new_state = state + free * dot(hidden, second[...])
    return atom_in, hidden, slope, new_state


def edge_pre(sent, big, src_row, dst_row):
    src_t = low(dot_nt(big[:, 768:1024], sent))
    dst_t = low(dot_nt(big[:, 1024:1280], sent))
    atoms = sent.shape[0]
    step = min(512, atoms)
    total = None
    for start in range(0, atoms, step):
        part = dot(src_t[:, start : start + step], onehot(step, src_row[...], start))
        part = part + dot(dst_t[:, start : start + step], onehot(step, dst_row[...], start))
        total = part if total is None else total + part
    return total


def middle_half(near, far, big, first, second, mid_in, *refs):
    matrices, graph, src_row, dst_row = refs[:7], refs[7:14], refs[14], refs[15]
    old_state, old_free = refs[16:18]
    atom_in_ref, hidden_ref, slope_atom_ref, state_ref, sent_ref, free_ref, slope_edge_ref = refs[18:25]
    out_refs = refs[25:]
    free = old_free[...]
    free_ref[...] = free
    send(free_ref)
    atom_in, hidden, slope, state = atom_forward(
        near, far, old_state[...].astype(F32), free.astype(F32), first, second
    )
    atom_in_ref[...] = atom_in
    hidden_ref[...] = hidden
    slope_atom_ref[...] = low(slope)
    state_ref[...] = state
    sent = low(state)
    sent_ref[...] = sent
    send(atom_in_ref, hidden_ref, slope_atom_ref, state_ref, sent_ref)
    act, slope_edge = silu_pair(edge_pre(sent, big, src_row, dst_row))
    slope_edge_ref[...] = low(slope_edge)
    send(slope_edge_ref)
    block_forward(mid_in[...] + act, [m[...] for m in matrices], graph, dst_row, out_refs)


def edge_tables(
    grad_pre, big, first, second, src_row, dst_row, free, slope_atom, grad_atoms, gain_ref, update_ref,
    pushed_ref,
):
    atoms = free.shape[0]
    step = min(512, atoms)
    src_t, dst_t = big[:, 768:1024], big[:, 1024:1280]
    for start in range(0, atoms, step):
        rows = slice(start, start + step)
        pick_src = onehot(step, src_row[...], start)
        pick_dst = onehot(step, dst_row[...], start)
        part = dot(low(dot_nt(pick_src, grad_pre)), src_t) + dot(low(dot_nt(pick_dst, grad_pre)), dst_t)
        grad_atoms[rows] = grad_atoms[rows] + part
    update = low(grad_atoms[...] * free)
    update_ref[...] = update
    send(update_ref)
    pushed = low(dot_nt(update, second[...]) * slope_atom)
    pushed_ref[...] = pushed
    send(pushed_ref)
    gain_ref[...] = low(dot_nt(first[...], pushed))


def turn(
    me, near, far, big, first, second, src_row, dst_row, edge_cotangent, own, state_in, free_ref, mid_in,
    atom_in_ref, hidden_ref, sent_ref, edge_ref, atom_out_ref, cotangent_ref, grad_pre_ref, atoms_ref,
    gain_ref, update_ref, pushed_ref, hold,
):
    free = free_ref[...].astype(F32)
    begin(mid_in)
    atom_in, hidden, slope, state = atom_forward(near, far, state_in[...], free, first, second)
    atom_in_ref[...] = atom_in
    hidden_ref[...] = hidden
    sent = low(state)
    sent_ref[...] = sent
    send(atom_in_ref, hidden_ref, sent_ref)
    hold[...] = state
    count = atom_out_ref.shape[0]
    mine = pl.ds(pl.multiple_of(me[0] * count, count), count)
    atom_out_ref[...] = low(hold[mine])
    act, slope_edge = silu_pair(edge_pre(sent, big, src_row, dst_row))
    edge_ref[...] = mid_in[...] + act
    send(edge_ref, atom_out_ref)
    eye = ones_where(iota((D_EDGE, D_EDGE), 0) == iota((D_EDGE, D_EDGE), 1))
    cotangent = dot_nt(eye, edge_cotangent[...])
    cotangent_ref[...] = cotangent
    grad_pre = low(cotangent * slope_edge)
    grad_pre_ref[...] = grad_pre
    send(cotangent_ref, grad_pre_ref)
    atoms_ref[...] = jnp.zeros(atoms_ref.shape, F32)
    atoms_ref.ref[mine] = own[...].astype(F32)
    edge_tables(
        grad_pre, big, first, second, src_row, dst_row, free, slope, atoms_ref, gain_ref, update_ref,
        pushed_ref,
    )


def large_grads(update, pushed, grad_pre, src_row, dst_row, atom_in, hidden, sent, out_ref):
    for lanes, value in large_values(update, pushed, grad_pre, src_row, dst_row, atom_in, hidden, sent):
        out_ref[:, lanes] = value


def large_pieces(
    me, update, pushed, grad_pre, src_row, dst_row, atom_in, hidden, sent, small, out_ref, hold
):
    hold[:, :PAD] = small[...].astype(F32)
    for lanes, value in large_values(update, pushed, grad_pre, src_row, dst_row, atom_in, hidden, sent):
        hold[:, PAD + lanes.start : PAD + lanes.stop] = value.astype(F32)
    groups, _, width = out_ref.shape
    for g in range(groups):
        out_ref[g ^ me[1]] = low(hold[:, g * width : (g + 1) * width])


def large_values(update, pushed, grad_pre, src_row, dst_row, atom_in, hidden, sent):
    atoms = sent.shape[0]
    step = min(512, atoms)
    grads = grad_pre[...]
    update_t = low(jnp.transpose(update[...].astype(F32)))
    pushed_t = low(jnp.transpose(pushed[...].astype(F32)))
    grad_src = jnp.zeros((D_EDGE, D_ATOM), F32)
    grad_dst = jnp.zeros((D_EDGE, D_ATOM), F32)
    for start in range(0, atoms, step):
        rows = slice(start, start + step)
        sums = [low(dot_nt(grads, onehot(step, row[...], start))) for row in (src_row, dst_row)]
        grad_src = grad_src + dot(sums[0], sent[rows])
        grad_dst = grad_dst + dot(sums[1], sent[rows])
    grad_second_t = dot(update_t, hidden[...])
    grad_first_t = dot(pushed_t, atom_in[...])
    return [
        (slice(0, 256), put_double(grad_first_t)),
        (slice(256, 768), put_double(grad_second_t)),
        (slice(768, 1024), low(grad_src)),
        (slice(1024, 1280), low(grad_dst)),
    ]


def turned(value_ref, out_ref):
    out_ref[...] = jnp.transpose(value_ref[...]).astype(out_ref.dtype)


def block_backward(near, far, grad_in, *refs, more_refs=()):
    mid, tri_refs, edge_ref, quad_refs = refs[0], refs[1:6], refs[6], refs[7:12]
    up_tri, up_quad, down_tri, down_quad, radial_t = refs[12:17]
    radial_basis, tri_basis, quad_basis, tri_in, tri_out, quad_in, quad_out = refs[17:24]
    dst_row = refs[24]
    gain_t = low(near[...].astype(F32) + far[...].astype(F32))
    atoms = gain_t.shape[1]
    step = min(512, atoms)
    grad_message = None
    for start in range(0, atoms, step):
        part = dot(gain_t[:, start : start + step], onehot(step, dst_row[...], start))
        grad_message = part if grad_message is None else grad_message + part
    grad_message = grad_message * edge_scale
    radial = dot(radial_t[...], radial_basis[...])
    grad_mid = grad_in[...] + grad_message * radial
    grad_radial = low(grad_message * mid[...].astype(F32))
    begin(*tri_refs[2:], edge_ref)
    small = put_wide(dot_nt(grad_radial, radial_basis[...]), OFF_RADIAL)
    total = grad_mid
    for kept, basis, inner, outer, up, down, following in (
        (tri_refs, tri_basis, tri_in, tri_out, up_tri, down_tri, quad_refs),
        (quad_refs, quad_basis, quad_in, quad_out, up_quad, down_quad, more_refs),
    ):
        value, more = pair_backward(
            grad_mid, edge_ref, basis, inner, outer, up[...], down[...], *kept, following
        )
        total = total + value
        small = small + more
    return total, low(small)


BACK = 28


def back_last(*refs):
    _, grad_ref, all_ref, hold, sem = refs[BACK:]
    grad, small = block_backward(*refs[:BACK])
    hold[...] = small
    copy = pltpu.make_async_copy(hold, all_ref.at[:, :PAD], sem)
    copy.start()
    grad_ref[...] = grad
    copy.wait()


def back_middle(me, *refs):
    back, refs = refs[:BACK], refs[BACK:]
    big, first, second, src_row, slope_edge, free_ref, slope_atom, held = refs[:8]
    small_ref, gain_ref, update_ref, pushed_ref, grad_pre_ref, grad_ref = refs[8:14]
    *parts, grad_atoms = refs[14:]
    grad, small = block_backward(*back, more_refs=(slope_edge, free_ref, slope_atom, held))
    small_ref[...] = small
    grad_ref[...] = grad
    grad_pre = low(grad * slope_edge[...].astype(F32))
    grad_pre_ref[...] = grad_pre
    send(grad_ref, grad_pre_ref)
    grad_atoms[...] = held[...]
    edge_tables(
        grad_pre, big, first, second, src_row, back[-1], free_ref[...].astype(F32),
        slope_atom[...].astype(F32), grad_atoms, gain_ref, update_ref, pushed_ref,
    )
    quarter, count, _ = parts[0].shape
    for k, step in enumerate(scatter_order(4 * quarter)):
        rows = pl.ds(pl.multiple_of((me[0] ^ step) * count, count), count)
        parts[k // quarter][k % quarter] = low(grad_atoms[rows])


def total_of(arrived):
    total = arrived[0].astype(F32)
    for s in range(1, arrived.shape[0]):
        total = total + arrived[s].astype(F32)
    return total


def sum_list(pieces):
    total = pieces[0][...].astype(F32)
    for piece in pieces[1:]:
        total = total + piece[...].astype(F32)
    return total


def sum_pieces(*refs):
    *pieces, out_ref = refs
    out_ref[:, :PAD] = jnp.zeros((out_ref.shape[0], PAD), BF16)
    out_ref[:, PAD:] = low(sum_list(pieces))
    send(out_ref)


def sum_parts(arrived, out_ref):
    out_ref[...] = low(total_of(arrived))


def adam(me, weights, first, second, *refs):
    *pieces, grad_ref, weights_ref, first_ref, second_ref, low_ref, hold = refs
    groups, _, lanes = hold.shape
    last, others = pieces[:groups], pieces[groups:]
    small = sum_list([piece[:, :PAD] for piece in last])
    for k, piece in enumerate(last):
        hold[me[1] ^ k] = piece[:, PAD:].astype(F32)
    joint = jnp.concatenate([hold[g] for g in range(groups)], axis=1)
    grad = jnp.concatenate(
        [small[:, :SMALL], joint[:, PAD:], joint[:, :SMALL], sum_list(others)], axis=1
    )
    grad_ref[...] = grad
    send(grad_ref)
    old = weights[...]
    new_first = beta_one * first[...] + (1.0 - beta_one) * grad
    new_second = beta_two * second[...] + (1.0 - beta_two) * grad * grad
    first_ref[...] = new_first
    second_ref[...] = new_second
    send(first_ref, second_ref)
    first_hat = new_first / (1.0 - beta_one**adam_step)
    second_hat = new_second / (1.0 - beta_two**adam_step)
    new = old - learn_rate * (first_hat / (jnp.sqrt(second_hat) + epsilon) + decay_rate * old)
    weights_ref[...] = new
    send(weights_ref)
    low_ref[...] = low(new)


def exchange(pieces):
    return lax.all_to_all(pieces, "shard", split_axis=0, concat_axis=0)


def sum_pair(table, owners, beside=None):
    rounds = []
    step = 1
    while step < owners:
        rounds.append([step])
        step = 2 * step
    if len(rounds) > 2:
        rounds = [[1, 2, 3]] + rounds[2:]
    for steps in rounds[:-1]:
        others = [moved(table, k, owners) for k in steps]
        if beside is not None:
            table, beside = lax.optimization_barrier((table, beside))
        total = table.astype(F32)
        for other in others:
            total = total + other.astype(F32)
        table = total.astype(BF16)
    return table, moved(table, rounds[-1][0], owners), beside


def moved(table, step, owners, axis="shard"):
    return lax.ppermute(table, axis, [(i, i ^ step) for i in range(owners)])


def per_device(
    edge_state, atom_state, radial_basis, triplet_basis, quad_basis, dst_owner, dst_local, src_owner,
    src_local, triplet_in, triplet_out, quad_in, quad_out, fixed_atoms, edge_cotangent,
    atom_cotangent, weights, first_moment, second_moment,
):
    owners = lax.axis_size("shard")
    groups = lax.axis_size("group")
    edges = edge_state.shape[0]
    count = atom_state.shape[0]
    atoms = count * owners
    items = triplet_in.shape[0]
    me = jnp.stack([lax.axis_index("shard"), lax.axis_index("group")]).astype(jnp.int32)
    weights_t = jnp.transpose(weights)
    cols = weights_t.shape[0]
    lanes = (BIG + PAD) // groups
    def gathered(piece):
        arrays = [piece]
        for steps in gather_rounds(owners):
            held = arrays[0] if len(arrays) == 1 else jnp.concatenate(arrays, axis=0)
            arrays = arrays + [moved(held, step, owners) for step in steps]
        return arrays

    [pack] = call(
        pack_first,
        [sds((1, ROWS, PAD), BF16)],
        [weights_t],
        flops=10**7,
        raw=[0],
        scratch=[pltpu.VMEM((cols, PAD), F32), pltpu.SemaphoreType.DMA],
    )
    pack, state = lax.optimization_barrier((pack, atom_state))
    pack = gathered(pack)
    [cargo] = call(
        pack_cargo,
        [sds((1, count + ROWS * (1 + 2 * slots(lanes)), D_ATOM), BF16)],
        [me, weights_t, state, fixed_atoms.reshape(1, count)],
        flops=10**7,
        late=[1, 2, 3],
        smem=1,
        scratch=[(groups, cols, lanes)],
    )
    cargo = gathered(cargo)
    dst_row = (dst_owner[:, 0] * count + dst_local).reshape(1, edges)
    src_row = (src_owner[:, 0] * count + src_local).reshape(1, edges)
    graph = [
        jnp.transpose(radial_basis),
        jnp.transpose(triplet_basis),
        jnp.transpose(quad_basis),
        triplet_in.reshape(1, items),
        triplet_out.reshape(1, items),
        quad_in.reshape(1, items),
        quad_out.reshape(1, items),
    ]
    kept = kept_shapes(edges, items)
    table_shape = sds((atoms, D_EDGE), BF16)
    edge_shape = sds((D_EDGE, edges), BF16)
    edge_wide = sds((D_EDGE, edges), F32)
    atom_shape = sds((atoms, D_ATOM), BF16)
    atom_wide = sds((atoms, D_ATOM), F32)
    gain_shape = sds((D_EDGE, atoms), BF16)
    raw_one, *kept_one, table = call(
        first_half,
        [sds((D_EDGE, PAD), BF16)] + kept + [table_shape],
        [me, edge_state] + graph + [dst_row] + pack,
        flops=8 * 10**9,
        kept=range(1, 1 + KEPT),
        smem=1,
    )
    table, cargo = lax.optimization_barrier((table, cargo))
    lanes_shape = sds((D_EDGE, lanes), BF16)
    wide, big_two, old_state, old_free = call(
        collect,
        [lanes_shape, lanes_shape] + [sds((atoms, D_ATOM), BF16)] * 2,
        [me] + cargo,
        flops=10**7,
        smem=1,
    )
    near, far, _ = sum_pair(table, owners)

    def everywhere(piece):
        return [piece] + [moved(piece, k, groups, "group") for k in range(1, groups)]

    prepared = list(
        call(
            prepare_one,
            [sds(s, BF16) for s in PREPARED],
            [me, raw_one] + everywhere(wide),
            flops=10**9,
            smem=1,
            scratch=[(groups, D_EDGE, lanes)],
        )
    )
    back_one, small_two, back_two = prepared[:5], prepared[5:12], prepared[12:16] + [prepared[11]]
    first_one, second_one, big_one = prepared[16:]
    (
        atom_in_one, hidden_one, slope_one, state_one, sent_one, free, slope_edge_one, *kept_two, table,
    ) = call(
        middle_half,
        [table_shape, atom_shape, atom_shape, atom_wide, atom_shape, atom_shape, edge_shape]
        + kept
        + [table_shape],
        [near, far, big_one, first_one, second_one, kept_one[0]]
        + small_two
        + graph
        + [src_row, dst_row, old_state, old_free],
        flops=10 * 10**9,
        late=[5],
        kept=range(7 + KEPT),
    )
    near, far, _ = sum_pair(table, owners)
    near, state_one, kept_two[0] = lax.optimization_barrier((near, state_one, kept_two[0]))
    first_two, second_two, big_two = call(
        prepare_two,
        [sds(s, BF16) for s in LARGE_SHAPES],
        [me] + everywhere(big_two),
        flops=10**9,
        smem=1,
        scratch=[(groups, D_EDGE, lanes)],
    )
    (
        atom_in_two, hidden_two, sent_two, edge_out_t, atom_out, grad_t, grad_pre, grad_atoms, gain, update,
        pushed,
    ) = call(
        turn,
        [table_shape, atom_shape, atom_shape, edge_wide, sds((count, D_ATOM), BF16), edge_wide, edge_shape,
         atom_wide, gain_shape, atom_shape, atom_shape],
        [me, near, far, big_two, first_two, second_two, src_row, dst_row, edge_cotangent,
         atom_cotangent] + fetch([state_one, free, kept_two[0]]),
        flops=2 * 10**9,
        kept=[4, 5, 7],
        smem=1,
        scratch=[(atoms, D_ATOM)],
    )

    def rows_first(value_t, dtype):
        return call(turned, [sds((edges, D_EDGE), dtype)], [value_t], flops=10**8)[0]

    edge_out = rows_first(edge_out_t, BF16)
    near, far, (grads_two, edge_out) = sum_pair(
        gain,
        owners,
        (call(
            large_grads,
            [sds((D_EDGE, BIG), BF16)],
            [update, pushed, grad_pre, src_row, dst_row, atom_in_two, hidden_two, sent_two],
            flops=10**9,
        )[0], edge_out),
    )
    arrived_two = exchange(grads_two.reshape(owners, cols, BIG))
    fetched = fetch([grad_t] + kept_two[1:] + [slope_edge_one, free, slope_one, grad_atoms])
    half = owners // 4
    grad_small_two, gain, update, pushed, grad_pre, grad_t, *parts = call(
        back_middle,
        [sds((D_EDGE, PAD), BF16), gain_shape, atom_shape, atom_shape, edge_shape, edge_wide,
         *[sds((half, count, D_ATOM), BF16)] * 4],
        [me, near, far]
        + fetched[:KEPT]
        + back_two
        + graph
        + [dst_row, big_one, first_one, second_one, src_row]
        + fetched[KEPT:],
        flops=10 * 10**9,
        kept=[5],
        smem=1,
        scratch=[(atoms, D_ATOM)],
    )
    [pieces] = call(
        large_pieces,
        [sds((groups, D_EDGE, lanes), BF16)],
        [me, update, pushed, grad_pre, src_row, dst_row, atom_in_one, hidden_one, sent_one, grad_small_two],
        flops=10**9,
        late=[6, 7, 8],
        smem=1,
        scratch=[(D_EDGE, PAD + BIG)],
    )
    near, far, (pieces, arrived_two) = sum_pair(gain, owners, (pieces, arrived_two))
    pieces = [pieces[0]] + [moved(pieces[k], k, groups, "group") for k in range(1, groups)]
    [grads_one] = call(sum_pieces, [sds((D_EDGE, PAD + lanes), BF16)], pieces, flops=10**7, kept=[0])
    grads_one, grad_t = lax.optimization_barrier((grads_one, grad_t))
    mine = parts[0].astype(F32)
    for k in range(1, 4):
        mine = mine + moved(parts[k], k, owners).astype(F32)
    mine = mine.astype(BF16)
    step = 4
    while half > 2:
        high, mine = mine[half // 2 :], mine[: half // 2]
        mine = (mine.astype(F32) + moved(high, step, owners).astype(F32)).astype(BF16)
        half, step = half // 2, 2 * step
    grad_atom = mine[0].astype(F32) + moved(mine[1], step, owners).astype(F32)
    grad_edge_t, grads_one = call(
        back_last,
        [edge_wide, sds((D_EDGE, PAD + lanes), BF16)],
        [near, far] + fetch([grad_t] + kept_one[1:]) + back_one + graph + [dst_row, grads_one],
        flops=10 * 10**9,
        kept=[1],
        alias={BACK: 1},
        scratch=[pltpu.VMEM((D_EDGE, PAD), BF16), pltpu.SemaphoreType.DMA],
    )
    grad_edge = rows_first(grad_edge_t, F32)
    grads_one, arrived_two = lax.optimization_barrier((grads_one, arrived_two))
    arrived_one = exchange(grads_one.reshape(owners, cols, PAD + lanes))

    def owned(arrived):
        [total] = call(sum_parts, [sds(arrived.shape[1:], BF16)], [arrived], flops=10**7)
        return everywhere(total)

    pieces = owned(arrived_one) + owned(arrived_two)
    rows = weights.shape[0]
    results = call(
        adam,
        [sds((cols, rows), F32)] * 4 + [sds((cols, rows), BF16)],
        [me, weights_t, jnp.transpose(first_moment), jnp.transpose(second_moment)] + pieces,
        flops=10**8,
        kept=range(5),
        smem=1,
        scratch=[(groups, cols, lanes)],
    )
    return (edge_out, atom_out, grad_edge, grad_atom) + tuple(jnp.transpose(r) for r in results)


def solution(mesh):
    both = P(("group", "shard"), None)
    line = P(("group", "shard"))
    flat = P(None, "shard")
    in_specs = (both,) * 6 + (line, both) + (line,) * 6 + (both, both) + (flat,) * 3
    out_specs = (both,) * 4 + (flat,) * 5
    return jax.shard_map(
        per_device, mesh=mesh, in_specs=in_specs, out_specs=out_specs, check_vma=False
    )
```

```python
import jax
import jax.numpy as jnp
from jax import lax
from jax.experimental import pallas as pl
from jax.experimental.pallas import tpu as pltpu
from jax.sharding import PartitionSpec as P

D_EDGE = 128
D_ATOM = 256
D_TRI = 64
D_QUAD = 32
D_BASIS = 16
BLOCKS = 2
FOLD = 256
CHUNK = 1024
SMALL = 220
BIG = 1280
PAD = 256
ROWS = 16

edge_scale = 0.25
pair_scale = 0.5
beta_one = 0.5
beta_two = 0.5
learn_rate = 0.1
decay_rate = 0.01
epsilon = 1e-08
adam_step = 4

OFF_DOWN = {D_TRI: 0, D_QUAD: 136}
OFF_BASIS = {D_TRI: 64, D_QUAD: 168}
OFF_UP = {D_TRI: 72, D_QUAD: 172}
OFF_RADIAL = 204

F32 = jnp.float32
BF16 = jnp.bfloat16


def sds(shape, dtype):
    return jax.ShapeDtypeStruct(shape, dtype)


class Late:
    def __init__(self, source, ref, sem):
        self.ref, self.copy = ref, pltpu.make_async_copy(source, ref, sem)
        self.shape, self.begun, self.here = ref.shape, False, False

    def start(self):
        if not self.begun:
            self.copy.start()
            self.begun = True

    def wait(self):
        if not self.here:
            self.start()
            self.copy.wait()
            self.here = True

    def __getitem__(self, index):
        self.wait()
        return self.ref[index]


class Kept:
    def __init__(self, target, ref, sem):
        self.ref, self.copy, self.sent = ref, pltpu.make_async_copy(ref, target, sem), False
        self.shape, self.dtype = ref.shape, ref.dtype

    def __getitem__(self, index):
        return self.ref[index]

    def __setitem__(self, index, value):
        self.ref[index] = value

    def send(self):
        if not self.sent:
            self.copy.start()
            self.sent = True


def begin(*refs):
    for ref in refs:
        if isinstance(ref, Late):
            ref.start()


def arrive(*refs):
    for ref in refs:
        if isinstance(ref, Late):
            ref.wait()


def send(*refs):
    for ref in refs:
        if isinstance(ref, Kept):
            ref.send()


def call(body, outs, args, flops=10**9, late=(), kept=(), smem=0, scratch=(), early=None, alias=None, raw=()):
    alias = alias or {}
    held = [i for i in kept if i not in alias.values()]
    moved = [args[i] for i in late] + [outs[i] for i in held]

    def kernel(*refs):
        refs = list(refs)
        ins, rest = refs[: len(args)], refs[len(args) :]
        results, rest = rest[: len(outs)], rest[len(outs) :]
        extra, rest = rest[: len(scratch)], rest[len(scratch) :]
        buffers, sems = rest[: len(moved)], rest[len(moved) :]
        for k, i in enumerate(late):
            ins[i] = Late(ins[i], buffers[k], sems[k])
        begin(*[ins[i] for i in (late if early is None else early)])
        for k, i in enumerate(held, len(late)):
            results[i] = Kept(results[i], buffers[k], sems[k])
        body(*ins, *results, *extra)
        for i in late:
            ins[i].wait()
        for i in held:
            results[i].send()
        for i in held:
            results[i].copy.wait()

    args = [pltpu.with_memory_space_constraint(x, pltpu.HBM) if i in late or i in alias or i in raw else x for i, x in enumerate(args)]
    outs = [pltpu.HBM(x.shape, x.dtype) if i in kept else x for i, x in enumerate(outs)]
    space = [pltpu.SMEM] * smem + [pltpu.VMEM] * (len(args) - smem)
    for i in [*late, *alias, *raw]:
        space[i] = pltpu.HBM
    return pl.pallas_call(
        kernel,
        out_shape=outs,
        in_specs=[pl.BlockSpec(memory_space=s) for s in space],
        out_specs=[
            pl.BlockSpec(memory_space=pltpu.HBM if i in kept else pltpu.VMEM)
            for i in range(len(outs))
        ],
        scratch_shapes=[pltpu.VMEM(x, F32) if isinstance(x, tuple) else x for x in scratch]
        + [pltpu.VMEM(m.shape, m.dtype) for m in moved]
        + [pltpu.SemaphoreType.DMA] * len(moved),
        input_output_aliases=alias,
        compiler_params=pltpu.CompilerParams(vmem_limit_bytes=24 * 2**20),
        cost_estimate=pl.CostEstimate(flops=flops, bytes_accessed=2**20, transcendentals=0),
        name=body.__name__,
    )(*args)


def fetch(arrays):
    count = len(arrays)

    def kernel(*refs):
        copies = [
            pltpu.make_async_copy(refs[i], refs[count + i], refs[2 * count + i]) for i in range(count)
        ]
        for copy in copies:
            copy.start()
        for copy in copies:
            copy.wait()

    results = pl.pallas_call(
        kernel,
        out_shape=[sds(x.shape, x.dtype) for x in arrays],
        in_specs=[pl.BlockSpec(memory_space=pltpu.HBM)] * count,
        out_specs=[pl.BlockSpec(memory_space=pltpu.VMEM)] * count,
        scratch_shapes=[pltpu.SemaphoreType.DMA] * count,
        compiler_params=pltpu.CompilerParams(vmem_limit_bytes=2**20 * 20),
        cost_estimate=pl.CostEstimate(flops=10**9, bytes_accessed=2**20, transcendentals=0),
        name="fetch",
    )(*[pltpu.with_memory_space_constraint(x, pltpu.HBM) for x in arrays])
    return list(results)


def dot(a, b):
    return jnp.dot(a, b, preferred_element_type=F32)


def dot_nt(a, b):
    return lax.dot_general(a, b, (((1,), (1,)), ((), ())), preferred_element_type=F32)


def low(v):
    return v.astype(BF16)


def iota(shape, axis):
    return lax.broadcasted_iota(jnp.int32, shape, axis)


def ones_where(mask):
    return jnp.where(mask, 1.0, 0.0).astype(BF16)


def onehot(count, row, first=0):
    parts = []
    for start in range(0, count, 256):
        size = min(256, count - start)
        ids = iota((size, row.shape[1]), 0).astype(F32).astype(BF16)
        mask = ids == (row - (first + start)).astype(F32).astype(BF16)
        parts.append(jnp.where(mask, jnp.ones((), BF16), jnp.zeros((), BF16)))
    return parts[0] if len(parts) == 1 else jnp.concatenate(parts, axis=0)


def sigmoid(v):
    return 0.5 + 0.5 * jnp.tanh(0.5 * v)


def silu_pair(v):
    s = sigmoid(v)
    return v * s, s * (1.0 + v * (1.0 - s))


def cut(value, width):
    count = FOLD // width
    length = value.shape[1] // count
    return jnp.concatenate([value[:, g * length : (g + 1) * length] for g in range(count)], axis=0)


def uncut(value, width):
    count = FOLD // width
    return jnp.concatenate([value[g * width : (g + 1) * width] for g in range(count)], axis=1)


def pick(folded, high, width):
    result = folded[:width]
    for g in range(1, FOLD // width):
        result = jnp.where(high == g, folded[g * width : (g + 1) * width], result)
    return result


def spread(value, high, width):
    value = low(value)
    high = high.astype(F32).astype(BF16)
    return jnp.concatenate(
        [jnp.where(high == g, value, jnp.zeros((), BF16)) for g in range(FOLD // width)], axis=0
    )


def high_low(index, length):
    return index >> (length.bit_length() - 1), index & (length - 1)


def small_t(raw, offset, width, columns):
    count = 128 // width
    total = None
    for p in range(count):
        lane, d = iota((PAD, columns), 0), iota((PAD, columns), 1)
        high, rest = high_low(d, count)
        sel = ones_where((rest == p) & (lane == offset + high))
        part = dot(raw[p * width : (p + 1) * width], sel)
        total = part if total is None else total + part
    return low(total)


def small_plain(raw, offset, width, rows):
    count = 128 // width
    total = None
    for p in range(count):
        d, lane = iota((rows, PAD), 0), iota((rows, PAD), 1)
        high, rest = high_low(d, count)
        sel = ones_where((rest == p) & (lane == offset + high))
        part = dot_nt(sel, raw[p * width : (p + 1) * width])
        total = part if total is None else total + part
    return low(total)


def wide_t(raw, offset, rows):
    lane, d = iota((PAD, rows), 0), iota((PAD, rows), 1)
    return low(dot(raw, ones_where(lane == offset + d)))


def wide_plain(raw, offset, rows):
    d, lane = iota((rows, PAD), 0), iota((rows, PAD), 1)
    return low(dot_nt(ones_where(lane == offset + d), raw))


def double_plain(raw, rows):
    d, lane = iota((rows, 2 * rows), 0), iota((rows, 2 * rows), 1)
    return jnp.concatenate(
        [low(dot_nt(ones_where(lane == 2 * d + p), raw)) for p in range(2)], axis=1
    )


def put_small(grad_t, offset, width):
    count = 128 // width
    columns = grad_t.shape[1]
    value = low(grad_t)
    parts = []
    for p in range(count):
        d, lane = iota((columns, PAD), 0), iota((columns, PAD), 1)
        high, rest = high_low(d, count)
        sel = ones_where((rest == p) & (lane == offset + high))
        parts.append(dot(value, sel))
    return jnp.concatenate(parts, axis=0)


def put_wide(grad_t, offset):
    columns = grad_t.shape[1]
    d, lane = iota((columns, PAD), 0), iota((columns, PAD), 1)
    return dot(low(grad_t), ones_where(lane == offset + d))


def put_double(grad_t):
    rows = grad_t.shape[1]
    d, lane = iota((rows, 2 * rows), 0), iota((rows, 2 * rows), 1)
    value = low(grad_t)
    return low(
        dot(value[:128], ones_where(lane == 2 * d)) + dot(value[128:], ones_where(lane == 2 * d + 1))
    )


def small_matrices(raw):
    return (
        [small_t(raw, OFF_DOWN[w], w, D_EDGE) for w in (D_TRI, D_QUAD)]
        + [small_t(raw, OFF_BASIS[w], w, D_BASIS) for w in (D_TRI, D_QUAD)]
        + [wide_t(raw, OFF_UP[w], w) for w in (D_TRI, D_QUAD)]
        + [wide_t(raw, OFF_RADIAL, D_BASIS)]
    )


def back_matrices(raw):
    return [wide_plain(raw, OFF_UP[w], w) for w in (D_TRI, D_QUAD)] + [
        small_plain(raw, OFF_DOWN[w], w, D_EDGE) for w in (D_TRI, D_QUAD)
    ]


SMALL_SHAPES = [
    (D_TRI, D_EDGE), (D_QUAD, D_EDGE), (D_TRI, D_BASIS), (D_QUAD, D_BASIS), (D_EDGE, D_TRI),
    (D_EDGE, D_QUAD), (D_EDGE, D_BASIS),
]
BACK_SHAPES = [(D_TRI, D_EDGE), (D_QUAD, D_EDGE), (D_EDGE, D_TRI), (D_EDGE, D_QUAD)]


def slots(width):
    return -(-width // PAD)


def padded(value, rows, lanes):
    have, wide = value.shape
    if wide < lanes:
        value = jnp.concatenate([value, jnp.zeros((have, lanes - wide), value.dtype)], axis=1)
    if have < rows:
        value = jnp.concatenate([value, jnp.zeros((rows - have, lanes), value.dtype)], axis=0)
    return value


def pack_first(weights, out_ref, hold, sem):
    copy = pltpu.make_async_copy(weights.at[:, :PAD], hold, sem)
    copy.start()
    copy.wait()
    out_ref[0] = low(padded(hold[...], ROWS, PAD))


def pack_cargo(
    me, weights, state, fixed, dst_owner, dst_local, src_owner, src_local, out_ref, dst_ref, src_ref, hold
):
    count = state.shape[0]
    free = (1 - fixed[...]).astype(F32)
    out_ref[0, :count] = state[...]
    out_ref[0, count : count + ROWS] = low(padded(free, ROWS, PAD))
    values = weights[...]
    half = SMALL + BIG
    gap = jnp.zeros((values.shape[0], PAD - SMALL), F32)
    one = jnp.concatenate([values[:, SMALL : half + SMALL], gap], axis=1)
    two = padded(values[:, half + SMALL :], values.shape[0], BIG + PAD)
    groups, _, width = hold.shape
    base = count + ROWS
    for side in (one, two):
        for g in range(groups):
            hold[g] = side[:, g * width : (g + 1) * width]
        mine = padded(hold[me[1]], ROWS, slots(width) * PAD)
        for k in range(slots(width)):
            out_ref[0, base : base + ROWS] = low(mine[:, k * PAD : (k + 1) * PAD])
            base = base + ROWS
    dst_ref[...] = dst_owner[...] * count + dst_local[...]
    src_ref[...] = src_owner[...] * count + src_local[...]


def order_of(owners):
    order = [0]
    for steps in gather_rounds(owners):
        order = order + [k ^ step for step in steps for k in order]
    return order


def gather_rounds(owners):
    rounds, step = [], owners // 2
    while step > 2:
        rounds.append([step])
        step = step // 2
    return rounds + ([[1, 2, 3]] if owners > 2 else [[1]])


def scatter_order(owners):
    order, step = [0], owners // 2
    while step > 2:
        order = order + [k ^ step for k in order]
        step = step // 2
    return [k ^ low_bits for low_bits in range(4) for k in order]


def arrivals(pieces):
    return [piece[i] for piece in pieces for i in range(piece.shape[0])]


def arrival_pick(me, order, cols):
    col = iota((1, len(order) * ROWS), 1)
    block, inside = high_low(col, ROWS)
    owner = jnp.zeros(col.shape, jnp.int32)
    for position, k in enumerate(order):
        owner = jnp.where(block == position, me ^ k, owner)
    return onehot(len(order) * cols, jnp.where(inside < cols, owner * cols + inside, -1))


def collect(me, *refs):
    *cargo, one_ref, two_ref, state_ref, free_ref = refs
    cargo = arrivals(cargo)
    owners = len(cargo)
    full, width = one_ref.shape
    count = state_ref.shape[0] // owners
    order = order_of(owners)
    sel = arrival_pick(me[0], order, full // owners)
    for side, ref in ((0, one_ref), (1, two_ref)):
        for k in range(slots(width)):
            start = count + ROWS * (1 + side * slots(width) + k)
            values = jnp.concatenate([c[start : start + ROWS] for c in cargo], axis=0)
            lanes = min(PAD, width - k * PAD)
            ref[:, k * PAD : k * PAD + lanes] = low(dot(sel, values))[:, :lanes]
    eye = iota((count, count), 0) == iota((count, count), 1)
    for piece, k in zip(cargo, order):
        rows = pl.ds(pl.multiple_of((me[0] ^ k) * count, count), count)
        state_ref[rows] = piece[:count]
        flag = piece[count : count + 1, :count].astype(F32)
        column = jnp.sum(jnp.where(eye, flag, 0.0), axis=1, keepdims=True)
        free_ref[rows] = low(jnp.broadcast_to(column, (count, D_ATOM)))


def joined(me, pieces, hold):
    for k, piece in enumerate(pieces):
        hold[me[1] ^ k] = piece[...].astype(F32)
    return low(jnp.concatenate([hold[g] for g in range(len(pieces))], axis=1))


def prepare_one(me, raw, *refs):
    *rest, hold = refs
    groups = hold.shape[0]
    wide = joined(me, rest[:groups], hold)
    raw_one = raw[...]
    raw_two = wide[:, BIG:]
    values = back_matrices(raw_one) + [wide_t(raw_one, OFF_RADIAL, D_BASIS)]
    values = values + small_matrices(raw_two) + back_matrices(raw_two)
    values = values + [double_plain(wide[:, :256], D_EDGE), double_plain(wide[:, 256:768], D_ATOM)]
    for ref, value in zip(rest[groups:], values + [wide[:, :BIG]]):
        ref[...] = value


def prepare_two(me, *refs):
    *rest, hold = refs
    groups = hold.shape[0]
    big = joined(me, rest[:groups], hold)
    first_ref, second_ref, big_ref = rest[groups:]
    first_ref[...] = double_plain(big[:, :256], D_EDGE)
    second_ref[...] = double_plain(big[:, 256:768], D_ATOM)
    big_ref[...] = big[:, :BIG]


LARGE_SHAPES = [(D_EDGE, D_ATOM), (D_ATOM, D_ATOM), (D_EDGE, BIG)]
PREPARED = BACK_SHAPES + [(D_EDGE, D_BASIS)] + SMALL_SHAPES + BACK_SHAPES + LARGE_SHAPES


def pair_forward(edge_t, basis_ref, in_ref, out_ref, down_t, basis_t, up_t, xg_ref, bt_ref):
    width, edges = down_t.shape[0], edge_t.shape[1]
    length = edges * width // FOLD
    act, slope_in = silu_pair(dot(down_t, edge_t))
    table = cut(low(act), width)
    total = jnp.zeros((FOLD, length), F32)
    items = in_ref.shape[1]
    chunk = min(CHUNK, items)
    for start in range(0, items, chunk):
        cols = slice(start, start + chunk)
        in_high, in_low = high_low(in_ref[:, cols], length)
        out_high, out_low = high_low(out_ref[:, cols], length)
        xg = pick(dot(table, onehot(length, in_low)), in_high, width)
        bt = dot(basis_t, basis_ref[:, cols])
        xg_ref[:, cols] = low(xg)
        bt_ref[:, cols] = low(bt)
        total = total + dot_nt(spread(xg * bt, out_high, width), onehot(length, out_low))
    send(xg_ref, bt_ref)
    agg_t = low(uncut(total, width) * pair_scale)
    value, slope_out = silu_pair(dot(up_t, agg_t))
    return value, slope_in, agg_t, slope_out


def pair_backward(
    grad_mid, edge_t, basis_ref, in_ref, out_ref, up, down, slope_out, agg_t, xg_ref, bt_ref, slope_in,
    following,
):
    width, edges = up.shape[0], slope_in.shape[1]
    length = edges * width // FOLD
    grad_out = low(grad_mid * slope_out[...].astype(F32))
    grad_up_t = dot_nt(grad_out, agg_t[...])
    table = cut(low(dot(up, grad_out) * pair_scale), width)
    begin(xg_ref, bt_ref)
    arrive(xg_ref, bt_ref)
    begin(*following)
    total = jnp.zeros((FOLD, length), F32)
    grad_basis_t = jnp.zeros((width, D_BASIS), F32)
    items = in_ref.shape[1]
    chunk = min(CHUNK, items)
    for start in range(0, items, chunk):
        cols = slice(start, start + chunk)
        in_high, in_low = high_low(in_ref[:, cols], length)
        out_high, out_low = high_low(out_ref[:, cols], length)
        gy = pick(dot(table, onehot(length, out_low)), out_high, width)
        grad_bt = low(gy * xg_ref[:, cols].astype(F32))
        grad_basis_t = grad_basis_t + dot_nt(grad_bt, basis_ref[:, cols])
        moved = gy * bt_ref[:, cols].astype(F32)
        total = total + dot_nt(spread(moved, in_high, width), onehot(length, in_low))
    grad_in = low(uncut(total, width) * slope_in[...].astype(F32))
    grad_down_t = dot_nt(grad_in, edge_t[...])
    small = (
        put_small(grad_down_t, OFF_DOWN[width], width)
        + put_small(grad_basis_t, OFF_BASIS[width], width)
        + put_wide(grad_up_t, OFF_UP[width])
    )
    return dot(down, grad_in), small


def block_forward(state_t, matrices, graph, dst_row, out_refs):
    radial_basis, tri_basis, quad_basis, tri_in, tri_out, quad_in, quad_out = graph
    down_tri, down_quad, basis_tri, basis_quad, up_tri, up_quad, radial_t = matrices
    mid_ref, mid_low_ref = out_refs[:2]
    tri_refs, edge_ref, quad_refs, table_ref = out_refs[2:7], out_refs[7], out_refs[8:13], out_refs[13]
    edge_t = low(state_t)
    edge_ref[...] = edge_t
    send(edge_ref)
    mid = state_t
    for refs, basis, inner, outer, down, basis_t, up in (
        (tri_refs, tri_basis, tri_in, tri_out, down_tri, basis_tri, up_tri),
        (quad_refs, quad_basis, quad_in, quad_out, down_quad, basis_quad, up_quad),
    ):
        slope_out_ref, agg_ref, xg_ref, bt_ref, slope_in_ref = refs
        value, slope_in, agg, slope_out = pair_forward(
            edge_t, basis, inner, outer, down, basis_t, up, xg_ref, bt_ref
        )
        slope_in_ref[...] = low(slope_in)
        agg_ref[...] = agg
        slope_out_ref[...] = low(slope_out)
        send(slope_in_ref, agg_ref, slope_out_ref)
        mid = mid + value
    mid_ref[...] = mid
    mid_low_ref[...] = low(mid)
    send(mid_ref, mid_low_ref)
    message = low(mid * dot(radial_t, radial_basis[...]))
    atoms = table_ref.shape[0]
    step = min(512, atoms)
    for start in range(0, atoms, step):
        rows = slice(start, start + step)
        table_ref[rows] = low(dot_nt(onehot(step, dst_row[...], start), message))


def kept_shapes(edges, items):
    edge = ((D_EDGE, edges), BF16)
    tri, quad = [
        [edge, ((w, edges), BF16), ((w, items), BF16), ((w, items), BF16), ((w, edges), BF16)]
        for w in (D_TRI, D_QUAD)
    ]
    return [sds(*x) for x in [((D_EDGE, edges), F32), edge] + tri + [edge] + quad]


KEPT = 13


def first_half(me, edge_state, *refs):
    graph, dst_row, rest = refs[:7], refs[7], refs[8:]
    pack = [ref for ref in rest if len(ref.shape) == 3]
    raw_ref, *out_refs = rest[len(pack) :]
    blocks = arrivals(pack)
    owners = len(blocks)
    sel = arrival_pick(me[0], order_of(owners), D_EDGE // owners)
    raw = low(dot(sel, jnp.concatenate(blocks, axis=0)))
    raw_ref[...] = raw
    eye = ones_where(iota((D_EDGE, D_EDGE), 0) == iota((D_EDGE, D_EDGE), 1))
    state_t = dot_nt(eye, edge_state[...])
    block_forward(state_t, small_matrices(raw), graph, dst_row, out_refs)


def atom_forward(near, far, state, free, first, second):
    atom_in = low((near[...].astype(F32) + far[...].astype(F32)) * edge_scale)
    act, slope = silu_pair(dot(atom_in, first[...]))
    hidden = low(act)
    new_state = state + free * dot(hidden, second[...])
    return atom_in, hidden, slope, new_state


def edge_pre(sent, big, src_row, dst_row):
    src_t = low(dot_nt(big[:, 768:1024], sent))
    dst_t = low(dot_nt(big[:, 1024:1280], sent))
    atoms = sent.shape[0]
    step = min(512, atoms)
    total = None
    for start in range(0, atoms, step):
        part = dot(src_t[:, start : start + step], onehot(step, src_row[...], start))
        part = part + dot(dst_t[:, start : start + step], onehot(step, dst_row[...], start))
        total = part if total is None else total + part
    return total


def middle_half(near, far, big, first, second, mid_in, *refs):
    matrices, graph, src_row, dst_row = refs[:7], refs[7:14], refs[14], refs[15]
    old_state, old_free = refs[16:18]
    atom_in_ref, hidden_ref, slope_atom_ref, state_ref, sent_ref, free_ref, slope_edge_ref = refs[18:25]
    out_refs = refs[25:]
    free = old_free[...]
    free_ref[...] = free
    send(free_ref)
    atom_in, hidden, slope, state = atom_forward(
        near, far, old_state[...].astype(F32), free.astype(F32), first, second
    )
    atom_in_ref[...] = atom_in
    hidden_ref[...] = hidden
    slope_atom_ref[...] = low(slope)
    state_ref[...] = state
    sent = low(state)
    sent_ref[...] = sent
    send(atom_in_ref, hidden_ref, slope_atom_ref, state_ref, sent_ref)
    act, slope_edge = silu_pair(edge_pre(sent, big, src_row, dst_row))
    slope_edge_ref[...] = low(slope_edge)
    send(slope_edge_ref)
    block_forward(mid_in[...] + act, [m[...] for m in matrices], graph, dst_row, out_refs)


def edge_tables(
    grad_pre, big, first, second, src_row, dst_row, free, slope_atom, grad_atoms, gain_ref, update_ref,
    pushed_ref,
):
    atoms = free.shape[0]
    step = min(512, atoms)
    src_t, dst_t = big[:, 768:1024], big[:, 1024:1280]
    for start in range(0, atoms, step):
        rows = slice(start, start + step)
        pick_src = onehot(step, src_row[...], start)
        pick_dst = onehot(step, dst_row[...], start)
        part = dot(low(dot_nt(pick_src, grad_pre)), src_t) + dot(low(dot_nt(pick_dst, grad_pre)), dst_t)
        grad_atoms[rows] = grad_atoms[rows] + part
    update = low(grad_atoms[...] * free)
    update_ref[...] = update
    send(update_ref)
    pushed = low(dot_nt(update, second[...]) * slope_atom)
    pushed_ref[...] = pushed
    send(pushed_ref)
    gain_ref[...] = low(dot_nt(first[...], pushed))


def turn(
    me, near, far, big, first, second, src_row, dst_row, edge_cotangent, own, state_in, free_ref, mid_in,
    atom_in_ref, hidden_ref, sent_ref, edge_ref, atom_out_ref, cotangent_ref, grad_pre_ref, atoms_ref,
    gain_ref, update_ref, pushed_ref, hold,
):
    free = free_ref[...].astype(F32)
    begin(mid_in)
    atom_in, hidden, slope, state = atom_forward(near, far, state_in[...], free, first, second)
    atom_in_ref[...] = atom_in
    hidden_ref[...] = hidden
    sent = low(state)
    sent_ref[...] = sent
    send(atom_in_ref, hidden_ref, sent_ref)
    hold[...] = state
    count = atom_out_ref.shape[0]
    mine = pl.ds(pl.multiple_of(me[0] * count, count), count)
    atom_out_ref[...] = low(hold[mine])
    act, slope_edge = silu_pair(edge_pre(sent, big, src_row, dst_row))
    edge_ref[...] = mid_in[...] + act
    send(edge_ref, atom_out_ref)
    eye = ones_where(iota((D_EDGE, D_EDGE), 0) == iota((D_EDGE, D_EDGE), 1))
    cotangent = dot_nt(eye, edge_cotangent[...])
    cotangent_ref[...] = cotangent
    grad_pre = low(cotangent * slope_edge)
    grad_pre_ref[...] = grad_pre
    send(cotangent_ref, grad_pre_ref)
    atoms_ref[...] = jnp.zeros(atoms_ref.shape, F32)
    atoms_ref.ref[mine] = own[...].astype(F32)
    edge_tables(
        grad_pre, big, first, second, src_row, dst_row, free, slope, atoms_ref, gain_ref, update_ref,
        pushed_ref,
    )


def large_grads(update, pushed, grad_pre, src_row, dst_row, atom_in, hidden, sent, out_ref):
    for lanes, value in large_values(update, pushed, grad_pre, src_row, dst_row, atom_in, hidden, sent):
        out_ref[:, lanes] = value


def large_pieces(
    me, update, pushed, grad_pre, src_row, dst_row, atom_in, hidden, sent, small, out_ref, hold
):
    hold[:, :PAD] = small[...].astype(F32)
    for lanes, value in large_values(update, pushed, grad_pre, src_row, dst_row, atom_in, hidden, sent):
        hold[:, PAD + lanes.start : PAD + lanes.stop] = value.astype(F32)
    groups, _, width = out_ref.shape
    for g in range(groups):
        out_ref[g ^ me[1]] = low(hold[:, g * width : (g + 1) * width])


def large_values(update, pushed, grad_pre, src_row, dst_row, atom_in, hidden, sent):
    atoms = sent.shape[0]
    step = min(512, atoms)
    grads = grad_pre[...]
    update_t = low(jnp.transpose(update[...].astype(F32)))
    pushed_t = low(jnp.transpose(pushed[...].astype(F32)))
    grad_src = jnp.zeros((D_EDGE, D_ATOM), F32)
    grad_dst = jnp.zeros((D_EDGE, D_ATOM), F32)
    for start in range(0, atoms, step):
        rows = slice(start, start + step)
        sums = [low(dot_nt(grads, onehot(step, row[...], start))) for row in (src_row, dst_row)]
        grad_src = grad_src + dot(sums[0], sent[rows])
        grad_dst = grad_dst + dot(sums[1], sent[rows])
    grad_second_t = dot(update_t, hidden[...])
    grad_first_t = dot(pushed_t, atom_in[...])
    return [
        (slice(0, 256), put_double(grad_first_t)),
        (slice(256, 768), put_double(grad_second_t)),
        (slice(768, 1024), low(grad_src)),
        (slice(1024, 1280), low(grad_dst)),
    ]


def turned(value_ref, out_ref):
    out_ref[...] = jnp.transpose(value_ref[...]).astype(out_ref.dtype)


def block_backward(near, far, grad_in, *refs, more_refs=()):
    mid, tri_refs, edge_ref, quad_refs = refs[0], refs[1:6], refs[6], refs[7:12]
    up_tri, up_quad, down_tri, down_quad, radial_t = refs[12:17]
    radial_basis, tri_basis, quad_basis, tri_in, tri_out, quad_in, quad_out = refs[17:24]
    dst_row = refs[24]
    gain_t = low(near[...].astype(F32) + far[...].astype(F32))
    atoms = gain_t.shape[1]
    step = min(512, atoms)
    grad_message = None
    for start in range(0, atoms, step):
        part = dot(gain_t[:, start : start + step], onehot(step, dst_row[...], start))
        grad_message = part if grad_message is None else grad_message + part
    grad_message = grad_message * edge_scale
    radial = dot(radial_t[...], radial_basis[...])
    grad_mid = grad_in[...] + grad_message * radial
    grad_radial = low(grad_message * mid[...].astype(F32))
    begin(*tri_refs[2:], edge_ref)
    small = put_wide(dot_nt(grad_radial, radial_basis[...]), OFF_RADIAL)
    total = grad_mid
    for kept, basis, inner, outer, up, down, following in (
        (tri_refs, tri_basis, tri_in, tri_out, up_tri, down_tri, quad_refs),
        (quad_refs, quad_basis, quad_in, quad_out, up_quad, down_quad, more_refs),
    ):
        value, more = pair_backward(
            grad_mid, edge_ref, basis, inner, outer, up[...], down[...], *kept, following
        )
        total = total + value
        small = small + more
    return total, low(small)


BACK = 28


def back_last(*refs):
    _, grad_ref, all_ref, hold, sem = refs[BACK:]
    grad, small = block_backward(*refs[:BACK])
    hold[...] = small
    copy = pltpu.make_async_copy(hold, all_ref.at[:, :PAD], sem)
    copy.start()
    grad_ref[...] = grad
    copy.wait()


def back_middle(me, *refs):
    back, refs = refs[:BACK], refs[BACK:]
    big, first, second, src_row, slope_edge, free_ref, slope_atom, held = refs[:8]
    small_ref, gain_ref, update_ref, pushed_ref, grad_pre_ref, grad_ref = refs[8:14]
    *parts, grad_atoms = refs[14:]
    grad, small = block_backward(*back, more_refs=(slope_edge, free_ref, slope_atom, held))
    small_ref[...] = small
    grad_ref[...] = grad
    grad_pre = low(grad * slope_edge[...].astype(F32))
    grad_pre_ref[...] = grad_pre
    send(grad_ref, grad_pre_ref)
    grad_atoms[...] = held[...]
    edge_tables(
        grad_pre, big, first, second, src_row, back[-1], free_ref[...].astype(F32),
        slope_atom[...].astype(F32), grad_atoms, gain_ref, update_ref, pushed_ref,
    )
    quarter, count, _ = parts[0].shape
    for k, step in enumerate(scatter_order(4 * quarter)):
        rows = pl.ds(pl.multiple_of((me[0] ^ step) * count, count), count)
        parts[k // quarter][k % quarter] = low(grad_atoms[rows])


def total_of(arrived):
    total = arrived[0].astype(F32)
    for s in range(1, arrived.shape[0]):
        total = total + arrived[s].astype(F32)
    return total


def sum_list(pieces):
    total = pieces[0][...].astype(F32)
    for piece in pieces[1:]:
        total = total + piece[...].astype(F32)
    return total


def sum_pieces(*refs):
    *pieces, out_ref = refs
    out_ref[:, :PAD] = jnp.zeros((out_ref.shape[0], PAD), BF16)
    out_ref[:, PAD:] = low(sum_list(pieces))
    send(out_ref)


def sum_parts(arrived, out_ref):
    out_ref[...] = low(total_of(arrived))


def adam(me, weights, first, second, *refs):
    *pieces, grad_ref, weights_ref, first_ref, second_ref, low_ref, hold = refs
    groups, _, lanes = hold.shape
    last, others = pieces[:groups], pieces[groups:]
    small = sum_list([piece[:, :PAD] for piece in last])
    for k, piece in enumerate(last):
        hold[me[1] ^ k] = piece[:, PAD:].astype(F32)
    joint = jnp.concatenate([hold[g] for g in range(groups)], axis=1)
    grad = jnp.concatenate(
        [small[:, :SMALL], joint[:, PAD:], joint[:, :SMALL], sum_list(others)], axis=1
    )
    grad_ref[...] = grad
    send(grad_ref)
    old = weights[...]
    new_first = beta_one * first[...] + (1.0 - beta_one) * grad
    new_second = beta_two * second[...] + (1.0 - beta_two) * grad * grad
    first_ref[...] = new_first
    second_ref[...] = new_second
    send(first_ref, second_ref)
    first_hat = new_first / (1.0 - beta_one**adam_step)
    second_hat = new_second / (1.0 - beta_two**adam_step)
    new = old - learn_rate * (first_hat / (jnp.sqrt(second_hat) + epsilon) + decay_rate * old)
    weights_ref[...] = new
    send(weights_ref)
    low_ref[...] = low(new)


def exchange(pieces):
    return lax.all_to_all(pieces, "shard", split_axis=0, concat_axis=0)


def sum_pair(table, owners, beside=None):
    rounds = []
    step = 1
    while step < owners:
        rounds.append([step])
        step = 2 * step
    if len(rounds) > 2:
        rounds = [[1, 2, 3]] + rounds[2:]
    for steps in rounds[:-1]:
        others = [moved(table, k, owners) for k in steps]
        if beside is not None:
            table, beside = lax.optimization_barrier((table, beside))
        total = table.astype(F32)
        for other in others:
            total = total + other.astype(F32)
        table = total.astype(BF16)
    return table, moved(table, rounds[-1][0], owners), beside


def moved(table, step, owners, axis="shard"):
    return lax.ppermute(table, axis, [(i, i ^ step) for i in range(owners)])


def per_device(
    edge_state, atom_state, radial_basis, triplet_basis, quad_basis, dst_owner, dst_local, src_owner,
    src_local, triplet_in, triplet_out, quad_in, quad_out, fixed_atoms, edge_cotangent,
    atom_cotangent, weights, first_moment, second_moment,
):
    owners = lax.axis_size("shard")
    groups = lax.axis_size("group")
    edges = edge_state.shape[0]
    count = atom_state.shape[0]
    atoms = count * owners
    items = triplet_in.shape[0]
    me = jnp.stack([lax.axis_index("shard"), lax.axis_index("group")]).astype(jnp.int32)
    weights_t = jnp.transpose(weights)
    cols = weights_t.shape[0]
    lanes = (BIG + PAD) // groups
    def gathered(piece):
        arrays = [piece]
        for steps in gather_rounds(owners):
            held = arrays[0] if len(arrays) == 1 else jnp.concatenate(arrays, axis=0)
            arrays = arrays + [moved(held, step, owners) for step in steps]
        return arrays

    [pack] = call(
        pack_first,
        [sds((1, ROWS, PAD), BF16)],
        [weights_t],
        flops=10**7,
        raw=[0],
        scratch=[pltpu.VMEM((cols, PAD), F32), pltpu.SemaphoreType.DMA],
    )
    pack, state = lax.optimization_barrier((pack, atom_state))
    pack = gathered(pack)
    cargo, dst_row, src_row = call(
        pack_cargo,
        [sds((1, count + ROWS * (1 + 2 * slots(lanes)), D_ATOM), BF16)]
        + [sds((1, edges), jnp.int32)] * 2,
        [me, weights_t, state, fixed_atoms.reshape(1, count)]
        + [x.reshape(1, edges) for x in (dst_owner, dst_local, src_owner, src_local)],
        flops=10**7,
        late=range(1, 8),
        smem=1,
        scratch=[(groups, cols, lanes)],
    )
    cargo = gathered(cargo)
    graph = [
        jnp.transpose(radial_basis),
        jnp.transpose(triplet_basis),
        jnp.transpose(quad_basis),
        triplet_in.reshape(1, items),
        triplet_out.reshape(1, items),
        quad_in.reshape(1, items),
        quad_out.reshape(1, items),
    ]
    kept = kept_shapes(edges, items)
    table_shape = sds((atoms, D_EDGE), BF16)
    edge_shape = sds((D_EDGE, edges), BF16)
    edge_wide = sds((D_EDGE, edges), F32)
    atom_shape = sds((atoms, D_ATOM), BF16)
    atom_wide = sds((atoms, D_ATOM), F32)
    gain_shape = sds((D_EDGE, atoms), BF16)
    raw_one, *kept_one, table = call(
        first_half,
        [sds((D_EDGE, PAD), BF16)] + kept + [table_shape],
        [me, edge_state] + graph + [dst_row] + pack,
        flops=8 * 10**9,
        kept=range(1, 1 + KEPT),
        smem=1,
    )
    table, cargo = lax.optimization_barrier((table, cargo))
    lanes_shape = sds((D_EDGE, lanes), BF16)
    wide, big_two, old_state, old_free = call(
        collect,
        [lanes_shape, lanes_shape] + [sds((atoms, D_ATOM), BF16)] * 2,
        [me] + cargo,
        flops=10**7,
        smem=1,
    )
    near, far, _ = sum_pair(table, owners)

    def everywhere(piece):
        return [piece] + [moved(piece, k, groups, "group") for k in range(1, groups)]

    prepared = list(
        call(
            prepare_one,
            [sds(s, BF16) for s in PREPARED],
            [me, raw_one] + everywhere(wide),
            flops=10**9,
            smem=1,
            scratch=[(groups, D_EDGE, lanes)],
        )
    )
    back_one, small_two, back_two = prepared[:5], prepared[5:12], prepared[12:16] + [prepared[11]]
    first_one, second_one, big_one = prepared[16:]
    (
        atom_in_one, hidden_one, slope_one, state_one, sent_one, free, slope_edge_one, *kept_two, table,
    ) = call(
        middle_half,
        [table_shape, atom_shape, atom_shape, atom_wide, atom_shape, atom_shape, edge_shape]
        + kept
        + [table_shape],
        [near, far, big_one, first_one, second_one, kept_one[0]]
        + small_two
        + graph
        + [src_row, dst_row, old_state, old_free],
        flops=10 * 10**9,
        late=[5],
        kept=range(7 + KEPT),
    )
    near, far, _ = sum_pair(table, owners)
    near, state_one, kept_two[0] = lax.optimization_barrier((near, state_one, kept_two[0]))
    first_two, second_two, big_two = call(
        prepare_two,
        [sds(s, BF16) for s in LARGE_SHAPES],
        [me] + everywhere(big_two),
        flops=10**9,
        smem=1,
        scratch=[(groups, D_EDGE, lanes)],
    )
    (
        atom_in_two, hidden_two, sent_two, edge_out_t, atom_out, grad_t, grad_pre, grad_atoms, gain, update,
        pushed,
    ) = call(
        turn,
        [table_shape, atom_shape, atom_shape, edge_wide, sds((count, D_ATOM), BF16), edge_wide, edge_shape,
         atom_wide, gain_shape, atom_shape, atom_shape],
        [me, near, far, big_two, first_two, second_two, src_row, dst_row, edge_cotangent,
         atom_cotangent] + fetch([state_one, free, kept_two[0]]),
        flops=2 * 10**9,
        kept=[4, 5, 7],
        smem=1,
        scratch=[(atoms, D_ATOM)],
    )

    def rows_first(value_t, dtype):
        return call(turned, [sds((edges, D_EDGE), dtype)], [value_t], flops=10**8)[0]

    edge_out = rows_first(edge_out_t, BF16)
    near, far, (grads_two, edge_out) = sum_pair(
        gain,
        owners,
        (call(
            large_grads,
            [sds((D_EDGE, BIG), BF16)],
            [update, pushed, grad_pre, src_row, dst_row, atom_in_two, hidden_two, sent_two],
            flops=10**9,
        )[0], edge_out),
    )
    arrived_two = exchange(grads_two.reshape(owners, cols, BIG))
    fetched = fetch([grad_t] + kept_two[1:] + [slope_edge_one, free, slope_one, grad_atoms])
    half = owners // 4
    grad_small_two, gain, update, pushed, grad_pre, grad_t, *parts = call(
        back_middle,
        [sds((D_EDGE, PAD), BF16), gain_shape, atom_shape, atom_shape, edge_shape, edge_wide,
         *[sds((half, count, D_ATOM), BF16)] * 4],
        [me, near, far]
        + fetched[:KEPT]
        + back_two
        + graph
        + [dst_row, big_one, first_one, second_one, src_row]
        + fetched[KEPT:],
        flops=10 * 10**9,
        kept=[5],
        smem=1,
        scratch=[(atoms, D_ATOM)],
    )
    [pieces] = call(
        large_pieces,
        [sds((groups, D_EDGE, lanes), BF16)],
        [me, update, pushed, grad_pre, src_row, dst_row, atom_in_one, hidden_one, sent_one, grad_small_two],
        flops=10**9,
        late=[6, 7, 8],
        smem=1,
        scratch=[(D_EDGE, PAD + BIG)],
    )
    near, far, (pieces, arrived_two) = sum_pair(gain, owners, (pieces, arrived_two))
    pieces = [pieces[0]] + [moved(pieces[k], k, groups, "group") for k in range(1, groups)]
    [grads_one] = call(sum_pieces, [sds((D_EDGE, PAD + lanes), BF16)], pieces, flops=10**7, kept=[0])
    grads_one, grad_t = lax.optimization_barrier((grads_one, grad_t))
    mine = parts[0].astype(F32)
    for k in range(1, 4):
        mine = mine + moved(parts[k], k, owners).astype(F32)
    mine = mine.astype(BF16)
    step = 4
    while half > 2:
        high, mine = mine[half // 2 :], mine[: half // 2]
        mine = (mine.astype(F32) + moved(high, step, owners).astype(F32)).astype(BF16)
        half, step = half // 2, 2 * step
    grad_atom = mine[0].astype(F32) + moved(mine[1], step, owners).astype(F32)
    grad_edge_t, grads_one = call(
        back_last,
        [edge_wide, sds((D_EDGE, PAD + lanes), BF16)],
        [near, far] + fetch([grad_t] + kept_one[1:]) + back_one + graph + [dst_row, grads_one],
        flops=10 * 10**9,
        kept=[1],
        alias={BACK: 1},
        scratch=[pltpu.VMEM((D_EDGE, PAD), BF16), pltpu.SemaphoreType.DMA],
    )
    grad_edge = rows_first(grad_edge_t, F32)
    grads_one, arrived_two = lax.optimization_barrier((grads_one, arrived_two))
    arrived_one = exchange(grads_one.reshape(owners, cols, PAD + lanes))

    def owned(arrived):
        [total] = call(sum_parts, [sds(arrived.shape[1:], BF16)], [arrived], flops=10**7)
        return everywhere(total)

    pieces = owned(arrived_one) + owned(arrived_two)
    rows = weights.shape[0]
    results = call(
        adam,
        [sds((cols, rows), F32)] * 4 + [sds((cols, rows), BF16)],
        [me, weights_t, jnp.transpose(first_moment), jnp.transpose(second_moment)] + pieces,
        flops=10**8,
        kept=range(5),
        smem=1,
        scratch=[(groups, cols, lanes)],
    )
    return (edge_out, atom_out, grad_edge, grad_atom) + tuple(jnp.transpose(r) for r in results)


def solution(mesh):
    both = P(("group", "shard"), None)
    line = P(("group", "shard"))
    flat = P(None, "shard")
    in_specs = (both,) * 6 + (line, both) + (line,) * 6 + (both, both) + (flat,) * 3
    out_specs = (both,) * 4 + (flat,) * 5
    return jax.shard_map(
        per_device, mesh=mesh, in_specs=in_specs, out_specs=out_specs, check_vma=False
    )
```

```python
import jax
import jax.numpy as jnp
from jax import lax
from jax.experimental import pallas as pl
from jax.experimental.pallas import tpu as pltpu
from jax.sharding import PartitionSpec as P

D_EDGE = 128
D_ATOM = 256
D_TRI = 64
D_QUAD = 32
D_BASIS = 16
BLOCKS = 2
FOLD = 256
CHUNK = 1024
SMALL = 220
BIG = 1280
PAD = 256
ROWS = 16

edge_scale = 0.25
pair_scale = 0.5
beta_one = 0.5
beta_two = 0.5
learn_rate = 0.1
decay_rate = 0.01
epsilon = 1e-08
adam_step = 4

OFF_DOWN = {D_TRI: 0, D_QUAD: 136}
OFF_BASIS = {D_TRI: 64, D_QUAD: 168}
OFF_UP = {D_TRI: 72, D_QUAD: 172}
OFF_RADIAL = 204

F32 = jnp.float32
BF16 = jnp.bfloat16


def sds(shape, dtype):
    return jax.ShapeDtypeStruct(shape, dtype)


class Late:
    def __init__(self, source, ref, sem):
        self.ref, self.copy = ref, pltpu.make_async_copy(source, ref, sem)
        self.shape, self.begun, self.here = ref.shape, False, False

    def start(self):
        if not self.begun:
            self.copy.start()
            self.begun = True

    def wait(self):
        if not self.here:
            self.start()
            self.copy.wait()
            self.here = True

    def __getitem__(self, index):
        self.wait()
        return self.ref[index]


class Kept:
    def __init__(self, target, ref, sem):
        self.ref, self.copy, self.sent = ref, pltpu.make_async_copy(ref, target, sem), False
        self.shape, self.dtype = ref.shape, ref.dtype

    def __getitem__(self, index):
        return self.ref[index]

    def __setitem__(self, index, value):
        self.ref[index] = value

    def send(self):
        if not self.sent:
            self.copy.start()
            self.sent = True


def begin(*refs):
    for ref in refs:
        if isinstance(ref, Late):
            ref.start()


def arrive(*refs):
    for ref in refs:
        if isinstance(ref, Late):
            ref.wait()


def send(*refs):
    for ref in refs:
        if isinstance(ref, Kept):
            ref.send()


def call(body, outs, args, flops=10**9, late=(), kept=(), smem=0, scratch=(), early=None, alias=None, raw=()):
    alias = alias or {}
    held = [i for i in kept if i not in alias.values()]
    moved = [args[i] for i in late] + [outs[i] for i in held]

    def kernel(*refs):
        refs = list(refs)
        ins, rest = refs[: len(args)], refs[len(args) :]
        results, rest = rest[: len(outs)], rest[len(outs) :]
        extra, rest = rest[: len(scratch)], rest[len(scratch) :]
        buffers, sems = rest[: len(moved)], rest[len(moved) :]
        for k, i in enumerate(late):
            ins[i] = Late(ins[i], buffers[k], sems[k])
        begin(*[ins[i] for i in (late if early is None else early)])
        for k, i in enumerate(held, len(late)):
            results[i] = Kept(results[i], buffers[k], sems[k])
        body(*ins, *results, *extra)
        for i in late:
            ins[i].wait()
        for i in held:
            results[i].send()
        for i in held:
            results[i].copy.wait()

    args = [pltpu.with_memory_space_constraint(x, pltpu.HBM) if i in late or i in alias or i in raw else x for i, x in enumerate(args)]
    outs = [pltpu.HBM(x.shape, x.dtype) if i in kept else x for i, x in enumerate(outs)]
    space = [pltpu.SMEM] * smem + [pltpu.VMEM] * (len(args) - smem)
    for i in [*late, *alias, *raw]:
        space[i] = pltpu.HBM
    return pl.pallas_call(
        kernel,
        out_shape=outs,
        in_specs=[pl.BlockSpec(memory_space=s) for s in space],
        out_specs=[
            pl.BlockSpec(memory_space=pltpu.HBM if i in kept else pltpu.VMEM)
            for i in range(len(outs))
        ],
        scratch_shapes=[pltpu.VMEM(x, F32) if isinstance(x, tuple) else x for x in scratch]
        + [pltpu.VMEM(m.shape, m.dtype) for m in moved]
        + [pltpu.SemaphoreType.DMA] * len(moved),
        input_output_aliases=alias,
        compiler_params=pltpu.CompilerParams(vmem_limit_bytes=24 * 2**20),
        cost_estimate=pl.CostEstimate(flops=flops, bytes_accessed=2**20, transcendentals=0),
        name=body.__name__,
    )(*args)


def fetch(arrays):
    count = len(arrays)

    def kernel(*refs):
        copies = [
            pltpu.make_async_copy(refs[i], refs[count + i], refs[2 * count + i]) for i in range(count)
        ]
        for copy in copies:
            copy.start()
        for copy in copies:
            copy.wait()

    results = pl.pallas_call(
        kernel,
        out_shape=[sds(x.shape, x.dtype) for x in arrays],
        in_specs=[pl.BlockSpec(memory_space=pltpu.HBM)] * count,
        out_specs=[pl.BlockSpec(memory_space=pltpu.VMEM)] * count,
        scratch_shapes=[pltpu.SemaphoreType.DMA] * count,
        compiler_params=pltpu.CompilerParams(vmem_limit_bytes=2**20 * 20),
        cost_estimate=pl.CostEstimate(flops=10**9, bytes_accessed=2**20, transcendentals=0),
        name="fetch",
    )(*[pltpu.with_memory_space_constraint(x, pltpu.HBM) for x in arrays])
    return list(results)


def dot(a, b):
    return jnp.dot(a, b, preferred_element_type=F32)


def dot_nt(a, b):
    return lax.dot_general(a, b, (((1,), (1,)), ((), ())), preferred_element_type=F32)


def low(v):
    return v.astype(BF16)


def iota(shape, axis):
    return lax.broadcasted_iota(jnp.int32, shape, axis)


def ones_where(mask):
    return jnp.where(mask, 1.0, 0.0).astype(BF16)


def onehot(count, row, first=0):
    parts = []
    for start in range(0, count, 256):
        size = min(256, count - start)
        ids = iota((size, row.shape[1]), 0).astype(F32).astype(BF16)
        mask = ids == (row - (first + start)).astype(F32).astype(BF16)
        parts.append(jnp.where(mask, jnp.ones((), BF16), jnp.zeros((), BF16)))
    return parts[0] if len(parts) == 1 else jnp.concatenate(parts, axis=0)


def sigmoid(v):
    return 0.5 + 0.5 * jnp.tanh(0.5 * v)


def silu_pair(v):
    s = sigmoid(v)
    return v * s, s * (1.0 + v * (1.0 - s))


def cut(value, width):
    count = FOLD // width
    length = value.shape[1] // count
    return jnp.concatenate([value[:, g * length : (g + 1) * length] for g in range(count)], axis=0)


def uncut(value, width):
    count = FOLD // width
    return jnp.concatenate([value[g * width : (g + 1) * width] for g in range(count)], axis=1)


def pick(folded, high, width):
    result = folded[:width]
    for g in range(1, FOLD // width):
        result = jnp.where(high == g, folded[g * width : (g + 1) * width], result)
    return result


def spread(value, high, width):
    value = low(value)
    high = high.astype(F32).astype(BF16)
    return jnp.concatenate(
        [jnp.where(high == g, value, jnp.zeros((), BF16)) for g in range(FOLD // width)], axis=0
    )


def high_low(index, length):
    return index >> (length.bit_length() - 1), index & (length - 1)


def small_t(raw, offset, width, columns):
    count = 128 // width
    total = None
    for p in range(count):
        lane, d = iota((PAD, columns), 0), iota((PAD, columns), 1)
        high, rest = high_low(d, count)
        sel = ones_where((rest == p) & (lane == offset + high))
        part = dot(raw[p * width : (p + 1) * width], sel)
        total = part if total is None else total + part
    return low(total)


def small_plain(raw, offset, width, rows):
    count = 128 // width
    total = None
    for p in range(count):
        d, lane = iota((rows, PAD), 0), iota((rows, PAD), 1)
        high, rest = high_low(d, count)
        sel = ones_where((rest == p) & (lane == offset + high))
        part = dot_nt(sel, raw[p * width : (p + 1) * width])
        total = part if total is None else total + part
    return low(total)


def wide_t(raw, offset, rows):
    lane, d = iota((PAD, rows), 0), iota((PAD, rows), 1)
    return low(dot(raw, ones_where(lane == offset + d)))


def wide_plain(raw, offset, rows):
    d, lane = iota((rows, PAD), 0), iota((rows, PAD), 1)
    return low(dot_nt(ones_where(lane == offset + d), raw))


def double_plain(raw, rows):
    d, lane = iota((rows, 2 * rows), 0), iota((rows, 2 * rows), 1)
    return jnp.concatenate(
        [low(dot_nt(ones_where(lane == 2 * d + p), raw)) for p in range(2)], axis=1
    )


def put_small(grad_t, offset, width):
    count = 128 // width
    columns = grad_t.shape[1]
    value = low(grad_t)
    parts = []
    for p in range(count):
        d, lane = iota((columns, PAD), 0), iota((columns, PAD), 1)
        high, rest = high_low(d, count)
        sel = ones_where((rest == p) & (lane == offset + high))
        parts.append(dot(value, sel))
    return jnp.concatenate(parts, axis=0)


def put_wide(grad_t, offset):
    columns = grad_t.shape[1]
    d, lane = iota((columns, PAD), 0), iota((columns, PAD), 1)
    return dot(low(grad_t), ones_where(lane == offset + d))


def put_double(grad_t):
    rows = grad_t.shape[1]
    d, lane = iota((rows, 2 * rows), 0), iota((rows, 2 * rows), 1)
    value = low(grad_t)
    return low(
        dot(value[:128], ones_where(lane == 2 * d)) + dot(value[128:], ones_where(lane == 2 * d + 1))
    )


def small_matrices(raw):
    return (
        [small_t(raw, OFF_DOWN[w], w, D_EDGE) for w in (D_TRI, D_QUAD)]
        + [small_t(raw, OFF_BASIS[w], w, D_BASIS) for w in (D_TRI, D_QUAD)]
        + [wide_t(raw, OFF_UP[w], w) for w in (D_TRI, D_QUAD)]
        + [wide_t(raw, OFF_RADIAL, D_BASIS)]
    )


def back_matrices(raw):
    return [wide_plain(raw, OFF_UP[w], w) for w in (D_TRI, D_QUAD)] + [
        small_plain(raw, OFF_DOWN[w], w, D_EDGE) for w in (D_TRI, D_QUAD)
    ]


SMALL_SHAPES = [
    (D_TRI, D_EDGE), (D_QUAD, D_EDGE), (D_TRI, D_BASIS), (D_QUAD, D_BASIS), (D_EDGE, D_TRI),
    (D_EDGE, D_QUAD), (D_EDGE, D_BASIS),
]
BACK_SHAPES = [(D_TRI, D_EDGE), (D_QUAD, D_EDGE), (D_EDGE, D_TRI), (D_EDGE, D_QUAD)]


def slots(width):
    return -(-width // PAD)


def padded(value, rows, lanes):
    have, wide = value.shape
    if wide < lanes:
        value = jnp.concatenate([value, jnp.zeros((have, lanes - wide), value.dtype)], axis=1)
    if have < rows:
        value = jnp.concatenate([value, jnp.zeros((rows - have, lanes), value.dtype)], axis=0)
    return value


def pack_first(weights, out_ref, hold, sem):
    copy = pltpu.make_async_copy(weights.at[:, :PAD], hold, sem)
    copy.start()
    copy.wait()
    out_ref[0] = low(padded(hold[...], ROWS, PAD))


def pack_cargo(
    me, weights, state, fixed, dst_owner, dst_local, src_owner, src_local, out_ref, dst_ref, src_ref, hold
):
    count = state.shape[0]
    free = (1 - fixed[...]).astype(F32)
    out_ref[0, :count] = state[...]
    out_ref[0, count : count + ROWS] = low(padded(free, ROWS, PAD))
    values = weights[...]
    half = SMALL + BIG
    gap = jnp.zeros((values.shape[0], PAD - SMALL), F32)
    one = jnp.concatenate([values[:, SMALL : half + SMALL], gap], axis=1)
    two = padded(values[:, half + SMALL :], values.shape[0], BIG + PAD)
    groups, _, width = hold.shape
    base = count + ROWS
    for side in (one, two):
        for g in range(groups):
            hold[g] = side[:, g * width : (g + 1) * width]
        mine = padded(hold[me[1]], ROWS, slots(width) * PAD)
        for k in range(slots(width)):
            out_ref[0, base : base + ROWS] = low(mine[:, k * PAD : (k + 1) * PAD])
            base = base + ROWS
    dst_ref[...] = dst_owner[...] * count + dst_local[...]
    src_ref[...] = src_owner[...] * count + src_local[...]


def order_of(owners):
    order = [0]
    for steps in gather_rounds(owners):
        order = order + [k ^ step for step in steps for k in order]
    return order


def gather_rounds(owners):
    rounds, step = [], owners // 2
    while step > 2:
        rounds.append([step])
        step = step // 2
    return rounds + ([[1, 2, 3]] if owners > 2 else [[1]])


def scatter_order(owners):
    order, step = [0], owners // 2
    while step > 2:
        order = order + [k ^ step for k in order]
        step = step // 2
    return [k ^ low_bits for low_bits in range(4) for k in order]


def arrivals(pieces):
    return [piece[i] for piece in pieces for i in range(piece.shape[0])]


def arrival_pick(me, order, cols):
    col = iota((1, len(order) * ROWS), 1)
    block, inside = high_low(col, ROWS)
    owner = jnp.zeros(col.shape, jnp.int32)
    for position, k in enumerate(order):
        owner = jnp.where(block == position, me ^ k, owner)
    return onehot(len(order) * cols, jnp.where(inside < cols, owner * cols + inside, -1))


def collect(me, *refs):
    *cargo, one_ref, two_ref, state_ref, free_ref = refs
    cargo = arrivals(cargo)
    owners = len(cargo)
    full, width = one_ref.shape
    count = state_ref.shape[0] // owners
    order = order_of(owners)
    sel = arrival_pick(me[0], order, full // owners)
    for side, ref in ((0, one_ref), (1, two_ref)):
        for k in range(slots(width)):
            start = count + ROWS * (1 + side * slots(width) + k)
            values = jnp.concatenate([c[start : start + ROWS] for c in cargo], axis=0)
            lanes = min(PAD, width - k * PAD)
            ref[:, k * PAD : k * PAD + lanes] = low(dot(sel, values))[:, :lanes]
    eye = iota((count, count), 0) == iota((count, count), 1)
    for piece, k in zip(cargo, order):
        rows = pl.ds(pl.multiple_of((me[0] ^ k) * count, count), count)
        state_ref[rows] = piece[:count]
        flag = piece[count : count + 1, :count].astype(F32)
        column = jnp.sum(jnp.where(eye, flag, 0.0), axis=1, keepdims=True)
        free_ref[rows] = low(jnp.broadcast_to(column, (count, D_ATOM)))


def joined(me, pieces, hold):
    for k, piece in enumerate(pieces):
        hold[me[1] ^ k] = piece[...].astype(F32)
    return low(jnp.concatenate([hold[g] for g in range(len(pieces))], axis=1))


def prepare_one(me, raw, *refs):
    *rest, hold = refs
    groups = hold.shape[0]
    wide = joined(me, rest[:groups], hold)
    raw_one = raw[...]
    raw_two = wide[:, BIG:]
    values = back_matrices(raw_one) + [wide_t(raw_one, OFF_RADIAL, D_BASIS)]
    values = values + small_matrices(raw_two) + back_matrices(raw_two)
    values = values + [double_plain(wide[:, :256], D_EDGE), double_plain(wide[:, 256:768], D_ATOM)]
    for ref, value in zip(rest[groups:], values + [wide[:, :BIG]]):
        ref[...] = value


def prepare_two(me, *refs):
    *rest, hold = refs
    groups = hold.shape[0]
    big = joined(me, rest[:groups], hold)
    first_ref, second_ref, big_ref = rest[groups:]
    first_ref[...] = double_plain(big[:, :256], D_EDGE)
    second_ref[...] = double_plain(big[:, 256:768], D_ATOM)
    big_ref[...] = big[:, :BIG]


LARGE_SHAPES = [(D_EDGE, D_ATOM), (D_ATOM, D_ATOM), (D_EDGE, BIG)]
PREPARED = BACK_SHAPES + [(D_EDGE, D_BASIS)] + SMALL_SHAPES + BACK_SHAPES + LARGE_SHAPES


def pair_forward(edge_t, basis_ref, in_ref, out_ref, down_t, basis_t, up_t, xg_ref, bt_ref):
    width, edges = down_t.shape[0], edge_t.shape[1]
    length = edges * width // FOLD
    act, slope_in = silu_pair(dot(down_t, edge_t))
    table = cut(low(act), width)
    total = jnp.zeros((FOLD, length), F32)
    items = in_ref.shape[1]
    chunk = min(CHUNK // 2, items)
    for start in range(0, items, chunk):
        cols = slice(start, start + chunk)
        in_high, in_low = high_low(in_ref[:, cols], length)
        out_high, out_low = high_low(out_ref[:, cols], length)
        xg = pick(dot(table, onehot(length, in_low)), in_high, width)
        bt = dot(basis_t, basis_ref[:, cols])
        xg_ref[:, cols] = low(xg)
        bt_ref[:, cols] = low(bt)
        total = total + dot_nt(spread(xg * bt, out_high, width), onehot(length, out_low))
    send(xg_ref, bt_ref)
    agg_t = low(uncut(total, width) * pair_scale)
    value, slope_out = silu_pair(dot(up_t, agg_t))
    return value, slope_in, agg_t, slope_out


def pair_backward(
    grad_mid, edge_t, basis_ref, in_ref, out_ref, up, down, slope_out, agg_t, xg_ref, bt_ref, slope_in,
    following,
):
    width, edges = up.shape[0], slope_in.shape[1]
    length = edges * width // FOLD
    grad_out = low(grad_mid * slope_out[...].astype(F32))
    grad_up_t = dot_nt(grad_out, agg_t[...])
    table = cut(low(dot(up, grad_out) * pair_scale), width)
    begin(xg_ref, bt_ref)
    arrive(xg_ref, bt_ref)
    begin(*following)
    total = jnp.zeros((FOLD, length), F32)
    grad_basis_t = jnp.zeros((width, D_BASIS), F32)
    items = in_ref.shape[1]
    chunk = min(CHUNK, items)
    for start in range(0, items, chunk):
        cols = slice(start, start + chunk)
        in_high, in_low = high_low(in_ref[:, cols], length)
        out_high, out_low = high_low(out_ref[:, cols], length)
        gy = pick(dot(table, onehot(length, out_low)), out_high, width)
        grad_bt = low(gy * xg_ref[:, cols].astype(F32))
        grad_basis_t = grad_basis_t + dot_nt(grad_bt, basis_ref[:, cols])
        moved = gy * bt_ref[:, cols].astype(F32)
        total = total + dot_nt(spread(moved, in_high, width), onehot(length, in_low))
    grad_in = low(uncut(total, width) * slope_in[...].astype(F32))
    grad_down_t = dot_nt(grad_in, edge_t[...])
    small = (
        put_small(grad_down_t, OFF_DOWN[width], width)
        + put_small(grad_basis_t, OFF_BASIS[width], width)
        + put_wide(grad_up_t, OFF_UP[width])
    )
    return dot(down, grad_in), small


def block_forward(state_t, matrices, graph, dst_row, out_refs):
    radial_basis, tri_basis, quad_basis, tri_in, tri_out, quad_in, quad_out = graph
    down_tri, down_quad, basis_tri, basis_quad, up_tri, up_quad, radial_t = matrices
    mid_ref, mid_low_ref = out_refs[:2]
    tri_refs, edge_ref, quad_refs, table_ref = out_refs[2:7], out_refs[7], out_refs[8:13], out_refs[13]
    edge_t = low(state_t)
    edge_ref[...] = edge_t
    send(edge_ref)
    mid = state_t
    for refs, basis, inner, outer, down, basis_t, up in (
        (tri_refs, tri_basis, tri_in, tri_out, down_tri, basis_tri, up_tri),
        (quad_refs, quad_basis, quad_in, quad_out, down_quad, basis_quad, up_quad),
    ):
        slope_out_ref, agg_ref, xg_ref, bt_ref, slope_in_ref = refs
        value, slope_in, agg, slope_out = pair_forward(
            edge_t, basis, inner, outer, down, basis_t, up, xg_ref, bt_ref
        )
        slope_in_ref[...] = low(slope_in)
        agg_ref[...] = agg
        slope_out_ref[...] = low(slope_out)
        send(slope_in_ref, agg_ref, slope_out_ref)
        mid = mid + value
    mid_ref[...] = mid
    mid_low_ref[...] = low(mid)
    send(mid_ref, mid_low_ref)
    message = low(mid * dot(radial_t, radial_basis[...]))
    atoms = table_ref.shape[0]
    step = min(512, atoms)
    for start in range(0, atoms, step):
        rows = slice(start, start + step)
        table_ref[rows] = low(dot_nt(onehot(step, dst_row[...], start), message))


def kept_shapes(edges, items):
    edge = ((D_EDGE, edges), BF16)
    tri, quad = [
        [edge, ((w, edges), BF16), ((w, items), BF16), ((w, items), BF16), ((w, edges), BF16)]
        for w in (D_TRI, D_QUAD)
    ]
    return [sds(*x) for x in [((D_EDGE, edges), F32), edge] + tri + [edge] + quad]


KEPT = 13


def first_half(me, edge_state, *refs):
    graph, dst_row, rest = refs[:7], refs[7], refs[8:]
    pack = [ref for ref in rest if len(ref.shape) == 3]
    raw_ref, *out_refs = rest[len(pack) :]
    blocks = arrivals(pack)
    owners = len(blocks)
    sel = arrival_pick(me[0], order_of(owners), D_EDGE // owners)
    raw = low(dot(sel, jnp.concatenate(blocks, axis=0)))
    raw_ref[...] = raw
    eye = ones_where(iota((D_EDGE, D_EDGE), 0) == iota((D_EDGE, D_EDGE), 1))
    state_t = dot_nt(eye, edge_state[...])
    block_forward(state_t, small_matrices(raw), graph, dst_row, out_refs)


def atom_forward(near, far, state, free, first, second):
    atom_in = low((near[...].astype(F32) + far[...].astype(F32)) * edge_scale)
    act, slope = silu_pair(dot(atom_in, first[...]))
    hidden = low(act)
    new_state = state + free * dot(hidden, second[...])
    return atom_in, hidden, slope, new_state


def edge_pre(sent, big, src_row, dst_row):
    src_t = low(dot_nt(big[:, 768:1024], sent))
    dst_t = low(dot_nt(big[:, 1024:1280], sent))
    atoms = sent.shape[0]
    step = min(512, atoms)
    total = None
    for start in range(0, atoms, step):
        part = dot(src_t[:, start : start + step], onehot(step, src_row[...], start))
        part = part + dot(dst_t[:, start : start + step], onehot(step, dst_row[...], start))
        total = part if total is None else total + part
    return total


def middle_half(near, far, big, first, second, mid_in, *refs):
    matrices, graph, src_row, dst_row = refs[:7], refs[7:14], refs[14], refs[15]
    old_state, old_free = refs[16:18]
    atom_in_ref, hidden_ref, slope_atom_ref, state_ref, sent_ref, free_ref, slope_edge_ref = refs[18:25]
    out_refs = refs[25:]
    free = old_free[...]
    free_ref[...] = free
    send(free_ref)
    atom_in, hidden, slope, state = atom_forward(
        near, far, old_state[...].astype(F32), free.astype(F32), first, second
    )
    atom_in_ref[...] = atom_in
    hidden_ref[...] = hidden
    slope_atom_ref[...] = low(slope)
    state_ref[...] = state
    sent = low(state)
    sent_ref[...] = sent
    send(atom_in_ref, hidden_ref, slope_atom_ref, state_ref, sent_ref)
    act, slope_edge = silu_pair(edge_pre(sent, big, src_row, dst_row))
    slope_edge_ref[...] = low(slope_edge)
    send(slope_edge_ref)
    block_forward(mid_in[...] + act, [m[...] for m in matrices], graph, dst_row, out_refs)


def edge_tables(
    grad_pre, big, first, second, src_row, dst_row, free, slope_atom, grad_atoms, gain_ref, update_ref,
    pushed_ref,
):
    atoms = free.shape[0]
    step = min(512, atoms)
    src_t, dst_t = big[:, 768:1024], big[:, 1024:1280]
    for start in range(0, atoms, step):
        rows = slice(start, start + step)
        pick_src = onehot(step, src_row[...], start)
        pick_dst = onehot(step, dst_row[...], start)
        part = dot(low(dot_nt(pick_src, grad_pre)), src_t) + dot(low(dot_nt(pick_dst, grad_pre)), dst_t)
        grad_atoms[rows] = grad_atoms[rows] + part
    update = low(grad_atoms[...] * free)
    update_ref[...] = update
    send(update_ref)
    pushed = low(dot_nt(update, second[...]) * slope_atom)
    pushed_ref[...] = pushed
    send(pushed_ref)
    gain_ref[...] = low(dot_nt(first[...], pushed))


def turn(
    me, near, far, big, first, second, src_row, dst_row, edge_cotangent, own, state_in, free_ref, mid_in,
    atom_in_ref, hidden_ref, sent_ref, edge_ref, atom_out_ref, cotangent_ref, grad_pre_ref, atoms_ref,
    gain_ref, update_ref, pushed_ref, hold,
):
    free = free_ref[...].astype(F32)
    begin(mid_in)
    atom_in, hidden, slope, state = atom_forward(near, far, state_in[...], free, first, second)
    atom_in_ref[...] = atom_in
    hidden_ref[...] = hidden
    sent = low(state)
    sent_ref[...] = sent
    send(atom_in_ref, hidden_ref, sent_ref)
    hold[...] = state
    count = atom_out_ref.shape[0]
    mine = pl.ds(pl.multiple_of(me[0] * count, count), count)
    atom_out_ref[...] = low(hold[mine])
    act, slope_edge = silu_pair(edge_pre(sent, big, src_row, dst_row))
    edge_ref[...] = mid_in[...] + act
    send(edge_ref, atom_out_ref)
    eye = ones_where(iota((D_EDGE, D_EDGE), 0) == iota((D_EDGE, D_EDGE), 1))
    cotangent = dot_nt(eye, edge_cotangent[...])
    cotangent_ref[...] = cotangent
    grad_pre = low(cotangent * slope_edge)
    grad_pre_ref[...] = grad_pre
    send(cotangent_ref, grad_pre_ref)
    atoms_ref[...] = jnp.zeros(atoms_ref.shape, F32)
    atoms_ref.ref[mine] = own[...].astype(F32)
    edge_tables(
        grad_pre, big, first, second, src_row, dst_row, free, slope, atoms_ref, gain_ref, update_ref,
        pushed_ref,
    )


def large_grads(update, pushed, grad_pre, src_row, dst_row, atom_in, hidden, sent, out_ref):
    for lanes, value in large_values(update, pushed, grad_pre, src_row, dst_row, atom_in, hidden, sent):
        out_ref[:, lanes] = value


def large_pieces(
    me, update, pushed, grad_pre, src_row, dst_row, atom_in, hidden, sent, small, out_ref, hold
):
    hold[:, :PAD] = small[...].astype(F32)
    for lanes, value in large_values(update, pushed, grad_pre, src_row, dst_row, atom_in, hidden, sent):
        hold[:, PAD + lanes.start : PAD + lanes.stop] = value.astype(F32)
    groups, _, width = out_ref.shape
    for g in range(groups):
        out_ref[g ^ me[1]] = low(hold[:, g * width : (g + 1) * width])


def large_values(update, pushed, grad_pre, src_row, dst_row, atom_in, hidden, sent):
    atoms = sent.shape[0]
    step = min(512, atoms)
    grads = grad_pre[...]
    update_t = low(jnp.transpose(update[...].astype(F32)))
    pushed_t = low(jnp.transpose(pushed[...].astype(F32)))
    grad_src = jnp.zeros((D_EDGE, D_ATOM), F32)
    grad_dst = jnp.zeros((D_EDGE, D_ATOM), F32)
    for start in range(0, atoms, step):
        rows = slice(start, start + step)
        sums = [low(dot_nt(grads, onehot(step, row[...], start))) for row in (src_row, dst_row)]
        grad_src = grad_src + dot(sums[0], sent[rows])
        grad_dst = grad_dst + dot(sums[1], sent[rows])
    grad_second_t = dot(update_t, hidden[...])
    grad_first_t = dot(pushed_t, atom_in[...])
    return [
        (slice(0, 256), put_double(grad_first_t)),
        (slice(256, 768), put_double(grad_second_t)),
        (slice(768, 1024), low(grad_src)),
        (slice(1024, 1280), low(grad_dst)),
    ]


def turned(value_ref, out_ref):
    out_ref[...] = jnp.transpose(value_ref[...]).astype(out_ref.dtype)


def block_backward(near, far, grad_in, *refs, more_refs=()):
    mid, tri_refs, edge_ref, quad_refs = refs[0], refs[1:6], refs[6], refs[7:12]
    up_tri, up_quad, down_tri, down_quad, radial_t = refs[12:17]
    radial_basis, tri_basis, quad_basis, tri_in, tri_out, quad_in, quad_out = refs[17:24]
    dst_row = refs[24]
    gain_t = low(near[...].astype(F32) + far[...].astype(F32))
    atoms = gain_t.shape[1]
    step = min(512, atoms)
    grad_message = None
    for start in range(0, atoms, step):
        part = dot(gain_t[:, start : start + step], onehot(step, dst_row[...], start))
        grad_message = part if grad_message is None else grad_message + part
    grad_message = grad_message * edge_scale
    radial = dot(radial_t[...], radial_basis[...])
    grad_mid = grad_in[...] + grad_message * radial
    grad_radial = low(grad_message * mid[...].astype(F32))
    begin(*tri_refs[2:], edge_ref)
    small = put_wide(dot_nt(grad_radial, radial_basis[...]), OFF_RADIAL)
    total = grad_mid
    for kept, basis, inner, outer, up, down, following in (
        (tri_refs, tri_basis, tri_in, tri_out, up_tri, down_tri, quad_refs),
        (quad_refs, quad_basis, quad_in, quad_out, up_quad, down_quad, more_refs),
    ):
        value, more = pair_backward(
            grad_mid, edge_ref, basis, inner, outer, up[...], down[...], *kept, following
        )
        total = total + value
        small = small + more
    return total, low(small)


BACK = 28


def back_last(*refs):
    _, grad_ref, all_ref, hold, sem = refs[BACK:]
    grad, small = block_backward(*refs[:BACK])
    hold[...] = small
    copy = pltpu.make_async_copy(hold, all_ref.at[:, :PAD], sem)
    copy.start()
    grad_ref[...] = grad
    copy.wait()


def back_middle(me, *refs):
    back, refs = refs[:BACK], refs[BACK:]
    big, first, second, src_row, slope_edge, free_ref, slope_atom, held = refs[:8]
    small_ref, gain_ref, update_ref, pushed_ref, grad_pre_ref, grad_ref = refs[8:14]
    *parts, grad_atoms = refs[14:]
    grad, small = block_backward(*back, more_refs=(slope_edge, free_ref, slope_atom, held))
    small_ref[...] = small
    grad_ref[...] = grad
    grad_pre = low(grad * slope_edge[...].astype(F32))
    grad_pre_ref[...] = grad_pre
    send(grad_ref, grad_pre_ref)
    grad_atoms[...] = held[...]
    edge_tables(
        grad_pre, big, first, second, src_row, back[-1], free_ref[...].astype(F32),
        slope_atom[...].astype(F32), grad_atoms, gain_ref, update_ref, pushed_ref,
    )
    quarter, count, _ = parts[0].shape
    for k, step in enumerate(scatter_order(4 * quarter)):
        rows = pl.ds(pl.multiple_of((me[0] ^ step) * count, count), count)
        parts[k // quarter][k % quarter] = low(grad_atoms[rows])


def total_of(arrived):
    total = arrived[0].astype(F32)
    for s in range(1, arrived.shape[0]):
        total = total + arrived[s].astype(F32)
    return total


def sum_list(pieces):
    total = pieces[0][...].astype(F32)
    for piece in pieces[1:]:
        total = total + piece[...].astype(F32)
    return total


def sum_pieces(*refs):
    *pieces, out_ref = refs
    out_ref[:, :PAD] = jnp.zeros((out_ref.shape[0], PAD), BF16)
    out_ref[:, PAD:] = low(sum_list(pieces))
    send(out_ref)


def sum_parts(arrived, out_ref):
    out_ref[...] = low(total_of(arrived))


def adam(me, weights, first, second, *refs):
    *pieces, grad_ref, weights_ref, first_ref, second_ref, low_ref, hold = refs
    groups, _, lanes = hold.shape
    last, others = pieces[:groups], pieces[groups:]
    small = sum_list([piece[:, :PAD] for piece in last])
    parts = [piece[:, PAD:].astype(F32) for piece in last]
    joint = []
    for g in range(groups):
        value = parts[0]
        for k in range(1, groups):
            value = jnp.where((me[1] ^ k) == g, parts[k], value)
        joint.append(value)
    joint = jnp.concatenate(joint, axis=1)
    grad = jnp.concatenate(
        [small[:, :SMALL], joint[:, PAD:], joint[:, :SMALL], sum_list(others)], axis=1
    )
    grad_ref[...] = grad
    send(grad_ref)
    old = weights[...]
    new_first = beta_one * first[...] + (1.0 - beta_one) * grad
    new_second = beta_two * second[...] + (1.0 - beta_two) * grad * grad
    first_ref[...] = new_first
    second_ref[...] = new_second
    send(first_ref, second_ref)
    first_hat = new_first / (1.0 - beta_one**adam_step)
    second_hat = new_second / (1.0 - beta_two**adam_step)
    new = old - learn_rate * (first_hat / (jnp.sqrt(second_hat) + epsilon) + decay_rate * old)
    weights_ref[...] = new
    send(weights_ref)
    low_ref[...] = low(new)


def exchange(pieces):
    return lax.all_to_all(pieces, "shard", split_axis=0, concat_axis=0)


def sum_pair(table, owners, beside=None):
    rounds = []
    step = 1
    while step < owners:
        rounds.append([step])
        step = 2 * step
    if len(rounds) > 2:
        rounds = [[1, 2, 3]] + rounds[2:]
    for steps in rounds[:-1]:
        others = [moved(table, k, owners) for k in steps]
        if beside is not None:
            table, beside = lax.optimization_barrier((table, beside))
        total = table.astype(F32)
        for other in others:
            total = total + other.astype(F32)
        table = total.astype(BF16)
    return table, moved(table, rounds[-1][0], owners), beside


def moved(table, step, owners, axis="shard"):
    return lax.ppermute(table, axis, [(i, i ^ step) for i in range(owners)])


def per_device(
    edge_state, atom_state, radial_basis, triplet_basis, quad_basis, dst_owner, dst_local, src_owner,
    src_local, triplet_in, triplet_out, quad_in, quad_out, fixed_atoms, edge_cotangent,
    atom_cotangent, weights, first_moment, second_moment,
):
    owners = lax.axis_size("shard")
    groups = lax.axis_size("group")
    edges = edge_state.shape[0]
    count = atom_state.shape[0]
    atoms = count * owners
    items = triplet_in.shape[0]
    me = jnp.stack([lax.axis_index("shard"), lax.axis_index("group")]).astype(jnp.int32)
    weights_t = jnp.transpose(weights)
    cols = weights_t.shape[0]
    lanes = (BIG + PAD) // groups
    def gathered(piece):
        arrays = [piece]
        for steps in gather_rounds(owners):
            held = arrays[0] if len(arrays) == 1 else jnp.concatenate(arrays, axis=0)
            arrays = arrays + [moved(held, step, owners) for step in steps]
        return arrays

    [pack] = call(
        pack_first,
        [sds((1, ROWS, PAD), BF16)],
        [weights_t],
        flops=10**7,
        raw=[0],
        scratch=[pltpu.VMEM((cols, PAD), F32), pltpu.SemaphoreType.DMA],
    )
    pack, state = lax.optimization_barrier((pack, atom_state))
    pack = gathered(pack)
    cargo, dst_row, src_row = call(
        pack_cargo,
        [sds((1, count + ROWS * (1 + 2 * slots(lanes)), D_ATOM), BF16)]
        + [sds((1, edges), jnp.int32)] * 2,
        [me, weights_t, state, fixed_atoms.reshape(1, count)]
        + [x.reshape(1, edges) for x in (dst_owner, dst_local, src_owner, src_local)],
        flops=10**7,
        late=range(1, 8),
        smem=1,
        scratch=[(groups, cols, lanes)],
    )
    cargo = gathered(cargo)
    graph = [
        jnp.transpose(radial_basis),
        jnp.transpose(triplet_basis),
        jnp.transpose(quad_basis),
        triplet_in.reshape(1, items),
        triplet_out.reshape(1, items),
        quad_in.reshape(1, items),
        quad_out.reshape(1, items),
    ]
    kept = kept_shapes(edges, items)
    table_shape = sds((atoms, D_EDGE), BF16)
    edge_shape = sds((D_EDGE, edges), BF16)
    edge_wide = sds((D_EDGE, edges), F32)
    atom_shape = sds((atoms, D_ATOM), BF16)
    atom_wide = sds((atoms, D_ATOM), F32)
    gain_shape = sds((D_EDGE, atoms), BF16)
    raw_one, *kept_one, table = call(
        first_half,
        [sds((D_EDGE, PAD), BF16)] + kept + [table_shape],
        [me, edge_state] + graph + [dst_row] + pack,
        flops=8 * 10**9,
        kept=range(1, 1 + KEPT),
        smem=1,
    )
    table, cargo = lax.optimization_barrier((table, cargo))
    lanes_shape = sds((D_EDGE, lanes), BF16)
    wide, big_two, old_state, old_free = call(
        collect,
        [lanes_shape, lanes_shape] + [sds((atoms, D_ATOM), BF16)] * 2,
        [me] + cargo,
        flops=10**7,
        smem=1,
    )
    near, far, _ = sum_pair(table, owners)

    def everywhere(piece):
        return [piece] + [moved(piece, k, groups, "group") for k in range(1, groups)]

    prepared = list(
        call(
            prepare_one,
            [sds(s, BF16) for s in PREPARED],
            [me, raw_one] + everywhere(wide),
            flops=10**9,
            smem=1,
            scratch=[(groups, D_EDGE, lanes)],
        )
    )
    back_one, small_two, back_two = prepared[:5], prepared[5:12], prepared[12:16] + [prepared[11]]
    first_one, second_one, big_one = prepared[16:]
    (
        atom_in_one, hidden_one, slope_one, state_one, sent_one, free, slope_edge_one, *kept_two, table,
    ) = call(
        middle_half,
        [table_shape, atom_shape, atom_shape, atom_wide, atom_shape, atom_shape, edge_shape]
        + kept
        + [table_shape],
        [near, far, big_one, first_one, second_one, kept_one[0]]
        + small_two
        + graph
        + [src_row, dst_row, old_state, old_free],
        flops=10 * 10**9,
        late=[5],
        kept=range(7 + KEPT),
    )
    near, far, _ = sum_pair(table, owners)
    near, state_one, kept_two[0] = lax.optimization_barrier((near, state_one, kept_two[0]))
    first_two, second_two, big_two = call(
        prepare_two,
        [sds(s, BF16) for s in LARGE_SHAPES],
        [me] + everywhere(big_two),
        flops=10**9,
        smem=1,
        scratch=[(groups, D_EDGE, lanes)],
    )
    (
        atom_in_two, hidden_two, sent_two, edge_out_t, atom_out, grad_t, grad_pre, grad_atoms, gain, update,
        pushed,
    ) = call(
        turn,
        [table_shape, atom_shape, atom_shape, edge_wide, sds((count, D_ATOM), BF16), edge_wide, edge_shape,
         atom_wide, gain_shape, atom_shape, atom_shape],
        [me, near, far, big_two, first_two, second_two, src_row, dst_row, edge_cotangent,
         atom_cotangent] + fetch([state_one, free, kept_two[0]]),
        flops=2 * 10**9,
        kept=[4, 5, 7],
        smem=1,
        scratch=[(atoms, D_ATOM)],
    )

    def rows_first(value_t, dtype):
        return call(turned, [sds((edges, D_EDGE), dtype)], [value_t], flops=10**8)[0]

    edge_out = rows_first(edge_out_t, BF16)
    near, far, (grads_two, edge_out) = sum_pair(
        gain,
        owners,
        (call(
            large_grads,
            [sds((D_EDGE, BIG), BF16)],
            [update, pushed, grad_pre, src_row, dst_row, atom_in_two, hidden_two, sent_two],
            flops=10**9,
        )[0], edge_out),
    )
    arrived_two = exchange(grads_two.reshape(owners, cols, BIG))
    fetched = fetch([grad_t] + kept_two[1:] + [slope_edge_one, free, slope_one, grad_atoms])
    half = owners // 4
    grad_small_two, gain, update, pushed, grad_pre, grad_t, *parts = call(
        back_middle,
        [sds((D_EDGE, PAD), BF16), gain_shape, atom_shape, atom_shape, edge_shape, edge_wide,
         *[sds((half, count, D_ATOM), BF16)] * 4],
        [me, near, far]
        + fetched[:KEPT]
        + back_two
        + graph
        + [dst_row, big_one, first_one, second_one, src_row]
        + fetched[KEPT:],
        flops=10 * 10**9,
        kept=[5],
        smem=1,
        scratch=[(atoms, D_ATOM)],
    )
    [pieces] = call(
        large_pieces,
        [sds((groups, D_EDGE, lanes), BF16)],
        [me, update, pushed, grad_pre, src_row, dst_row, atom_in_one, hidden_one, sent_one, grad_small_two],
        flops=10**9,
        late=[6, 7, 8],
        smem=1,
        scratch=[(D_EDGE, PAD + BIG)],
    )
    near, far, (pieces, arrived_two) = sum_pair(gain, owners, (pieces, arrived_two))
    pieces = [pieces[0]] + [moved(pieces[k], k, groups, "group") for k in range(1, groups)]
    [grads_one] = call(sum_pieces, [sds((D_EDGE, PAD + lanes), BF16)], pieces, flops=10**7, kept=[0])
    grads_one, grad_t = lax.optimization_barrier((grads_one, grad_t))
    mine = parts[0].astype(F32)
    for k in range(1, 4):
        mine = mine + moved(parts[k], k, owners).astype(F32)
    mine = mine.astype(BF16)
    step = 4
    while half > 2:
        high, mine = mine[half // 2 :], mine[: half // 2]
        mine = (mine.astype(F32) + moved(high, step, owners).astype(F32)).astype(BF16)
        half, step = half // 2, 2 * step
    grad_atom = mine[0].astype(F32) + moved(mine[1], step, owners).astype(F32)
    grad_edge_t, grads_one = call(
        back_last,
        [edge_wide, sds((D_EDGE, PAD + lanes), BF16)],
        [near, far] + fetch([grad_t] + kept_one[1:]) + back_one + graph + [dst_row, grads_one],
        flops=10 * 10**9,
        kept=[1],
        alias={BACK: 1},
        scratch=[pltpu.VMEM((D_EDGE, PAD), BF16), pltpu.SemaphoreType.DMA],
    )
    grad_edge = rows_first(grad_edge_t, F32)
    grads_one, arrived_two = lax.optimization_barrier((grads_one, arrived_two))
    arrived_one = exchange(grads_one.reshape(owners, cols, PAD + lanes))

    def owned(arrived):
        [total] = call(sum_parts, [sds(arrived.shape[1:], BF16)], [arrived], flops=10**7)
        return everywhere(total)

    pieces = owned(arrived_one) + owned(arrived_two)
    rows = weights.shape[0]
    results = call(
        adam,
        [sds((cols, rows), F32)] * 4 + [sds((cols, rows), BF16)],
        [me, weights_t, jnp.transpose(first_moment), jnp.transpose(second_moment)] + pieces,
        flops=10**8,
        kept=range(5),
        smem=1,
        scratch=[(groups, cols, lanes)],
    )
    return (edge_out, atom_out, grad_edge, grad_atom) + tuple(jnp.transpose(r) for r in results)


def solution(mesh):
    both = P(("group", "shard"), None)
    line = P(("group", "shard"))
    flat = P(None, "shard")
    in_specs = (both,) * 6 + (line, both) + (line,) * 6 + (both, both) + (flat,) * 3
    out_specs = (both,) * 4 + (flat,) * 5
    return jax.shard_map(
        per_device, mesh=mesh, in_specs=in_specs, out_specs=out_specs, check_vma=False
    )
```
